32 devices in a mesh: grp: 8 (over y, x, core), hd: 4 (over z).
Axes of the slice: x: 2, y: 2, z: 4, core: 2. Of those that a mesh axis runs over, the one named last changes fastest.
Arguments:
- pixels: bfloat16 [96, 256, 1024], P(('grp', 'hd')), may hold values from -6 to 6
- latents: bfloat16 [96, 256, 1024], P(('grp', 'hd')), may hold values from -6 to 6
- skip: bfloat16 [96, 256, 1024], P(('grp', 'hd')), may hold values from -6 to 6
- counts: int32 [96], P('grp'), may hold values from 1 to 256, as said below
- cotangent: bfloat16 [96, 256, 1024], P(('grp', 'hd')), may hold values from -6 to 6
- attn_in: float32 [6, 1024, 1024], P(None, None, ('grp', 'hd')), may hold values from -0.1875 to 0.1875
- attn_out: float32 [2, 1024, 1024], P(None, None, ('grp', 'hd')), may hold values from -2 to 2
- w_in: float32 [1024, 4096], P(None, ('grp', 'hd')), may hold values from -0.1875 to 0.1875
- w_out: float32 [4096, 1024], P(None, ('grp', 'hd')), may hold values from -0.09375 to 0.09375
- gains: float32 [4, 1024], P(None, ('grp', 'hd')), may hold values from 0.5 to 1.5
- attn_in_first: float32 [6, 1024, 1024], P(None, None, ('grp', 'hd')), may hold values from -896 to 896
- attn_in_second: float32 [6, 1024, 1024], P(None, None, ('grp', 'hd')), may hold values from 12288 to 196608
- attn_out_first: float32 [2, 1024, 1024], P(None, None, ('grp', 'hd')), may hold values from -80 to 80
- attn_out_second: float32 [2, 1024, 1024], P(None, None, ('grp', 'hd')), may hold values from 96 to 1536
- w_in_first: float32 [1024, 4096], P(None, ('grp', 'hd')), may hold values from -256 to 256
- w_in_second: float32 [1024, 4096], P(None, ('grp', 'hd')), may hold values from 1117 to 17873
- w_out_first: float32 [4096, 1024], P(None, ('grp', 'hd')), may hold values from -512 to 512
- w_out_second: float32 [4096, 1024], P(None, ('grp', 'hd')), may hold values from 4423 to 70778
- gains_first: float32 [4, 1024], P(None, ('grp', 'hd')), may hold values from -7524.8325 to 7524.8325
- gains_second: float32 [4, 1024], P(None, ('grp', 'hd')), may hold values from 12288 to 14155776, as said below
Outputs:
- latents_out: bfloat16 [96, 256, 1024], P(('grp', 'hd'))
- pixels_grad: float32 [96, 256, 1024], P(('grp', 'hd'))
- latents_grad: float32 [96, 256, 1024], P(('grp', 'hd'))
- attn_in_moment: float32 [6, 1024, 1024], P(None, None, ('grp', 'hd'))
- attn_in_square: float32 [6, 1024, 1024], P(None, None, ('grp', 'hd'))
- attn_in_new: float32 [6, 1024, 1024], P(None, None, ('grp', 'hd'))
- attn_out_moment: float32 [2, 1024, 1024], P(None, None, ('grp', 'hd'))
- attn_out_square: float32 [2, 1024, 1024], P(None, None, ('grp', 'hd'))
- attn_out_new: float32 [2, 1024, 1024], P(None, None, ('grp', 'hd'))
- w_in_moment: float32 [1024, 4096], P(None, ('grp', 'hd'))
- w_in_square: float32 [1024, 4096], P(None, ('grp', 'hd'))
- w_in_new: float32 [1024, 4096], P(None, ('grp', 'hd'))
- w_out_moment: float32 [4096, 1024], P(None, ('grp', 'hd'))
- w_out_square: float32 [4096, 1024], P(None, ('grp', 'hd'))
- w_out_new: float32 [4096, 1024], P(None, ('grp', 'hd'))
- gains_moment: float32 [4, 1024], P(None, ('grp', 'hd'))
- gains_square: float32 [3, 1024], P(None, ('grp', 'hd'))
- mlp_gain_square: float32 [1024], P(('grp', 'hd'))
- gains_new: float32 [4, 1024], P(None, ('grp', 'hd'))
The draws below stay inside these ranges and needn't reach their ends.
Inputs may be any that keep to these rules, and one draw needn't show every extreme that they name: The first counts[i] input rows of image i are visible, the rest are padding; some image has all 256 rows visible. `gains_second`: entries are positive.
All inputs are finite; a program needn't handle non-finite values.
Results may differ from the reference program's by a relative error of at most 0.029.
Values may be sent and summed in bfloat16 or wider, within the bound.
No kernel may reach another device: no remote copies, remote signals or barrier semaphores. Data moves between devices by JAX's collectives and lax.ppermute only.
A program may use at most 320 MiB of HBM per device.

```python
import math
import jax
import jax.numpy as jnp
from jax import lax

D = 1024
NH = 8
HS = 128
FF = 4096
LAT = 256
PIX = 256
STEP = 5
IMAGES = 96


def draw_counts(key, part):
    key = jax.random.fold_in(key, 11)
    count_key, pick_key = jax.random.split(key)
    visible = jax.random.randint(count_key, (IMAGES,), 1, PIX + 1)
    chosen = jax.random.randint(pick_key, (), 0, IMAGES)
    return jnp.where(jnp.arange(IMAGES) == chosen, PIX, visible).astype(jnp.int32)


def draw_gains_first(key, part):
    key = jax.random.fold_in(key, 29)
    values = jnp.clip(jax.random.normal(key, (4, D), jnp.float32), -6.0, 6.0)
    factors = jnp.array([8.0, 5.0, 4.0, 3.0], jnp.float32)[:, None]
    return values * factors * jnp.float32((IMAGES * LAT) ** 0.5)


def draw_gains_second(key, part):
    key = jax.random.fold_in(key, 23)
    spread = jax.random.uniform(key, (4, D), jnp.float32)
    factors = jnp.array([144.0, 64.0, 64.0, 0.5], jnp.float32)[:, None]
    return factors * jnp.float32(IMAGES * LAT) * jnp.exp(spread * math.log(4.0))


def raised(values, rng, source, target, parts, factor):
    def block_of(axis_at):
        return (jnp.arange(values.shape[axis_at]) // (values.shape[axis_at] // parts)).reshape((-1,) + (1,) * (values.ndim - 1 - axis_at))

    near = jax.random.permutation(rng, parts)[block_of(target)]
    far = (block_of(target) + parts // 2) % parts
    return jnp.where((block_of(source) == near) | (block_of(source) == far), factor * values, values)


def steps_of(stream_key, extent, pieces, least, top_value):
    level = 1.0
    for axis_at, shards_of in pieces:
        steps = jax.random.uniform(jax.random.fold_in(jax.random.fold_in(stream_key, 6), axis_at), (shards_of,), jnp.float32, least / len(pieces), top_value / len(pieces))
        level = level * jnp.repeat(jnp.exp(steps), extent[axis_at] // shards_of).reshape((-1,) + (1,) * (len(extent) - 1 - axis_at))
    return level


def noise(rng, dims, width, reach, pieces=(), held_as=jnp.bfloat16):
    gain = steps_of(rng, dims, pieces, -0.22, 0.18) if pieces else 1.0
    entries = jax.random.normal(rng, dims, jnp.float32) * width * gain
    return jnp.minimum(jnp.maximum(entries, -reach), reach).astype(held_as)


def bell_draw_with(rng, shape, deviation, bound, cuts, heavy, kind=jnp.bfloat16):
    entries = deviation * jax.random.normal(rng, shape, jnp.float32)
    if cuts:
        entries = entries * steps_of(rng, shape, cuts, -0.22, 0.18)
    return jnp.clip(raised(entries, jax.random.fold_in(rng, 3), *heavy), -bound, bound).astype(kind)


def setup_inputs(seed: int = 0) -> dict:
    key_of = jax.random.split(jax.random.key(seed), 21)
    return {
        "pixels": noise(key_of[0], (IMAGES, PIX, D), 1.0, 6.0, ((0, 32),)),
        "latents": noise(key_of[1], (IMAGES, LAT, D), 1.0, 6.0, ((0, 32),)),
        "skip": noise(key_of[2], (IMAGES, LAT, D), 1.0, 6.0, ((0, 32),)),
        "counts": draw_counts(jax.random.fold_in(key_of[20], 71), 0),
        "cotangent": bell_draw_with(key_of[4], (IMAGES, LAT, D), 1.0, 6.0, ((0, 32),), (0, 2, 32, 2.75)),
        "attn_in": noise(key_of[5], (6, D, D), D ** -0.5, 0.1875, ((2, 32),), jnp.float32),
        "attn_out": noise(key_of[6], (2, D, D), (2 * D // LAT) ** -0.5, 2.0, ((2, 32),), jnp.float32),
        "w_in": noise(key_of[7], (D, FF), D ** -0.5, 0.1875, ((1, 32),), jnp.float32),
        "w_out": noise(key_of[8], (FF, D), FF ** -0.5, 0.09375, ((1, 32),), jnp.float32),
        "gains": jnp.clip(1.0 + 0.1 * jax.random.normal(key_of[9], (4, D), jnp.float32), 0.5, 1.5),
        "attn_in_first": noise(key_of[10], (6, D, D), ((IMAGES * LAT) ** 0.5), 896.0, ((2, 32),), jnp.float32),
        "attn_in_second": jnp.clip(jnp.exp(math.log(196608.0) - 2.7725887 * jax.random.uniform(key_of[11], (6, D, D), jnp.float32) ** steps_of(key_of[11], (6, D, D), ((2, 32),), -0.2, 0.2)), 12288.0, 196608.0),
        "attn_out_first": noise(key_of[12], (2, D, D), ((2 * IMAGES * LAT // PIX) ** 0.5), 80.0, ((2, 32),), jnp.float32),
        "attn_out_second": jnp.clip(jnp.exp(math.log(1536.0) - 2.7725887 * jax.random.uniform(key_of[13], (2, D, D), jnp.float32) ** steps_of(key_of[13], (2, D, D), ((2, 32),), -0.2, 0.2)), 96.0, 1536.0),
        "w_in_first": noise(key_of[14], (D, FF), (0.3 * (IMAGES * LAT) ** 0.5), 256.0, ((1, 32),), jnp.float32),
        "w_in_second": jnp.clip(jnp.exp(math.log(17873.0) - 2.7726447 * jax.random.uniform(key_of[15], (D, FF), jnp.float32) ** steps_of(key_of[15], (D, FF), ((1, 32),), -0.2, 0.2)), 1117.0, 17873.0),
        "w_out_first": noise(key_of[16], (FF, D), (0.6 * (IMAGES * LAT) ** 0.5), 512.0, ((1, 32),), jnp.float32),
        "w_out_second": jnp.clip(jnp.exp(math.log(70778.0) - 2.77273 * jax.random.uniform(key_of[17], (FF, D), jnp.float32) ** steps_of(key_of[17], (FF, D), ((1, 32),), -0.2, 0.2)), 4423.0, 70778.0),
        "gains_first": draw_gains_first(jax.random.fold_in(key_of[20], 71), 0),
        "gains_second": draw_gains_second(jax.random.fold_in(key_of[20], 71), 0),
    }


@jax.custom_vjp
def low(v):
    return lax.optimization_barrier(v.astype(jnp.bfloat16)).astype(jnp.float32)

@jax.custom_vjp
def low_back(v):
    return v

def low_keep(v):
    return (low(v), None)

def low_pass(kept, grad):
    return (grad,)

def back_keep(v):
    return (v, None)

def back_low(kept, grad):
    return (low(grad),)
low.defvjp(low_keep, low_pass)
low_back.defvjp(back_keep, back_low)

def normed(row_block, gain_row):
    return row_block * lax.rsqrt(lax.optimization_barrier(jnp.mean(row_block * row_block, axis=-1, keepdims=True)) + 1e-06) * gain_row

def project(row_block, matrix):
    return jnp.einsum('bnd,de->bne', row_block, matrix, precision=lax.Precision.HIGHEST)

def attend(queries, key_rows, value_rows, visible):
    image_count = queries.shape[0]
    query_heads = queries.reshape(image_count, queries.shape[1], NH, HS)
    key_heads = key_rows.reshape(image_count, key_rows.shape[1], NH, HS)
    value_heads = value_rows.reshape(image_count, value_rows.shape[1], NH, HS)
    scores = jnp.einsum('bqhd,bkhd->bhqk', query_heads, key_heads, precision=lax.Precision.HIGHEST)
    scores = low_back(scores * HS ** (-0.5))
    scores = jnp.where(visible[:, None, None, :], scores, -1e+30)
    highest = lax.optimization_barrier(jnp.max(scores, axis=-1, keepdims=True))
    exponent = jnp.exp(scores - highest)
    probs = low(exponent / lax.optimization_barrier(jnp.sum(exponent, axis=-1, keepdims=True)))
    context = jnp.einsum('bhqk,bkhd->bqhd', probs, value_heads, precision=lax.Precision.HIGHEST)
    return low_back(low(context.reshape(queries.shape)))

def block(pixel_rows, latent_rows, visible, mixing, outward, lift, lower, gain_rows):
    pixel_norm = low(normed(pixel_rows, gain_rows[0]))
    latent_norm = low(normed(latent_rows, gain_rows[1]))
    queries = low_back(low(project(latent_norm, mixing[0])))
    key_rows = low_back(low(project(pixel_norm, mixing[1])))
    value_rows = low_back(low(project(pixel_norm, mixing[2])))
    context = attend(queries, key_rows, value_rows, visible)
    first_sum = latent_rows + low_back(project(context, outward[0]))
    self_norm = low(normed(first_sum, gain_rows[2]))
    queries2 = low_back(low(project(self_norm, mixing[3])))
    keys2 = low_back(low(project(self_norm, mixing[4])))
    values2 = low_back(low(project(self_norm, mixing[5])))
    all_keys = jnp.ones((latent_rows.shape[0], latent_rows.shape[1]), jnp.bool_)
    context2 = attend(queries2, keys2, values2, all_keys)
    second_sum = first_sum + low_back(project(context2, outward[1]))
    mlp_norm = low(normed(second_sum, gain_rows[3]))
    hidden = low_back(project(mlp_norm, lift))
    active = low(jax.nn.gelu(hidden))
    return second_sum + low_back(project(active, lower))

def adamw(weight, grad, first_old, second_old, learn_rate, decay):
    first_new = 0.5 * first_old + 0.5 * grad
    second_new = 0.5 * second_old + 0.5 * grad * grad
    correction = 1.0 - 0.5 ** STEP
    normed_step = first_new / correction / (jnp.sqrt(second_new / correction) + 1e-08)
    return (first_new, second_new, weight - learn_rate * (normed_step + decay * weight))

def reference(pixels, latents, skip, counts, cotangent, attn_in, attn_out, w_in, w_out, gains, attn_in_first, attn_in_second, attn_out_first, attn_out_second, w_in_first, w_in_second, w_out_first, w_out_second, gains_first, gains_second):
    batch_size = 8
    batches = IMAGES // batch_size
    visible_all = jnp.arange(PIX)[None, :] < counts[:, None]

    def forward(pixel_f, latent_f, mixing_f, outward_f, lift_f, lower_f, gain_f):
        mixing = low(mixing_f)
        outward = low(outward_f)
        lift = low(lift_f)
        lower = low(lower_f)
        gain_rows = low(gain_f)

        def one_batch(batch_item):
            return block(batch_item[0], batch_item[1], batch_item[2], mixing, outward, lift, lower, gain_rows)
        stacked = (pixel_f.reshape(batches, batch_size, PIX, D), latent_f.reshape(batches, batch_size, LAT, D), visible_all.reshape(batches, batch_size, PIX))
        return lax.map(jax.checkpoint(one_batch), stacked).reshape(IMAGES, LAT, D)
    result, pull_back = jax.vjp(forward, pixels.astype(jnp.float32), latents.astype(jnp.float32), attn_in, attn_out, w_in, w_out, gains)
    grads = pull_back(cotangent.astype(jnp.float32))
    latents_out = (result + skip.astype(jnp.float32)).astype(jnp.bfloat16)
    mix_first, mix_second, mix_new = adamw(attn_in, grads[2], attn_in_first, attn_in_second, 0.05, 0.1)
    out_first, out_second, out_new = adamw(attn_out, grads[3], attn_out_first, attn_out_second, 0.3, 0.1)
    lift_first, lift_second, lift_new = adamw(w_in, grads[4], w_in_first, w_in_second, 0.05, 0.1)
    lower_first, lower_second, lower_new = adamw(w_out, grads[5], w_out_first, w_out_second, 0.03, 0.1)
    gain_first, gain_second, gain_new = adamw(gains, grads[6], gains_first, gains_second, 0.4, 0.0)
    return (latents_out, grads[0], grads[1], mix_first, mix_second, mix_new, out_first, out_second, out_new, lift_first, lift_second, lift_new, lower_first, lower_second, lower_new, gain_first, gain_second[:3], gain_second[3], gain_new)
```

```python
import functools

import jax
import jax.numpy as jnp
from jax import lax
from jax.experimental import pallas as pl
from jax.experimental.pallas import tpu as pltpu
from jax.sharding import PartitionSpec as P

NH = 8
STEP = 5
AXES = ("grp", "hd")

MIB = 1 << 20
F32, LOW = jnp.float32, jnp.bfloat16
VMEM = pl.BlockSpec(memory_space=pltpu.VMEM)
SMEM = pl.BlockSpec(memory_space=pltpu.SMEM)


ANY = pl.BlockSpec(memory_space=pl.ANY)


def adamw(weight, grad, first_old, second_old, learn_rate, decay):
    first_new = 0.5 * first_old + 0.5 * grad
    second_new = 0.5 * second_old + 0.5 * grad * grad
    correction = 1.0 - 0.5**STEP
    normed_step = first_new / correction / (jnp.sqrt(second_new / correction) + 1e-08)
    return (first_new, second_new, weight - learn_rate * (normed_step + decay * weight))


def log2(n):
    return n.bit_length() - 1


def bit_orders(groups, depth):
    near = log2(depth)
    z_bits = list(range(near))[::-1]
    outer = list(range(near + 1, near + log2(groups)))
    half = (len(outer) + 1) // 2
    x_bits, y_bits = outer[:half][::-1], outer[half:][::-1]
    return {
        "xzy": x_bits + z_bits + y_bits,
        "yzx": y_bits + z_bits + x_bits,
        "zxy": z_bits + x_bits + y_bits,
        "zyx": z_bits + y_bits + x_bits,
    }


def swap(block, bit, total):
    return lax.ppermute(block, AXES, [(j, j ^ (1 << bit)) for j in range(total)])


def spread_of(order, core, total):
    bits = list(order) + [core]
    return [sum(((p >> t) & 1) << b for t, b in enumerate(bits)) for p in range(total)]


def gather_chain(shard, order, core, total):
    held = shard[None]
    for bit in order[:-1]:
        held = jnp.concatenate([held, swap(held, bit, total)], axis=0)
    came = swap(held, order[-1], total)
    return [held, came, swap(held, core, total), swap(came, core, total)]


def added(a, b):
    return (a.astype(jnp.float32) + b.astype(jnp.float32)).astype(jnp.bfloat16)


def scatter_chain(pieces, order, core, total):
    away = added(pieces[1], swap(pieces[3], core, total))
    held = added(pieces[0], swap(pieces[2], core, total))
    held = added(held, swap(away, order[-1], total))
    for bit in reversed(order[:-1]):
        half = held.shape[0] // 2
        held = added(held[:half], swap(held[half:], bit, total))
    return held[0]


def device_index():
    return lax.axis_index("grp") * lax.axis_size("hd") + lax.axis_index("hd")


def place_kernel(spreads, blocks_of, *refs):
    *refs, sems = refs
    count = 4 * len(spreads)
    pieces, wholes = refs[:count], refs[count:]
    me = device_index()
    for c, spread in enumerate(spreads):
        each = len(spread) // 4
        for p, mask in enumerate(spread):
            block = pieces[4 * c + p // each].at[p % each]
            for m, (part, place) in enumerate(blocks_of[c](block, wholes, me ^ mask)):
                pltpu.make_async_copy(part, place, sems.at[m]).start()
    for m, whole in enumerate(wholes):
        pltpu.make_async_copy(whole, whole, sems.at[m]).wait()


def cut_kernel(spreads, blocks_of, count, *refs):
    *refs, sems = refs
    wholes, pieces = refs[:count], refs[count:]
    me = device_index()
    for c, spread in enumerate(spreads):
        each = len(spread) // 4
        for p, mask in enumerate(spread):
            at = 4 * c + p // each
            for part, place in blocks_of[c](pieces[at].at[p % each], wholes, me ^ mask):
                pltpu.make_async_copy(place, part, sems.at[at]).start()
    for m, piece in enumerate(pieces):
        pltpu.make_async_copy(piece, piece, sems.at[m]).wait()


def row_blocks(rows, block, wholes, owner):
    start = pl.multiple_of(owner * rows, rows)
    return [
        (block.at[pl.ds(m * rows, rows), :], whole.at[pl.ds(start, rows), :])
        for m, whole in enumerate(wholes)
    ]


def row_half(rows, at, width, block, wholes, owner):
    start = pl.multiple_of(owner * rows, rows)
    return [(block, wholes[0].at[pl.ds(start, rows), pl.ds(at, width)])]


def column_half(columns, at, width, block, wholes, owner):
    start = pl.multiple_of(owner * columns, columns)
    return [(block, wholes[0].at[pl.ds(at, width), pl.ds(start, columns)])]


def place(pieces, spreads, blocks_of, shapes):
    return pl.pallas_call(
        functools.partial(place_kernel, spreads, blocks_of),
        out_shape=[jax.ShapeDtypeStruct(s, LOW) for s in shapes],
        in_specs=[ANY] * len(pieces),
        out_specs=[VMEM] * len(shapes),
        scratch_shapes=[pltpu.SemaphoreType.DMA((len(shapes),))],
        compiler_params=pltpu.CompilerParams(vmem_limit_bytes=20 * MIB),
    )(*pieces)


def cut(wholes, spreads, blocks_of, shapes):
    return pl.pallas_call(
        functools.partial(cut_kernel, spreads, blocks_of, len(wholes)),
        out_shape=[
            jax.ShapeDtypeStruct((len(spread) // 4,) + shape, LOW)
            for spread, shape in zip(spreads, shapes)
            for _ in range(4)
        ],
        in_specs=[VMEM] * len(wholes),
        out_specs=[ANY] * (4 * len(shapes)),
        scratch_shapes=[pltpu.SemaphoreType.DMA((4 * len(shapes),))],
        compiler_params=pltpu.CompilerParams(vmem_limit_bytes=20 * MIB),
    )(*wholes)


ATTENTION_CHAINS = (("xzy", (1, 2)), ("yzx", (0, 6)), ("zxy", (3, 4)), ("zyx", (5, 7)))
LOWER_CHAINS = ("xzy", "yzx")
LIFT_CHAINS = ("zxy", "zyx")


def gather_weights(attention, lower, lift, groups, depth):
    total, core = groups * depth, log2(depth)
    orders = bit_orders(groups, depth)
    rows = attention[0].shape[0]
    if rows % 16 or lift.shape[1] % 128:
        whole = [lax.all_gather(a, AXES, axis=0, tiled=True) for a in attention]
        return (
            whole,
            lax.all_gather(lower, AXES, axis=0, tiled=True),
            lax.all_gather(lift, AXES, axis=1, tiled=True),
        )
    matrices = [None] * 8
    for name, members in ATTENTION_CHAINS:
        shard = jnp.concatenate([attention[m] for m in members], axis=0)
        pieces = gather_chain(shard, orders[name], core, total)
        placed = place(
            pieces,
            [spread_of(orders[name], core, total)],
            [functools.partial(row_blocks, rows)],
            [(rows * total, attention[0].shape[1])] * len(members),
        )
        for m, whole in zip(members, placed):
            matrices[m] = whole
    (lower_whole,) = place(
        [p for h, name in enumerate(LOWER_CHAINS) for p in gather_chain(half_of(lower, 1, h), orders[name], core, total)],
        [spread_of(orders[name], core, total) for name in LOWER_CHAINS],
        [functools.partial(row_half, rows, h * lower.shape[1] // 2, lower.shape[1] // 2) for h in range(2)],
        [(rows * total, lower.shape[1])],
    )
    (lift_whole,) = place(
        [p for h, name in enumerate(LIFT_CHAINS) for p in gather_chain(half_of(lift, 0, h), orders[name], core, total)],
        [spread_of(orders[name], core, total) for name in LIFT_CHAINS],
        [functools.partial(column_half, lift.shape[1], h * lift.shape[0] // 2, lift.shape[0] // 2) for h in range(2)],
        [(lift.shape[0], lift.shape[1] * total)],
    )
    return matrices, lower_whole, lift_whole


def scatter_attention(grads, groups, depth):
    total, core = groups * depth, log2(depth)
    orders = bit_orders(groups, depth)
    rows = grads[0].shape[0] // total
    if rows % 16:
        return {
            m: lax.psum_scatter(g, AXES, scatter_dimension=0, tiled=True) for m, g in grads.items()
        }
    sums = {}
    for name, members in ATTENTION_CHAINS:
        pieces = cut(
            [grads[m] for m in members],
            [spread_of(orders[name], core, total)],
            [functools.partial(row_blocks, rows)],
            [(rows * len(members), grads[0].shape[1])],
        )
        own = scatter_chain(pieces, orders[name], core, total)
        for at, m in enumerate(members):
            sums[m] = own[at * rows : (at + 1) * rows]
    return sums


def scatter_mlp(lower_grad, lift_grad, groups, depth):
    total, core = groups * depth, log2(depth)
    orders = bit_orders(groups, depth)
    rows, columns = lower_grad.shape[0] // total, lift_grad.shape[1] // total
    if rows % 16 or columns % 128:
        return (
            lax.psum_scatter(lower_grad, AXES, scatter_dimension=0, tiled=True),
            lax.psum_scatter(lift_grad, AXES, scatter_dimension=1, tiled=True),
        )
    half = lift_grad.shape[0] // 2
    pieces = cut(
        [lift_grad],
        [spread_of(orders[name], core, total) for name in LIFT_CHAINS],
        [functools.partial(column_half, columns, h * half, half) for h in range(2)],
        [(half, columns)] * 2,
    )
    lift_sums = [
        scatter_chain(pieces[4 * h : 4 * h + 4], orders[name], core, total) for h, name in enumerate(LIFT_CHAINS)
    ]
    half = lower_grad.shape[1] // 2
    pieces = cut(
        [lower_grad],
        [spread_of(orders[name], core, total) for name in LOWER_CHAINS],
        [functools.partial(row_half, rows, h * half, half) for h in range(2)],
        [(rows, half)] * 2,
    )
    lower_sums = [
        scatter_chain(pieces[4 * h : 4 * h + 4], orders[name], core, total) for h, name in enumerate(LOWER_CHAINS)
    ]
    return jnp.concatenate(lower_sums, axis=1), jnp.concatenate(lift_sums, axis=0)


def half_of(array, along, which):
    half = array.shape[along] // 2
    return lax.slice_in_dim(array, which * half, (which + 1) * half, axis=along)


def block_matrix(spread, total):
    mine = jnp.array(spread, jnp.int32)[None, :] ^ device_index()
    return (lax.broadcasted_iota(jnp.int32, (total, total), 0) == mine).astype(F32)


def gather_gains(gains, groups, depth):
    total, core = groups * depth, log2(depth)
    if total > 32:
        return lax.all_gather(gains, AXES, axis=1, tiled=True).astype(F32)
    order = bit_orders(groups, depth)["xzy"]
    rows, columns = gains.shape
    held = gains.reshape(1, -1)
    for bit in (*order, core):
        held = jnp.concatenate([held, swap(held, bit, total)], axis=0)
    whole = jnp.dot(block_matrix(spread_of(order, core, total), total).astype(LOW), held, preferred_element_type=F32)
    return jnp.swapaxes(whole.reshape(total, rows, columns), 0, 1).reshape(rows, -1)


def scatter_gains(grads, groups, depth):
    total, core = groups * depth, log2(depth)
    if total > 32:
        return lax.psum_scatter(grads.astype(LOW), AXES, scatter_dimension=1, tiled=True).astype(F32)
    order = bit_orders(groups, depth)["xzy"]
    rows = grads.shape[0]
    blocks = jnp.swapaxes(grads.reshape(rows, total, -1), 0, 1).reshape(total, -1)
    held = jnp.dot(
        block_matrix(spread_of(order, core, total), total).T, blocks, precision=lax.Precision.HIGHEST
    )
    for bit in (core, *reversed(order)):
        half = held.shape[0] // 2
        held = held[:half] + swap(held[half:], bit, total)
    return held.reshape(rows, -1)


def dot_nn(a, b):
    return lax.dot_general(a, b, (((1,), (0,)), ((), ())), preferred_element_type=F32)


def dot_nt(a, b):
    return lax.dot_general(a, b, (((1,), (1,)), ((), ())), preferred_element_type=F32)


def dot_tn(a, b):
    return lax.dot_general(a, b, (((0,), (0,)), ((), ())), preferred_element_type=F32)


def unit_rows(rows):
    inverse = lax.rsqrt(jnp.mean(rows * rows, axis=-1, keepdims=True) + 1e-06)
    return rows * inverse, inverse


def norm_grad(rows, gain, upstream):
    unit, inverse = unit_rows(rows)
    scaled = upstream * gain
    inner = jnp.mean(scaled * unit, axis=-1, keepdims=True)
    return (scaled - unit * inner) * inverse, jnp.sum(upstream * unit, axis=0, keepdims=True)


def heads_probs(query, key, count, scale):
    scores = dot_nt(query, key) * scale
    if count is not None:
        place = lax.broadcasted_iota(jnp.int32, scores.shape, 1)
        scores = jnp.where(place < count, scores, -1e30)
    exponent = jnp.exp(scores - jnp.max(scores, axis=-1, keepdims=True))
    return exponent / jnp.sum(exponent, axis=-1, keepdims=True)


def attend_kernel(cross, images, size, *refs):
    if cross:
        counts, gains, source, target, *refs = refs
    else:
        gains, target, *refs = refs
        counts, source = None, target
    (wq, wk, wv, wo, q_out, k_out, v_out, context_out, sum_out, wq_v, wk_v, wv_v, wo_v, sems) = refs
    copies = []
    for at, (src, dst) in enumerate(((wk, wk_v), (wv, wv_v), (wq, wq_v), (wo, wo_v))):
        copies.append(pltpu.make_async_copy(src, dst, sems.at[at]))
        copies[-1].start()
    key_gain, query_gain = (0, 1) if cross else (2, 2)
    rows = source[...].astype(F32)
    normal = (unit_rows(rows)[0] * gains[key_gain : key_gain + 1, :]).astype(LOW)
    copies[0].wait()
    k_out[...] = dot_nt(normal, wk_v[...]).astype(LOW)
    copies[1].wait()
    v_out[...] = dot_nt(normal, wv_v[...]).astype(LOW)
    if cross:
        rows = target[...].astype(F32)
        normal = (unit_rows(rows)[0] * gains[query_gain : query_gain + 1, :]).astype(LOW)
    copies[2].wait()
    q_out[...] = dot_nt(normal, wq_v[...]).astype(LOW)
    width = q_out.shape[1] // NH
    scale = width ** (-0.5)

    def one_image(image, carry):
        span = pl.ds(pl.multiple_of(image * size, size), size)
        count = counts[image] if cross else None
        for h in range(NH):
            part = slice(h * width, (h + 1) * width)
            weights = heads_probs(q_out[span, part], k_out[span, part], count, scale).astype(LOW)
            context_out[span, part] = dot_nn(weights, v_out[span, part]).astype(LOW)
        return carry

    lax.fori_loop(0, images, one_image, 0)
    copies[3].wait()
    sum_out[...] = target[...].astype(F32) + dot_nt(context_out[...], wo_v[...])


def attend_block(gains, source, target, counts, weights, images):
    cross = source is not None
    rows, width = target.shape
    low = jax.ShapeDtypeStruct((rows, width), LOW)
    head = (counts, gains, source, target) if cross else (gains, target)
    return pl.pallas_call(
        functools.partial(attend_kernel, cross, images, rows // images),
        out_shape=[low] * 4 + [jax.ShapeDtypeStruct((rows, width), F32)],
        in_specs=([SMEM] if cross else []) + [VMEM] * (3 if cross else 2) + [ANY] * 4,
        out_specs=[VMEM] * 5,
        scratch_shapes=[pltpu.VMEM((width, width), LOW)] * 4 + [pltpu.SemaphoreType.DMA((4,))],
        compiler_params=pltpu.CompilerParams(vmem_limit_bytes=48 * MIB),
        cost_estimate=pl.CostEstimate(
            flops=8 * rows * width * width + 4 * rows * width * (rows // images),
            bytes_accessed=12 * rows * width + 8 * width * width,
            transcendentals=rows * NH * (rows // images),
        ),
    )(*head, *weights)


def attend_grad_kernel(cross, images, size, *refs):
    if cross:
        counts, gains, source, target, *refs = refs
    else:
        gains, target, *refs = refs
        counts, source = None, target
    (upstream, q_in, k_in, v_in, context_in, wq, wk, wv, wo, *refs) = refs
    outs = 2 if cross else 1
    grads_out, gain_outs, (gq_out, gk_out, gv_out, go_out) = refs[:outs], refs[outs : 2 * outs], refs[2 * outs : 2 * outs + 4]
    (dq, dk, dv, dc, wq_v, wk_v, wv_v, wo_v, sems) = refs[2 * outs + 4 :]
    copies = []
    for at, (src, dst) in enumerate(((wo, wo_v), (wq, wq_v), (wk, wk_v), (wv, wv_v))):
        copies.append(pltpu.make_async_copy(src, dst, sems.at[at]))
        copies[-1].start()
    up_low = upstream[...].astype(LOW)
    copies[0].wait()
    dc[...] = dot_nn(up_low, wo_v[...]).astype(LOW)
    go_out[...] = dot_tn(up_low, context_in[...]).astype(LOW)
    width = q_in.shape[1] // NH
    scale = width ** (-0.5)

    def one_image(image, carry):
        span = pl.ds(pl.multiple_of(image * size, size), size)
        count = counts[image] if cross else None
        for h in range(NH):
            part = slice(h * width, (h + 1) * width)
            query, key, value, grad = q_in[span, part], k_in[span, part], v_in[span, part], dc[span, part]
            probs = heads_probs(query, key, count, scale)
            prob_grad = dot_nt(grad, value)
            dv[span, part] = dot_tn(probs.astype(LOW), grad).astype(LOW)
            score_grad = probs * (prob_grad - jnp.sum(probs * prob_grad, axis=-1, keepdims=True))
            score_grad = score_grad.astype(LOW)
            dq[span, part] = (dot_nn(score_grad, key) * scale).astype(LOW)
            dk[span, part] = (dot_tn(score_grad, query) * scale).astype(LOW)
        return carry

    lax.fori_loop(0, images, one_image, 0)
    key_gain, query_gain = (0, 1) if cross else (2, 2)
    rows = target[...].astype(F32)
    gain = gains[query_gain : query_gain + 1, :]
    normal = (unit_rows(rows)[0] * gain).astype(LOW)
    gq_out[...] = dot_tn(dq[...], normal).astype(LOW)
    copies[1].wait()
    back = dot_nn(dq[...], wq_v[...])
    copies[2].wait()
    copies[3].wait()
    if cross:
        extra, gain_grad = norm_grad(rows, gain, back)
        grads_out[0][...] = upstream[...] + extra
        gain_outs[0][...] = gain_grad
        rows = source[...].astype(F32)
        gain = gains[key_gain : key_gain + 1, :]
        normal = (unit_rows(rows)[0] * gain).astype(LOW)
        back = dot_nn(dk[...], wk_v[...])
    else:
        back += dot_nn(dk[...], wk_v[...])
    back += dot_nn(dv[...], wv_v[...])
    gk_out[...] = dot_tn(dk[...], normal).astype(LOW)
    gv_out[...] = dot_tn(dv[...], normal).astype(LOW)
    extra, gain_grad = norm_grad(rows, gain, back)
    if cross:
        grads_out[1][...] = extra
    else:
        grads_out[0][...] = upstream[...] + extra
    gain_outs[-1][...] = gain_grad


def attend_grad(gains, source, target, counts, upstream, saved, weights, images):
    cross = source is not None
    rows, width = target.shape
    outs = 2 if cross else 1
    head = (counts, gains, source, target) if cross else (gains, target)
    result = pl.pallas_call(
        functools.partial(attend_grad_kernel, cross, images, rows // images),
        out_shape=[jax.ShapeDtypeStruct((rows, width), F32)] * outs
        + [jax.ShapeDtypeStruct((1, width), F32)] * outs
        + [jax.ShapeDtypeStruct((width, width), LOW)] * 4,
        in_specs=([SMEM] if cross else []) + [VMEM] * (3 if cross else 2) + [VMEM] * 5 + [ANY] * 4,
        out_specs=[VMEM] * (2 * outs + 4),
        scratch_shapes=[pltpu.VMEM((rows, width), LOW)] * 4
        + [pltpu.VMEM((width, width), LOW)] * 4
        + [pltpu.SemaphoreType.DMA((4,))],
        compiler_params=pltpu.CompilerParams(vmem_limit_bytes=60 * MIB),
        cost_estimate=pl.CostEstimate(
            flops=16 * rows * width * width + 10 * rows * width * (rows // images),
            bytes_accessed=20 * rows * width + 16 * width * width,
            transcendentals=rows * NH * (rows // images),
        ),
    )(*head, upstream, *saved, *weights)
    return result[:outs], result[outs : 2 * outs], result[2 * outs :]


def mlp_kernel(gain_row, second, cotangent, skip, lift, lower, out, second_grad, gain_grad, lift_grad, lower_grad, normal, normal_t, cot_t, total, back):
    step = pl.program_id(0)

    @pl.when(step == 0)
    def first():
        low = (unit_rows(second[...])[0] * gain_row[...]).astype(LOW)
        normal[...] = low
        normal_t[...] = low.T
        cot_t[...] = cotangent[...].T
        total[...] = second[...]
        back[...] = jnp.zeros_like(back)

    hidden = dot_nn(normal[...], lift[...])
    square = hidden * hidden
    root = 0.7978845608028654
    tanh = jnp.tanh(root * hidden * (1.0 + 0.044715 * square))
    half = 0.5 * (1.0 + tanh)
    active = (hidden * half).astype(LOW)
    slope = half + 0.5 * hidden * (1.0 - tanh * tanh) * (root * (1.0 + 3 * 0.044715 * square))
    lower_grad[...] = dot_nn(cot_t[...], active).astype(LOW)
    total[...] += dot_nt(active, lower[...])
    hidden_grad = (dot_nn(cotangent[...], lower[...]) * slope).astype(LOW)
    lift_grad[...] = dot_nn(normal_t[...], hidden_grad).astype(LOW)
    back[...] += dot_nt(hidden_grad, lift[...])

    @pl.when(step == pl.num_programs(0) - 1)
    def last():
        out[...] = (total[...] + skip[...].astype(F32)).astype(LOW)
        extra, gains = norm_grad(second[...], gain_row[...], back[...])
        second_grad[...] = cotangent[...].astype(F32) + extra
        gain_grad[...] = gains


def mlp_block(gain_row, second, cotangent, skip, lift, lower):
    rows, width = second.shape
    hidden, block = lift.shape[1], 512
    whole = lambda shape: pl.BlockSpec(shape, lambda f: (0, 0), pipeline_mode=pl.Buffered(1))
    once = lambda shape: pl.BlockSpec(shape, lambda f: (0, 0))
    chunk = pl.BlockSpec((width, block), lambda f: (0, f))
    return pl.pallas_call(
        mlp_kernel,
        grid=(hidden // block,),
        out_shape=[
            jax.ShapeDtypeStruct((rows, width), LOW),
            jax.ShapeDtypeStruct((rows, width), F32),
            jax.ShapeDtypeStruct((1, width), F32),
            jax.ShapeDtypeStruct((width, hidden), LOW),
            jax.ShapeDtypeStruct((width, hidden), LOW),
        ],
        in_specs=[whole((1, width))] + [whole((rows, width))] * 3 + [chunk] * 2,
        out_specs=[once((rows, width))] * 2 + [once((1, width))] + [chunk] * 2,
        scratch_shapes=[
            pltpu.VMEM((rows, width), LOW),
            pltpu.VMEM((width, rows), LOW),
            pltpu.VMEM((width, rows), LOW),
            pltpu.VMEM((rows, width), F32),
            pltpu.VMEM((rows, width), F32),
        ],
        compiler_params=pltpu.CompilerParams(vmem_limit_bytes=60 * MIB),
        cost_estimate=pl.CostEstimate(
            flops=12 * rows * width * hidden,
            bytes_accessed=8 * width * hidden + 16 * rows * width,
            transcendentals=rows * hidden,
        ),
    )(gain_row, second, cotangent, skip, lift, lower)


def local(
    pixels,
    latents,
    skip,
    counts,
    cotangent,
    attn_in,
    attn_out,
    w_in,
    w_out,
    gains,
    attn_in_first,
    attn_in_second,
    attn_out_first,
    attn_out_second,
    w_in_first,
    w_in_second,
    w_out_first,
    w_out_second,
    gains_first,
    gains_second,
):
    groups, depth = lax.axis_size("grp"), lax.axis_size("hd")
    gain_rows = gather_gains(gains.astype(LOW), groups, depth)
    attn_in_t = jnp.swapaxes(attn_in, 1, 2).astype(LOW)
    attn_out_t = jnp.swapaxes(attn_out, 1, 2).astype(LOW)
    attention = [attn_in_t[m] for m in range(6)] + [attn_out_t[m] for m in range(2)]
    mats, lower, lift = gather_weights(attention, w_out.T.astype(LOW), w_in.astype(LOW), groups, depth)

    images, size, width = latents.shape
    flat = lambda rows: rows.reshape(-1, width)
    whole = lambda rows: rows.reshape(images, -1, width)
    pixel_rows, latent_rows = flat(pixels), flat(latents)
    own_counts = lax.dynamic_slice_in_dim(counts, lax.axis_index("hd") * images, images)
    cross, own = (mats[0], mats[1], mats[2], mats[6]), (mats[3], mats[4], mats[5], mats[7])
    *saved, first_sum = attend_block(gain_rows, pixel_rows, latent_rows, own_counts, cross, images)
    *saved2, second_sum = attend_block(gain_rows, None, first_sum, None, own, images)
    latents_out, second_grad, gain3_grad, lift_grad, lower_grad = mlp_block(
        gain_rows[3:], second_sum, flat(cotangent), flat(skip), lift, lower
    )
    lower_sum, lift_sum = scatter_mlp(lower_grad, lift_grad, groups, depth)
    (first_grad,), (gain2_grad,), grads2 = attend_grad(
        gain_rows, None, first_sum, None, second_grad, saved2, own, images
    )
    (latents_grad, pixels_grad), (gain1_grad, gain0_grad), grads = attend_grad(
        gain_rows, pixel_rows, latent_rows, own_counts, first_grad, saved, cross, images
    )
    sums = scatter_attention(
        dict(zip((3, 4, 5, 7, 0, 1, 2, 6), (*grads2, *grads))), groups, depth
    )
    gains_grad = jnp.concatenate([gain0_grad, gain1_grad, gain2_grad, gain3_grad], axis=0)
    gains_sum = scatter_gains(gains_grad, groups, depth)
    mixing_sum = jnp.swapaxes(jnp.stack([sums[m] for m in range(6)]), 1, 2).astype(F32)
    outward_sum = jnp.swapaxes(jnp.stack([sums[6], sums[7]]), 1, 2).astype(F32)
    mix = adamw(attn_in, mixing_sum, attn_in_first, attn_in_second, 0.05, 0.1)
    out = adamw(attn_out, outward_sum, attn_out_first, attn_out_second, 0.3, 0.1)
    lift_new = adamw(w_in, lift_sum.astype(F32), w_in_first, w_in_second, 0.05, 0.1)
    lower_new = adamw(w_out, lower_sum.T.astype(F32), w_out_first, w_out_second, 0.03, 0.1)
    gain_first, gain_second, gain_new = adamw(
        gains, gains_sum, gains_first, gains_second, 0.4, 0.0
    )
    return (
        whole(latents_out),
        whole(pixels_grad),
        whole(latents_grad),
        *mix,
        *out,
        *lift_new,
        *lower_new,
        gain_first,
        gain_second[:3],
        gain_second[3],
        gain_new,
    )


def solution(mesh):
    return jax.shard_map(
        local,
        mesh=mesh,
        in_specs=(
            P(("grp", "hd"), None, None),
            P(("grp", "hd"), None, None),
            P(("grp", "hd"), None, None),
            P("grp"),
            P(("grp", "hd"), None, None),
            P(None, None, ("grp", "hd")),
            P(None, None, ("grp", "hd")),
            P(None, ("grp", "hd")),
            P(None, ("grp", "hd")),
            P(None, ("grp", "hd")),
            P(None, None, ("grp", "hd")),
            P(None, None, ("grp", "hd")),
            P(None, None, ("grp", "hd")),
            P(None, None, ("grp", "hd")),
            P(None, ("grp", "hd")),
            P(None, ("grp", "hd")),
            P(None, ("grp", "hd")),
            P(None, ("grp", "hd")),
            P(None, ("grp", "hd")),
            P(None, ("grp", "hd")),
        ),
        out_specs=(
            P(("grp", "hd"), None, None),
            P(("grp", "hd"), None, None),
            P(("grp", "hd"), None, None),
            P(None, None, ("grp", "hd")),
            P(None, None, ("grp", "hd")),
            P(None, None, ("grp", "hd")),
            P(None, None, ("grp", "hd")),
            P(None, None, ("grp", "hd")),
            P(None, None, ("grp", "hd")),
            P(None, ("grp", "hd")),
            P(None, ("grp", "hd")),
            P(None, ("grp", "hd")),
            P(None, ("grp", "hd")),
            P(None, ("grp", "hd")),
            P(None, ("grp", "hd")),
            P(None, ("grp", "hd")),
            P(None, ("grp", "hd")),
            P(("grp", "hd")),
            P(None, ("grp", "hd")),
        ),
        check_vma=False,
    )
```

```python
import functools

import jax
import jax.numpy as jnp
from jax import lax
from jax.experimental import pallas as pl
from jax.experimental.pallas import tpu as pltpu
from jax.sharding import PartitionSpec as P

NH = 8
STEP = 5
AXES = ("grp", "hd")

MIB = 1 << 20
F32, LOW = jnp.float32, jnp.bfloat16
VMEM = pl.BlockSpec(memory_space=pltpu.VMEM)
SMEM = pl.BlockSpec(memory_space=pltpu.SMEM)


ANY = pl.BlockSpec(memory_space=pl.ANY)


def adamw(weight, grad, first_old, second_old, learn_rate, decay):
    first_new = 0.5 * first_old + 0.5 * grad
    second_new = 0.5 * second_old + 0.5 * grad * grad
    correction = 1.0 - 0.5**STEP
    normed_step = first_new / correction / (jnp.sqrt(second_new / correction) + 1e-08)
    return (first_new, second_new, weight - learn_rate * (normed_step + decay * weight))


def log2(n):
    return n.bit_length() - 1


def outer_bits(groups, depth):
    first, last = log2(depth) + 1, log2(depth) + log2(groups)
    middle = (first + last) // 2
    return list(range(first, middle)), list(range(middle, last))


def swap(block, bit, total):
    return lax.ppermute(block, AXES, [(j, j ^ (1 << bit)) for j in range(total)])


def spread_of(order, core, total):
    bits = list(order) + [core]
    return tuple(sum(((p >> t) & 1) << b for t, b in enumerate(bits)) for p in range(total))


def added(a, b):
    return (a.astype(F32) + b.astype(F32)).astype(LOW)


def device_index():
    return lax.axis_index("grp") * lax.axis_size("hd") + lax.axis_index("hd")


def gather_steps(shard, order, core, total):
    held = shard
    for bit in order[:-1]:
        (came,) = yield [functools.partial(swap, held, bit, total)]
        held = jnp.concatenate([held, came], axis=0)
    (came,) = yield [functools.partial(swap, held, order[-1], total)]
    first, second = yield [functools.partial(swap, held, core, total), functools.partial(swap, came, core, total)]
    return [held, came, first, second]


def scatter_steps(mine, theirs, x_bit, y_bit, core, total):
    (came,) = yield [functools.partial(swap, theirs, core, total)]
    half = mine.shape[1] // 2
    away = [added(mine[k, half:], came[k, half:]) for k in range(2)]
    held = [added(mine[k, :half], came[k, :half]) for k in range(2)]
    came = yield [functools.partial(swap, block, bit, total) for block, bit in zip(away, (y_bit, x_bit))]
    half //= 2
    away = [added(held[k][half:], came[k][half:]) for k in range(2)]
    held = [added(held[k][:half], came[k][:half]) for k in range(2)]
    came = yield [functools.partial(swap, block, bit, total) for block, bit in zip(away, (x_bit, y_bit))]
    both = jnp.stack([added(held[k], came[k]) for k in range(2)], axis=1)
    (came,) = yield [functools.partial(lax.all_to_all, both, "hd", 0, 0, tiled=True)]
    return jnp.sum(came.astype(F32), axis=0)


class Chain:
    def __init__(self, steps):
        self.steps, self.result, self.under_way = steps, None, None
        self.wanted = next(steps)

    def start(self):
        if self.under_way is None:
            self.under_way = [exchange() for exchange in self.wanted]

    def advance(self, came):
        self.under_way = None
        try:
            self.wanted = self.steps.send(came)
        except StopIteration as stop:
            self.wanted, self.result = [], stop.value


def in_round(chains, compute=None, *beside, longer=()):
    chains = [chain for chain in chains if chain.wanted]
    for chain in chains:
        chain.start()
    ending = [chain for chain in chains if chain not in longer]
    done = compute() if compute else ()
    came, done, beside = lax.optimization_barrier(([chain.under_way for chain in ending], done, beside))
    for chain, blocks in zip(ending, came):
        chain.advance(blocks)
    return beside[0] if beside else done


def place_blocks(refs, spread, dst, rows, sem):
    if spread is None:
        pltpu.make_async_copy(refs[0].at[:, rows], dst, sem).start()
        return
    me, each = device_index(), len(spread) // 4
    for p, mask in enumerate(spread):
        pltpu.make_async_copy(refs[p // each].at[p % each, rows], dst.at[me ^ mask], sem).start()


def cut_blocks(halves, refs, depth, sems, masks=range(32)):
    me = device_index()
    for mask in masks:
        owner = me ^ mask
        place = mask // (2 * depth)
        for half, src_of, rows in halves:
            group = place if half == 0 else place // 2 + place % 2 * 2
            dst = refs[mask // depth % 2].at[half, group * depth + (owner & (depth - 1))]
            dst = dst if rows is None else dst.at[rows]
            pltpu.make_async_copy(src_of(owner), dst, sems.at[mask // depth % 2]).start()


def await_whole(refs, sems):
    for at, ref in enumerate(refs):
        pltpu.make_async_copy(ref, ref, sems.at[at]).wait()


def blocks_of(shape):
    return [jax.ShapeDtypeStruct((2, 16, *shape), LOW)] * 2


BLOCK = 512
PARTS = 4
CALLS = 2


def pack_kernel(attn_in, attn_out, w_out, w_in, cross, own, cross_out, own_out, mlp):
    rows = attn_in.shape[1]
    for at, (to, to_out) in enumerate(((cross, cross_out), (own, own_out))):
        for m in range(3):
            to[0, m * rows : (m + 1) * rows, :] = attn_in[3 * at + m].astype(LOW)
        to_out[0] = attn_out[at].astype(LOW)
    width = w_out.shape[1] // PARTS
    for c in range(PARTS):
        mlp[c * rows : (c + 1) * rows, :] = w_out[:, c * width : (c + 1) * width].astype(LOW)
    mlp[PARTS * rows :, :] = w_in[...].T.astype(LOW)


def pack(attn_in_t, attn_out_t, w_out_t, w_in):
    rows, width = attn_in_t.shape[1:]
    return pl.pallas_call(
        pack_kernel,
        out_shape=[jax.ShapeDtypeStruct((1, 3 * rows, width), LOW)] * 2
        + [jax.ShapeDtypeStruct((1, rows, width), LOW)] * 2
        + [jax.ShapeDtypeStruct((PARTS * rows + w_in.shape[1], width), LOW)],
        in_specs=[VMEM] * 4,
        out_specs=[VMEM] * 5,
        compiler_params=pltpu.CompilerParams(vmem_limit_bytes=16 * MIB),
    )(attn_in_t, attn_out_t, w_out_t, w_in)


def from_all(own):
    total = lax.axis_size("grp") * lax.axis_size("hd")
    return lax.all_to_all(jnp.broadcast_to(own[None], (total, *own.shape)), AXES, 0, 0, tiled=True)


def gather_gains(gains):
    rows = gains.shape[0]
    every = from_all(gains.astype(LOW).reshape(-1)).astype(F32)
    return jnp.swapaxes(every.reshape(every.shape[0], rows, -1), 0, 1).reshape(rows, -1)


def scatter_gains(grads):
    total = lax.axis_size("grp") * lax.axis_size("hd")
    rows = grads.shape[0]
    blocks = jnp.swapaxes(grads.reshape(rows, total, -1), 0, 1).reshape(total, -1)
    came = lax.all_to_all(blocks, AXES, 0, 0, tiled=True)
    return jnp.sum(came, axis=0).reshape(rows, -1)


def dot_nn(a, b):
    return lax.dot_general(a, b, (((1,), (0,)), ((), ())), preferred_element_type=F32)


def dot_nt(a, b):
    return lax.dot_general(a, b, (((1,), (1,)), ((), ())), preferred_element_type=F32)


def dot_tn(a, b):
    return lax.dot_general(a, b, (((0,), (0,)), ((), ())), preferred_element_type=F32)


def unit_rows(rows):
    inverse = lax.rsqrt(jnp.mean(rows * rows, axis=-1, keepdims=True) + 1e-06)
    return rows * inverse, inverse


def norm_grad(rows, gain, upstream):
    unit, inverse = unit_rows(rows)
    scaled = upstream * gain
    inner = jnp.mean(scaled * unit, axis=-1, keepdims=True)
    return (scaled - unit * inner) * inverse, jnp.sum(upstream * unit, axis=0, keepdims=True)


def head_scores(query, key, count, scale):
    scores = dot_nt(query, key) * scale
    if count is not None:
        place = lax.broadcasted_iota(jnp.int32, scores.shape, 1)
        scores = jnp.where(place < count, scores, -1e30)
    return scores


def matrix(weights):
    return weights[...].reshape(-1, weights.shape[2])


def attend_kernel(cross, images, size, spreads, *refs):
    if cross:
        counts, gains, source, target, *refs = refs
    else:
        gains, target, *refs = refs
        counts, source = None, target
    *pieces, q_out, k_out, v_out, context_out, sum_out, log_out, whole, weights, sems, out_sem = refs
    rows = weights.shape[2]
    count = len(pieces) // 2
    for m in (1, 2, 0):
        place_blocks(pieces[:count], spreads[0], weights.at[m], pl.ds(m * rows, rows), sems.at[m])
    place_blocks(pieces[count:], spreads[1], weights.at[3], slice(None), sems.at[3])

    def arrived(m):
        pltpu.make_async_copy(weights.at[m], weights.at[m], sems.at[m]).wait()
        return matrix(weights.at[m])

    key_gain, query_gain = (0, 1) if cross else (2, 2)
    rows = source[...].astype(F32)
    normal = (unit_rows(rows)[0] * gains[key_gain : key_gain + 1, :]).astype(LOW)
    k_out[...] = dot_nt(normal, arrived(1)).astype(LOW)
    v_out[...] = dot_nt(normal, arrived(2)).astype(LOW)
    if cross:
        rows = target[...].astype(F32)
        normal = (unit_rows(rows)[0] * gains[query_gain : query_gain + 1, :]).astype(LOW)
    q_out[...] = dot_nt(normal, arrived(0)).astype(LOW)
    out_weights = arrived(3)
    keep = pltpu.make_async_copy(weights, whole, out_sem)
    keep.start()
    width = q_out.shape[1] // NH
    scale = width ** (-0.5)

    def one_image(image, carry):
        span = pl.ds(pl.multiple_of(image * size, size), size)
        count = counts[image] if cross else None
        for h in range(NH):
            part = slice(h * width, (h + 1) * width)
            scores = head_scores(q_out[span, part], k_out[span, part], count, scale)
            highest = jnp.max(scores, axis=-1, keepdims=True)
            exponent = jnp.exp(scores - highest)
            row_total = jnp.sum(exponent, axis=-1, keepdims=True)
            probs = (exponent * (1.0 / row_total)).astype(LOW)
            context_out[span, part] = dot_nn(probs, v_out[span, part]).astype(LOW)
            log_out[span, h : h + 1] = highest + jnp.log(row_total)
        return carry

    lax.fori_loop(0, images, one_image, 0)
    sum_out[...] = target[...].astype(F32) + dot_nt(context_out[...], out_weights)
    keep.wait()


def attend_block(gains, source, target, counts, pieces, spreads, images):
    cross = source is not None
    rows, width = target.shape
    low = jax.ShapeDtypeStruct((rows, width), LOW)
    weights = (4, 32, width // 32, width)
    head = (counts, gains, source, target) if cross else (gains, target)
    return pl.pallas_call(
        functools.partial(attend_kernel, cross, images, rows // images, spreads),
        out_shape=[low] * 4
        + [jax.ShapeDtypeStruct(shape, F32) for shape in ((rows, width), (rows, NH))]
        + [jax.ShapeDtypeStruct(weights, LOW)],
        in_specs=([SMEM] if cross else []) + [VMEM] * (3 if cross else 2) + [ANY] * len(pieces),
        out_specs=[VMEM] * 6 + [ANY],
        scratch_shapes=[pltpu.VMEM(weights, LOW), pltpu.SemaphoreType.DMA((4,)), pltpu.SemaphoreType.DMA],
        compiler_params=pltpu.CompilerParams(vmem_limit_bytes=48 * MIB),
        cost_estimate=pl.CostEstimate(
            flops=8 * rows * width * width + 4 * rows * width * (rows // images),
            bytes_accessed=12 * rows * width + 8 * width * width,
            transcendentals=rows * NH * (rows // images),
        ),
    )(*head, *pieces)


def fetch(whole, members, scratch, sems):
    copies = []
    for at, (m, to) in enumerate(zip(members, scratch)):
        copies.append(pltpu.make_async_copy(whole.at[m], to, sems.at[at]))
        copies[-1].start()
    return copies


def scores_grad_kernel(cross, images, size, *refs):
    if cross:
        counts, *refs = refs
    (upstream, q_in, k_in, v_in, context_in, log_in, whole, dq, dk, dv, dc, wo_v, sems) = refs
    (copy,) = fetch(whole, (3,), (wo_v,), sems)
    up_low = upstream[...].astype(LOW)
    copy.wait()
    dc[...] = dot_nn(up_low, matrix(wo_v)).astype(LOW)
    width = q_in.shape[1] // NH
    scale = width ** (-0.5)

    def one_image(image, carry):
        span = pl.ds(pl.multiple_of(image * size, size), size)
        count = counts[image] if cross else None
        for h in range(NH):
            part = slice(h * width, (h + 1) * width)
            query, key, value, grad = q_in[span, part], k_in[span, part], v_in[span, part], dc[span, part]
            probs = jnp.exp(head_scores(query, key, count, scale) - log_in[span, h : h + 1])
            prob_grad = dot_nt(grad, value)
            dv[span, part] = dot_tn(probs.astype(LOW), grad).astype(LOW)
            inner = jnp.sum(grad.astype(F32) * context_in[span, part].astype(F32), axis=-1, keepdims=True)
            score_grad = probs * (prob_grad - inner)
            score_grad = score_grad.astype(LOW)
            dq[span, part] = (dot_nn(score_grad, key) * scale).astype(LOW)
            dk[span, part] = (dot_tn(score_grad, query) * scale).astype(LOW)
        return carry

    lax.fori_loop(0, images, one_image, 0)


def scores_grad(counts, upstream, saved, whole, images):
    cross = counts is not None
    rows, width = upstream.shape
    return pl.pallas_call(
        functools.partial(scores_grad_kernel, cross, images, rows // images),
        out_shape=[jax.ShapeDtypeStruct((rows, width), LOW)] * 3,
        in_specs=([SMEM] if cross else []) + [VMEM] * 6 + [ANY],
        out_specs=[VMEM] * 3,
        scratch_shapes=[
            pltpu.VMEM((rows, width), LOW),
            pltpu.VMEM(whole.shape[1:], LOW),
            pltpu.SemaphoreType.DMA((1,)),
        ],
        compiler_params=pltpu.CompilerParams(vmem_limit_bytes=48 * MIB),
        cost_estimate=pl.CostEstimate(
            flops=2 * rows * width * width + 10 * rows * width * (rows // images),
            bytes_accessed=18 * rows * width + 4 * width * width,
            transcendentals=rows * NH * (rows // images),
        ),
    )(*([counts] if cross else []), upstream, *saved, whole)


def matrix_shares(count, rows):
    shares = []
    for m in range(count // 2 * 2):
        shares.append((m % 2, m, 0, rows, m // 2 * rows))
    if count % 2:
        for half in range(2):
            shares.append((half, count - 1, half * rows // 2, rows // 2, count // 2 * rows))
    return shares


def matrix_blocks(sums, count, rows):
    parts = [[] for _ in range(count)]
    for half, m, _, length, at in matrix_shares(count, rows):
        parts[m].append(sums[half, at : at + length])
    return [part[0] if len(part) == 1 else jnp.concatenate(part, axis=0) for part in parts]


def matrix_grad_kernel(cross, depth, *refs):
    if cross:
        gains, source, target, *refs = refs
    else:
        gains, target, *refs = refs
    upstream, context, dq, dk, dv, *refs = refs
    *outs, grads, sems = refs
    key_gain, query_gain = (0, 1) if cross else (2, 2)
    width = target.shape[1]

    def finish(m, grad):
        grads[m] = grad.astype(LOW)
        if depth is None:
            pltpu.make_async_copy(grads.at[m], outs[m], sems.at[m]).start()
            return
        rows = width // 32

        def part(first, count):
            return lambda owner: grads.at[m, pl.ds(pl.multiple_of(owner * rows + first, count), count), :]

        halves = [
            (half, part(first, count), pl.ds(at, count)) for half, m_at, first, count, at in matrix_shares(grads.shape[0], rows) if m_at == m
        ]
        cut_blocks(halves, outs, depth, sems)

    rows = target[...].astype(F32)
    normal = (unit_rows(rows)[0] * gains[query_gain : query_gain + 1, :]).astype(LOW)
    finish(0, dot_tn(dq[...], normal))
    if cross:
        rows = source[...].astype(F32)
        normal = (unit_rows(rows)[0] * gains[key_gain : key_gain + 1, :]).astype(LOW)
    finish(1, dot_tn(dk[...], normal))
    finish(2, dot_tn(dv[...], normal))
    finish(3, dot_tn(upstream[...].astype(LOW), context[...]))
    await_whole(outs, sems)


def matrix_grads(gains, source, target, upstream, context, score_grads, depth):
    cross = source is not None
    rows, width = target.shape
    head = (gains, source, target) if cross else (gains, target)
    count = 4
    if depth is None:
        out_shape = [jax.ShapeDtypeStruct((width, width), LOW)] * count
    else:
        out_shape = blocks_of((count * width // 64, width))
    return pl.pallas_call(
        functools.partial(matrix_grad_kernel, cross, depth),
        out_shape=out_shape,
        in_specs=[VMEM] * (len(head) + 5),
        out_specs=[ANY] * len(out_shape),
        scratch_shapes=[pltpu.VMEM((count, width, width), LOW), pltpu.SemaphoreType.DMA((len(out_shape),))],
        compiler_params=pltpu.CompilerParams(vmem_limit_bytes=48 * MIB),
        cost_estimate=pl.CostEstimate(
            flops=2 * count * rows * width * width,
            bytes_accessed=16 * rows * width + 2 * count * width * width,
            transcendentals=rows,
        ),
    )(*head, upstream, context, *score_grads)


def project_grad_kernel(cross, *refs):
    if cross:
        gains, source, target, *refs = refs
    else:
        gains, target, *refs = refs
    (upstream, dq, dk, dv, whole, *refs) = refs
    outs = 2 if cross else 1
    grads_out, gain_outs = refs[:outs], refs[outs : 2 * outs]
    (wq_v, wk_v, wv_v, sems) = refs[2 * outs :]
    copies = fetch(whole, (0, 1, 2), (wq_v, wk_v, wv_v), sems)
    key_gain, query_gain = (0, 1) if cross else (2, 2)
    rows = target[...].astype(F32)
    gain = gains[query_gain : query_gain + 1, :]
    copies[0].wait()
    back = dot_nn(dq[...], matrix(wq_v))
    copies[1].wait()
    copies[2].wait()
    if cross:
        extra, gain_grad = norm_grad(rows, gain, back)
        grads_out[0][...] = upstream[...] + extra
        gain_outs[0][...] = gain_grad
        rows = source[...].astype(F32)
        gain = gains[key_gain : key_gain + 1, :]
        back = dot_nn(dk[...], matrix(wk_v))
    else:
        back += dot_nn(dk[...], matrix(wk_v))
    back += dot_nn(dv[...], matrix(wv_v))
    extra, gain_grad = norm_grad(rows, gain, back)
    if cross:
        grads_out[1][...] = extra
    else:
        grads_out[0][...] = upstream[...] + extra
    gain_outs[-1][...] = gain_grad


def project_grad(gains, source, target, upstream, score_grads, whole):
    cross = source is not None
    rows, width = target.shape
    outs = 2 if cross else 1
    head = (gains, source, target) if cross else (gains, target)
    result = pl.pallas_call(
        functools.partial(project_grad_kernel, cross),
        out_shape=[jax.ShapeDtypeStruct((rows, width), F32)] * outs + [jax.ShapeDtypeStruct((1, width), F32)] * outs,
        in_specs=[VMEM] * (len(head) + 4) + [ANY],
        out_specs=[VMEM] * (2 * outs),
        scratch_shapes=[pltpu.VMEM(whole.shape[1:], LOW)] * 3
        + [pltpu.SemaphoreType.DMA((3,))],
        compiler_params=pltpu.CompilerParams(vmem_limit_bytes=48 * MIB),
        cost_estimate=pl.CostEstimate(
            flops=6 * rows * width * width, bytes_accessed=20 * rows * width + 6 * width * width, transcendentals=rows
        ),
    )(*head, upstream, *score_grads, whole)
    return result[:outs], result[outs:]


def fetch_bands(bands, copies, sems):
    for at, (first, to) in enumerate(copies):
        pltpu.make_async_copy(bands.at[:, pl.ds(first, to.shape[1])], to, sems.at[at]).start()

    def wait():
        for at, (_, to) in enumerate(copies):
            pltpu.make_async_copy(to, to, sems.at[at]).wait()

    return wait


def mlp_forward_kernel(call, depth, second, cotangent, *refs):
    if call == 0:
        gain_row, bands, normal, partial, hidden_grad, *refs = refs
    else:
        normal, skip, bands, out, hidden_grad, *refs = refs
    *outs, cot_t, total, lower_v, lift_v, grad_v, sems, send_sems = refs
    step = pl.program_id(0)
    parts, last_step = PARTS // CALLS, pl.num_programs(0) - 1

    @pl.when(step == 0)
    def first():
        rows = lower_v.shape[2]
        copies = [((call * parts + c) * rows, lower_v.at[c]) for c in range(parts)]
        wait = fetch_bands(bands, copies, sems)
        count, units = lift_v.shape[:2]
        lift = pltpu.make_async_copy(
            bands.at[pl.ds(call * count, count), pl.ds(PARTS * rows, units)], lift_v, sems.at[parts]
        )
        lift.start()
        if call == 0:
            normal[...] = (unit_rows(second[...])[0] * gain_row[...]).astype(LOW)
        cot_t[...] = cotangent[...].T
        total[...] = second[...]
        lift.wait()
        wait()

    units = lift_v.shape[1]
    lift = lift_v[pl.ds(step * (BLOCK // units), BLOCK // units)].reshape(BLOCK, -1)
    share = lower_v.shape[3] // BLOCK
    span = pl.ds(pl.multiple_of(step % share * BLOCK, BLOCK), BLOCK)
    lower = lower_v[step // share, :, :, span].reshape(-1, BLOCK)
    hidden = dot_nt(normal[...], lift)
    square = hidden * hidden
    root = 0.7978845608028654
    tanh = jnp.tanh(root * hidden * (1.0 + 0.044715 * square))
    half = 0.5 * (1.0 + tanh)
    active = (hidden * half).astype(LOW)
    slope = half + 0.5 * hidden * (1.0 - tanh * tanh) * (root * (1.0 + 3 * 0.044715 * square))
    grad_v[:, pl.ds(pl.multiple_of(step * BLOCK, BLOCK), BLOCK)] = dot_nn(cot_t[...], active).astype(LOW)
    total[...] += dot_nt(active, lower)
    hidden_grad[...] = (dot_nn(cotangent[...], lower) * slope).astype(LOW)

    for half in range(2):
        size = grad_v.shape[1] // 2

        @pl.when(step == (half + 1) * size // BLOCK - 1)
        def send():
            columns = pl.ds(half * size, size)
            if depth is None:
                pltpu.make_async_copy(grad_v.at[:, columns], outs[0].at[:, columns], send_sems.at[0]).start()
                return
            rows = grad_v.shape[0] // 32
            src_of = lambda owner: grad_v.at[pl.ds(pl.multiple_of(owner * rows, rows), rows), columns]
            cut_blocks([(half, src_of, None)], outs, depth, send_sems)

    @pl.when(step == last_step)
    def last():
        if call == 0:
            partial[...] = total[...]
        else:
            out[...] = (total[...] + skip[...].astype(F32)).astype(LOW)
        await_whole(outs, send_sems)


def mlp_forward(call, second, cotangent, others, bands, hidden, depth):
    rows, width = second.shape
    units, parts = hidden // CALLS, PARTS // CALLS
    whole = lambda shape: pl.BlockSpec(shape, lambda f: (0, 0), pipeline_mode=pl.Buffered(1))
    once = lambda shape: pl.BlockSpec(shape, lambda f: (0, 0))
    low = jax.ShapeDtypeStruct((rows, width), LOW)
    if depth is None:
        outs = [jax.ShapeDtypeStruct((width, units), LOW)]
    else:
        outs = blocks_of((width // 32, units // 2))
    return pl.pallas_call(
        functools.partial(mlp_forward_kernel, call, depth),
        grid=(units // BLOCK,),
        out_shape=[low]
        + [jax.ShapeDtypeStruct((rows, width), F32)] * (call == 0)
        + [jax.ShapeDtypeStruct((rows, units), LOW)]
        + outs,
        in_specs=[whole((rows, width))] * 2 + [whole(other.shape) for other in others] + [ANY],
        out_specs=[once((rows, width))] * (2 if call == 0 else 1)
        + [pl.BlockSpec((rows, BLOCK), lambda f: (0, f))]
        + [ANY] * len(outs),
        scratch_shapes=[
            pltpu.VMEM((width, rows), LOW),
            pltpu.VMEM((rows, width), F32),
            pltpu.VMEM((parts, 32, width // 32, units // parts), LOW),
            pltpu.VMEM((32 // CALLS, hidden // 32, width), LOW),
            pltpu.VMEM((width, units), LOW),
            pltpu.SemaphoreType.DMA((parts + 1,)),
            pltpu.SemaphoreType.DMA((len(outs),)),
        ],
        compiler_params=pltpu.CompilerParams(vmem_limit_bytes=56 * MIB),
        cost_estimate=pl.CostEstimate(
            flops=8 * rows * width * units,
            bytes_accessed=6 * width * units + 12 * rows * width + 2 * rows * units,
            transcendentals=rows * units,
        ),
    )(second, cotangent, *others, bands)


def mlp_backward_kernel(depth, gain_row, second, cotangent, normal, hidden_grad0, hidden_grad1, bands, *refs):
    second_grad, gain_grad, *refs = refs
    *outs, normal_t, back, lift_v, grad_v, sem, send_sems = refs
    step = pl.program_id(0)
    steps = pl.num_programs(0)

    @pl.when(step == 0)
    def first():
        units = lift_v.shape[1]
        lift = pltpu.make_async_copy(bands.at[:, pl.ds(bands.shape[1] - units, units)], lift_v, sem)
        lift.start()
        normal_t[...] = normal[...].T
        back[...] = jnp.zeros_like(back)
        lift.wait()

    units = lift_v.shape[1]
    share = BLOCK // units
    lift = lift_v[pl.ds(step * share, share)].reshape(BLOCK, -1)
    hidden_grad = jnp.where(step < steps // 2, hidden_grad0[...], hidden_grad1[...])
    grad_v[step] = dot_nn(normal_t[...], hidden_grad).astype(LOW)
    back[...] += dot_nn(hidden_grad, lift)

    if depth is None:
        start = pl.multiple_of(step * BLOCK, BLOCK)
        pltpu.make_async_copy(grad_v.at[step], outs[0].at[:, pl.ds(start, BLOCK)], send_sems.at[0]).start()
    else:
        me = device_index()
        for group in range(32 // share):

            @pl.when(step == (me // share) ^ group)
            def send():
                size = grad_v.shape[1] // 2

                def part(half):
                    return lambda owner: grad_v.at[
                        step, pl.ds(half * size, size), pl.ds(pl.multiple_of(owner % share * units, units), units)
                    ]

                halves = [(half, part(half), None) for half in range(2)]
                cut_blocks(halves, outs, depth, send_sems, range(group * share, (group + 1) * share))

    @pl.when(step == steps - 1)
    def last():
        extra, gains = norm_grad(second[...], gain_row[...], back[...])
        second_grad[...] = cotangent[...].astype(F32) + extra
        gain_grad[...] = gains
        await_whole(outs, send_sems)


def mlp_backward(gain_row, second, cotangent, normal, hidden_grads, bands, hidden, depth):
    rows, width = second.shape
    whole = lambda shape: pl.BlockSpec(shape, lambda f: (0, 0), pipeline_mode=pl.Buffered(1))
    once = lambda shape: pl.BlockSpec(shape, lambda f: (0, 0))
    half = hidden // BLOCK // 2
    if depth is None:
        outs = [jax.ShapeDtypeStruct((width, hidden), LOW)]
    else:
        outs = blocks_of((width // 2, hidden // 32))
    return pl.pallas_call(
        functools.partial(mlp_backward_kernel, depth),
        grid=(hidden // BLOCK,),
        out_shape=[jax.ShapeDtypeStruct((rows, width), F32), jax.ShapeDtypeStruct((1, width), F32)] + outs,
        in_specs=[whole((1, width))]
        + [whole((rows, width))] * 3
        + [
            pl.BlockSpec((rows, BLOCK), lambda f: (0, jnp.minimum(f, half - 1))),
            pl.BlockSpec((rows, BLOCK), lambda f: (0, jnp.maximum(f - half, 0))),
            ANY,
        ],
        out_specs=[once((rows, width)), once((1, width))] + [ANY] * len(outs),
        scratch_shapes=[
            pltpu.VMEM((width, rows), LOW),
            pltpu.VMEM((rows, width), F32),
            pltpu.VMEM((32, hidden // 32, width), LOW),
            pltpu.VMEM((hidden // BLOCK, width, BLOCK), LOW),
            pltpu.SemaphoreType.DMA,
            pltpu.SemaphoreType.DMA((len(outs),)),
        ],
        compiler_params=pltpu.CompilerParams(vmem_limit_bytes=56 * MIB),
        cost_estimate=pl.CostEstimate(
            flops=4 * rows * width * hidden,
            bytes_accessed=4 * width * hidden + 12 * rows * width + 2 * rows * hidden,
            transcendentals=0,
        ),
    )(gain_row, second, cotangent, normal, *hidden_grads, bands)


def local(
    pixels,
    latents,
    skip,
    counts,
    cotangent,
    attn_in,
    attn_out,
    w_in,
    w_out,
    gains,
    attn_in_first,
    attn_in_second,
    attn_out_first,
    attn_out_second,
    w_in_first,
    w_in_second,
    w_out_first,
    w_out_second,
    gains_first,
    gains_second,
):
    groups, depth = lax.axis_size("grp"), lax.axis_size("hd")
    total, core = groups * depth, log2(depth)
    fast = total == 32 and depth == 4
    images, size, width = latents.shape
    hidden = w_out.shape[0]
    flat = lambda rows: rows.reshape(-1, width)
    whole = lambda rows: rows.reshape(images, -1, width)
    pixel_rows, latent_rows, cot_rows = flat(pixels), flat(latents), flat(cotangent)
    attn_in_t, attn_out_t, w_out_t = jnp.swapaxes(attn_in, 1, 2), jnp.swapaxes(attn_out, 1, 2), w_out.T
    own_counts = lax.dynamic_slice_in_dim(counts, lax.axis_index("hd") * images, images)
    cut = depth if fast else None

    def cross_forward(pieces, spreads):
        return attend_block(gain_rows, pixel_rows, latent_rows, own_counts, pieces, spreads, images)

    def self_forward(pieces, spreads):
        return attend_block(gain_rows, None, first_sum, None, pieces, spreads, images)

    if fast:
        (x_bit,), (y_bit,) = outer_bits(groups, depth)
        *shards, mlp_shard = pack(attn_in_t, attn_out_t, w_out_t, w_in)
        orders = ((1, 0, x_bit, y_bit), (1, 0, y_bit, x_bit), (x_bit, y_bit, 1, 0), (y_bit, x_bit, 1, 0))
        spreads = [spread_of(order, core, total) for order in orders]
        chains = [Chain(gather_steps(shard, order, core, total)) for shard, order in zip(shards, orders)]
        in_round(chains)
        mlp_shard = in_round(chains, None, mlp_shard)
        bands = lax.all_gather(mlp_shard, AXES, axis=0)
        gain_rows = in_round(chains, lambda: gather_gains(gains))
        while any(chain.wanted for chain in chains):
            in_round(chains)
        *saved, first_sum, logs, weights = cross_forward(chains[0].result + chains[2].result, spreads[::2])
        *saved2, second_sum, logs2, weights2 = self_forward(chains[1].result + chains[3].result, spreads[1::2])
    else:
        every = lambda shard: lax.all_gather(shard.astype(LOW), AXES, axis=0, tiled=True).reshape(32, -1, shard.shape[1])
        inward = lambda m: jnp.concatenate([every(attn_in_t[3 * m + k]) for k in range(3)], axis=1)
        gain_rows = gather_gains(gains)
        lower = every(w_out_t)
        lift = lax.all_gather(w_in.astype(LOW), AXES, axis=1, tiled=True).T.reshape(32, -1, width)
        bands = jnp.concatenate([*jnp.split(lower, PARTS, axis=2), lift], axis=1)
        *saved, first_sum, logs, weights = cross_forward([inward(0), every(attn_out_t[0])], (None, None))
        *saved2, second_sum, logs2, weights2 = self_forward([inward(1), every(attn_out_t[1])], (None, None))

    normal, partial, hidden_grad0, *lower_grad0 = mlp_forward(
        0, second_sum, cot_rows, (gain_rows[3:],), bands, hidden, cut
    )

    def mlp_second():
        return mlp_forward(1, partial, cot_rows, (normal, flat(skip)), bands, hidden, cut)

    def mlp_back():
        return mlp_backward(
            gain_rows[3:], second_sum, cot_rows, normal, (hidden_grad0, hidden_grad1), bands, hidden, cut
        )

    def self_scores():
        return scores_grad(None, second_grad, (*saved2, logs2), weights2, images)

    def self_matrices():
        return matrix_grads(gain_rows, None, first_sum, second_grad, saved2[3], score_grads2, cut)

    def self_project():
        return project_grad(gain_rows, None, first_sum, second_grad, score_grads2, weights2)

    def cross_scores():
        return scores_grad(own_counts, first_grad, (*saved, logs), weights, images)

    def cross_matrices():
        return matrix_grads(gain_rows, pixel_rows, latent_rows, first_grad, saved[3], score_grads, cut)

    def cross_project():
        return project_grad(gain_rows, pixel_rows, latent_rows, first_grad, score_grads, weights)

    if fast:
        scatter = lambda blocks: Chain(scatter_steps(*blocks, x_bit, y_bit, core, total))
        live = [scatter(lower_grad0)]
        latents_out, hidden_grad1, *lower_grad1 = in_round(live, mlp_second)
        live.append(scatter(lower_grad1))
        second_grad, gain3_grad, *lift_grad = in_round(live, mlp_back)
        live.append(scatter(lift_grad))
        score_grads2 = in_round(live, self_scores)
        live.append(scatter(in_round(live, self_matrices)))
        (first_grad,), (gain2_grad,) = in_round(live, self_project)
        score_grads = in_round(live, cross_scores)
        live.append(scatter(in_round(live, cross_matrices)))
        in_round(live, longer=live[:4])
        (latents_grad, pixels_grad), (gain1_grad, gain0_grad) = in_round(live, cross_project)
        gains_grad = jnp.concatenate([gain0_grad, gain1_grad, gain2_grad, gain3_grad], axis=0)
        gains_sum = scatter_gains(gains_grad)
        while any(chain.wanted for chain in live):
            in_round(live)
        lower0, lower1, lift_sum, own, cross = [chain.result for chain in live]
        lower_sum = jnp.concatenate([*lower0, *lower1], axis=1)
        lift_sum = jnp.concatenate([*lift_sum], axis=0)
        sums, sums2 = [matrix_blocks(block, 4, attn_in.shape[2]) for block in (cross, own)]
    else:
        latents_out, hidden_grad1, lower_grad1 = mlp_second()
        second_grad, gain3_grad, lift_grad = mlp_back()
        score_grads2 = self_scores()
        grads2 = self_matrices()
        (first_grad,), (gain2_grad,) = self_project()
        score_grads = cross_scores()
        grads = cross_matrices()
        (latents_grad, pixels_grad), (gain1_grad, gain0_grad) = cross_project()
        gains_grad = jnp.concatenate([gain0_grad, gain1_grad, gain2_grad, gain3_grad], axis=0)
        gains_sum = scatter_gains(gains_grad)
        sum_of = lambda grad, along: lax.psum_scatter(grad, AXES, scatter_dimension=along, tiled=True)
        sums = [sum_of(g, 0) for g in grads]
        sums2 = [sum_of(g, 0) for g in grads2]
        lift_sum = sum_of(lift_grad, 1)
        lower_sum = sum_of(jnp.concatenate([*lower_grad0, lower_grad1], axis=1), 0)
    mixing_sum = jnp.swapaxes(jnp.stack([*sums[:3], *sums2[:3]]), 1, 2).astype(F32)
    outward_sum = jnp.swapaxes(jnp.stack([sums[3], sums2[3]]), 1, 2).astype(F32)
    mix = adamw(attn_in, mixing_sum, attn_in_first, attn_in_second, 0.05, 0.1)
    out = adamw(attn_out, outward_sum, attn_out_first, attn_out_second, 0.3, 0.1)
    lift_new = adamw(w_in, lift_sum.astype(F32), w_in_first, w_in_second, 0.05, 0.1)
    lower_new = adamw(w_out, lower_sum.T.astype(F32), w_out_first, w_out_second, 0.03, 0.1)
    gain_first, gain_second, gain_new = adamw(
        gains, gains_sum, gains_first, gains_second, 0.4, 0.0
    )
    return (
        whole(latents_out),
        whole(pixels_grad),
        whole(latents_grad),
        *mix,
        *out,
        *lift_new,
        *lower_new,
        gain_first,
        gain_second[:3],
        gain_second[3],
        gain_new,
    )


def solution(mesh):
    return jax.shard_map(
        local,
        mesh=mesh,
        in_specs=(
            P(("grp", "hd"), None, None),
            P(("grp", "hd"), None, None),
            P(("grp", "hd"), None, None),
            P("grp"),
            P(("grp", "hd"), None, None),
            P(None, None, ("grp", "hd")),
            P(None, None, ("grp", "hd")),
            P(None, ("grp", "hd")),
            P(None, ("grp", "hd")),
            P(None, ("grp", "hd")),
            P(None, None, ("grp", "hd")),
            P(None, None, ("grp", "hd")),
            P(None, None, ("grp", "hd")),
            P(None, None, ("grp", "hd")),
            P(None, ("grp", "hd")),
            P(None, ("grp", "hd")),
            P(None, ("grp", "hd")),
            P(None, ("grp", "hd")),
            P(None, ("grp", "hd")),
            P(None, ("grp", "hd")),
        ),
        out_specs=(
            P(("grp", "hd"), None, None),
            P(("grp", "hd"), None, None),
            P(("grp", "hd"), None, None),
            P(None, None, ("grp", "hd")),
            P(None, None, ("grp", "hd")),
            P(None, None, ("grp", "hd")),
            P(None, None, ("grp", "hd")),
            P(None, None, ("grp", "hd")),
            P(None, None, ("grp", "hd")),
            P(None, ("grp", "hd")),
            P(None, ("grp", "hd")),
            P(None, ("grp", "hd")),
            P(None, ("grp", "hd")),
            P(None, ("grp", "hd")),
            P(None, ("grp", "hd")),
            P(None, ("grp", "hd")),
            P(None, ("grp", "hd")),
            P(("grp", "hd")),
            P(None, ("grp", "hd")),
        ),
        check_vma=False,
    )
```

```python
import functools

import jax
import jax.numpy as jnp
from jax import lax
from jax.experimental import pallas as pl
from jax.experimental.pallas import tpu as pltpu
from jax.sharding import PartitionSpec as P

NH = 8
STEP = 5
AXES = ("grp", "hd")

MIB = 1 << 20
F32, LOW = jnp.float32, jnp.bfloat16
VMEM = pl.BlockSpec(memory_space=pltpu.VMEM)
SMEM = pl.BlockSpec(memory_space=pltpu.SMEM)


ANY = pl.BlockSpec(memory_space=pl.ANY)


def adamw(weight, grad, first_old, second_old, learn_rate, decay):
    first_new = 0.5 * first_old + 0.5 * grad
    second_new = 0.5 * second_old + 0.5 * grad * grad
    correction = 1.0 - 0.5**STEP
    normed_step = first_new / correction / (jnp.sqrt(second_new / correction) + 1e-08)
    return (first_new, second_new, weight - learn_rate * (normed_step + decay * weight))


def log2(n):
    return n.bit_length() - 1


def outer_bits(groups, depth):
    first, last = log2(depth) + 1, log2(depth) + log2(groups)
    middle = (first + last) // 2
    return list(range(first, middle)), list(range(middle, last))


def swap(block, bit, total):
    return lax.ppermute(block, AXES, [(j, j ^ (1 << bit)) for j in range(total)])


def spread_of(order, core, total):
    bits = list(order) + [core]
    return tuple(sum(((p >> t) & 1) << b for t, b in enumerate(bits)) for p in range(total))


def added(a, b):
    return (a.astype(F32) + b.astype(F32)).astype(LOW)


def device_index():
    return lax.axis_index("grp") * lax.axis_size("hd") + lax.axis_index("hd")


def gather_steps(shard, order, core, total):
    held = shard
    for bit in order[:-1]:
        (came,) = yield [functools.partial(swap, held, bit, total)]
        held = jnp.concatenate([held, came], axis=0)
    (came,) = yield [functools.partial(swap, held, order[-1], total)]
    first, second = yield [functools.partial(swap, held, core, total), functools.partial(swap, came, core, total)]
    return [held, came, first, second]


def scatter_steps(mine, theirs, x_bit, y_bit, core, total, last=False):
    (came,) = yield [functools.partial(swap, theirs, core, total)]
    half = mine.shape[1] // 2
    away = [added(mine[k, half:], came[k, half:]) for k in range(2)]
    held = [added(mine[k, :half], came[k, :half]) for k in range(2)]
    came = yield [functools.partial(swap, block, bit, total) for block, bit in zip(away, (y_bit, x_bit))]
    half //= 2
    away = [added(held[k][half:], came[k][half:]) for k in range(2)]
    held = [added(held[k][:half], came[k][:half]) for k in range(2)]
    came = yield [functools.partial(swap, block, bit, total) for block, bit in zip(away, (x_bit, y_bit))]
    both = jnp.stack([added(held[k], came[k]) for k in range(2)], axis=1)
    if last:
        (came,) = yield [functools.partial(lax.all_to_all, both, "hd", 0, 0, tiled=True)]
        return jnp.sum(came.astype(F32), axis=0)
    for bit in range(core):
        half = both.shape[0] // 2
        (came,) = yield [functools.partial(swap, both[half:], bit, total)]
        both = added(both[:half], came)
    return both[0].astype(F32)


class Chain:
    def __init__(self, steps):
        self.steps, self.result, self.under_way = steps, None, None
        self.wanted = next(steps)

    def start(self):
        if self.under_way is None:
            self.under_way = [exchange() for exchange in self.wanted]

    def advance(self, came):
        self.under_way = None
        try:
            self.wanted = self.steps.send(came)
        except StopIteration as stop:
            self.wanted, self.result = [], stop.value


def in_round(chains, compute=None, *beside, longer=()):
    chains = [chain for chain in chains if chain.wanted]
    for chain in chains:
        chain.start()
    ending = [chain for chain in chains if chain not in longer]
    done = compute() if compute else ()
    came, done, beside = lax.optimization_barrier(([chain.under_way for chain in ending], done, beside))
    for chain, blocks in zip(ending, came):
        chain.advance(blocks)
    return beside[0] if beside else done


def place_blocks(refs, spread, dst, rows, sem):
    if spread is None:
        pltpu.make_async_copy(refs[0].at[:, rows], dst, sem).start()
        return
    me, each = device_index(), len(spread) // 4
    for p, mask in enumerate(spread):
        pltpu.make_async_copy(refs[p // each].at[p % each, rows], dst.at[me ^ mask], sem).start()


def z_place(mask, owner, depth, last):
    if last:
        return owner & (depth - 1)
    return sum(((mask >> bit) & 1) << (log2(depth) - 1 - bit) for bit in range(log2(depth)))


def cut_blocks(halves, refs, depth, sems, last=False):
    me = device_index()
    for mask in range(32):
        owner = me ^ mask
        place = mask // (2 * depth)
        for half, src_of, rows in halves:
            group = place if half == 0 else place // 2 + place % 2 * 2
            dst = refs[mask // depth % 2].at[half, group * depth + z_place(mask, owner, depth, last)]
            dst = dst if rows is None else dst.at[rows]
            pltpu.make_async_copy(src_of(owner), dst, sems.at[mask // depth % 2]).start()


def bring(src, dst, sem):
    copy = pltpu.make_async_copy(src, dst, sem)
    copy.start()
    return copy


def await_whole(refs, sems):
    for at, ref in enumerate(refs):
        pltpu.make_async_copy(ref, ref, sems.at[at]).wait()


def blocks_of(shape):
    return [jax.ShapeDtypeStruct((2, 16, *shape), LOW)] * 2


BLOCK = 512
PARTS = 4
CALLS = 2


def pack_kernel(attn_in, attn_out, w_out, w_in, cross, own, cross_out, own_out, mlp):
    rows = attn_in.shape[1]
    for at, (to, to_out) in enumerate(((cross, cross_out), (own, own_out))):
        for m in range(3):
            to[0, m * rows : (m + 1) * rows, :] = attn_in[3 * at + m].astype(LOW)
        to_out[0] = attn_out[at].astype(LOW)
    width = w_out.shape[1] // PARTS
    for c in range(PARTS):
        mlp[c * rows : (c + 1) * rows, :] = w_out[:, c * width : (c + 1) * width].astype(LOW)
    mlp[PARTS * rows :, :] = w_in[...].T.astype(LOW)


def pack(attn_in_t, attn_out_t, w_out_t, w_in):
    rows, width = attn_in_t.shape[1:]
    return pl.pallas_call(
        pack_kernel,
        out_shape=[jax.ShapeDtypeStruct((1, 3 * rows, width), LOW)] * 2
        + [jax.ShapeDtypeStruct((1, rows, width), LOW)] * 2
        + [jax.ShapeDtypeStruct((PARTS * rows + w_in.shape[1], width), LOW)],
        in_specs=[VMEM] * 4,
        out_specs=[VMEM] * 5,
        compiler_params=pltpu.CompilerParams(vmem_limit_bytes=16 * MIB),
    )(attn_in_t, attn_out_t, w_out_t, w_in)


def from_all(own):
    total = lax.axis_size("grp") * lax.axis_size("hd")
    return lax.all_to_all(jnp.broadcast_to(own[None], (total, *own.shape)), AXES, 0, 0, tiled=True)


def gather_gains(gains):
    rows = gains.shape[0]
    every = from_all(gains.astype(LOW).reshape(-1)).astype(F32)
    return jnp.swapaxes(every.reshape(every.shape[0], rows, -1), 0, 1).reshape(rows, -1)


def scatter_gains(grads):
    total = lax.axis_size("grp") * lax.axis_size("hd")
    rows = grads.shape[0]
    blocks = jnp.swapaxes(grads.reshape(rows, total, -1), 0, 1).reshape(total, -1)
    came = lax.all_to_all(blocks, AXES, 0, 0, tiled=True)
    return jnp.sum(came, axis=0).reshape(rows, -1)


def dot_nn(a, b):
    return lax.dot_general(a, b, (((1,), (0,)), ((), ())), preferred_element_type=F32)


def dot_nt(a, b):
    return lax.dot_general(a, b, (((1,), (1,)), ((), ())), preferred_element_type=F32)


def dot_tn(a, b):
    return lax.dot_general(a, b, (((0,), (0,)), ((), ())), preferred_element_type=F32)


ROWS = 32


def unit_rows(rows):
    inverse = lax.rsqrt(jnp.mean(rows * rows, axis=-1, keepdims=True) + 1e-06)
    return rows * inverse, inverse


def normalise(source, gain, out):
    for at in range(0, source.shape[0], ROWS):
        span = slice(at, at + ROWS)
        out[span, :] = (unit_rows(source[span, :].astype(F32))[0] * gain).astype(LOW)


def norm_grad(source, gain, upstream, base, out, first=0):
    gain_grad = 0.0
    for at in range(0, upstream.shape[0], ROWS):
        span = slice(first + at, first + at + ROWS)
        unit, inverse = unit_rows(source[span, :].astype(F32))
        grad = upstream[at : at + ROWS]
        scaled = grad * gain
        inner = jnp.mean(scaled * unit, axis=-1, keepdims=True)
        extra = (scaled - unit * inner) * inverse
        out[span, :] = extra if base is None else base[span, :].astype(F32) + extra
        gain_grad += jnp.sum((grad * unit).reshape(ROWS // 8, 8, -1), axis=0)
    return jnp.sum(gain_grad, axis=0, keepdims=True)


SHARES = 2


def in_shares(rows, work, scratch, out, sem):
    count = rows // SHARES
    for at in range(0, rows, count):
        work(at, count)
        bring(scratch.at[at : at + count], out.at[at : at + count], sem)


def head_scores(query, key, count, scale):
    scores = dot_nt(query, key) * scale
    if count is not None:
        place = lax.broadcasted_iota(jnp.int32, scores.shape, 1)
        scores = jnp.where(place < count, scores, -1e30)
    return scores


def matrix(weights):
    return weights[...].reshape(-1, weights.shape[2])


def attend_kernel(cross, images, size, spreads, *refs):
    if cross:
        counts, gains, source, target, *refs = refs
    else:
        gains, target, *refs = refs
    *pieces, q_out, k_out, v_out, context_out, sum_out, log_out, whole, refs = *refs[:-14], *refs[-14:-7], refs[-7:]
    kept, target_v, source_v, weights, normal, total, sems = refs
    q_v, k_v, v_v, context_v = (kept.at[m] for m in range(4))
    rows = weights.shape[2]
    count = len(pieces) // 2
    come = [bring(source, source_v, sems.at[4])] if cross else []
    come.append(bring(target, target_v, sems.at[5]))
    for m in (1, 2, 0):
        place_blocks(pieces[:count], spreads[0], weights.at[m], pl.ds(m * rows, rows), sems.at[m])
    place_blocks(pieces[count:], spreads[1], weights.at[3], slice(None), sems.at[3])

    def arrived(m):
        pltpu.make_async_copy(weights.at[m], weights.at[m], sems.at[m]).wait()
        return matrix(weights.at[m])

    key_gain, query_gain = (0, 1) if cross else (2, 2)
    come[0].wait()
    normalise(source_v if cross else target_v, gains[key_gain : key_gain + 1, :], normal)
    k_v[...] = dot_nt(normal[...], arrived(1)).astype(LOW)
    leave = [bring(k_v, k_out, sems.at[6])]
    v_v[...] = dot_nt(normal[...], arrived(2)).astype(LOW)
    leave.append(bring(v_v, v_out, sems.at[7]))
    if cross:
        come[1].wait()
        normalise(target_v, gains[query_gain : query_gain + 1, :], normal)
    q_v[...] = dot_nt(normal[...], arrived(0)).astype(LOW)
    leave.append(bring(q_v, q_out, sems.at[8]))
    out_weights = arrived(3)
    leave.append(bring(weights, whole, sems.at[9]))
    width = q_v.shape[1] // NH
    scale = width ** (-0.5)

    def one_image(image, carry):
        span = pl.ds(pl.multiple_of(image * size, size), size)
        count = counts[image] if cross else None
        for h in range(NH):
            part = slice(h * width, (h + 1) * width)
            scores = head_scores(q_v[span, part], k_v[span, part], count, scale)
            highest = jnp.max(scores, axis=-1, keepdims=True)
            exponent = jnp.exp(scores - highest)
            row_total = jnp.sum(exponent, axis=-1, keepdims=True)
            probs = (exponent * (1.0 / row_total)).astype(LOW)
            context_v[span, part] = dot_nn(probs, v_v[span, part]).astype(LOW)
            log_out[span, h : h + 1] = highest + jnp.log(row_total)
        return carry

    lax.fori_loop(0, images, one_image, 0)
    leave.append(bring(context_v, context_out, sems.at[10]))

    def work(at, count):
        span = slice(at, at + count)
        total[span, :] = target_v[span, :].astype(F32) + dot_nt(context_v[span, :], out_weights)

    in_shares(total.shape[0], work, total, sum_out, sems.at[11])
    for copy in leave:
        copy.wait()
    pltpu.make_async_copy(total, sum_out, sems.at[11]).wait()


def attend_block(gains, source, target, counts, pieces, spreads, images):
    cross = source is not None
    rows, width = target.shape
    low = jax.ShapeDtypeStruct((rows, width), LOW)
    weights = (4, 32, width // 32, width)
    head = (counts, gains, source, target) if cross else (gains, target)
    return pl.pallas_call(
        functools.partial(attend_kernel, cross, images, rows // images, spreads),
        out_shape=[low] * 4
        + [jax.ShapeDtypeStruct(shape, F32) for shape in ((rows, width), (rows, NH))]
        + [jax.ShapeDtypeStruct(weights, LOW)],
        in_specs=([SMEM] if cross else []) + [VMEM] + [ANY] * (2 if cross else 1) + [ANY] * len(pieces),
        out_specs=[ANY] * 5 + [VMEM, ANY],
        scratch_shapes=[
            pltpu.VMEM((4, rows, width), LOW),
            pltpu.VMEM((rows, width), target.dtype),
            pltpu.VMEM((rows if cross else 8, width), LOW),
            pltpu.VMEM(weights, LOW),
            pltpu.VMEM((rows, width), LOW),
            pltpu.VMEM((rows, width), F32),
            pltpu.SemaphoreType.DMA((12,)),
        ],
        compiler_params=pltpu.CompilerParams(vmem_limit_bytes=48 * MIB),
        cost_estimate=pl.CostEstimate(
            flops=8 * rows * width * width + 4 * rows * width * (rows // images),
            bytes_accessed=12 * rows * width + 8 * width * width,
            transcendentals=rows * NH * (rows // images),
        ),
    )(*head, *pieces)


def scores_grad_kernel(cross, images, size, *refs):
    if cross:
        counts, *refs = refs
    upstream, q_in, k_in, v_in, context_in, log_in, whole, *refs = refs
    grads_out, (up_v, kept, grads, dc, wo_v, sems) = refs[:3], refs[3:]
    come = [bring(upstream, up_v, sems.at[0]), bring(whole.at[3], wo_v, sems.at[1])]
    come += [bring(src, kept.at[m], sems.at[2 + m]) for m, src in enumerate((q_in, k_in, v_in, context_in))]
    q_v, k_v, v_v, context_v = (kept.at[m] for m in range(4))
    dq, dk, dv = (grads.at[m] for m in range(3))
    for copy in come[:2]:
        copy.wait()
    dc[...] = dot_nn(up_v[...].astype(LOW), matrix(wo_v)).astype(LOW)
    for copy in come[2:]:
        copy.wait()
    width = q_v.shape[1] // NH
    scale = width ** (-0.5)

    def one_image(image, carry):
        span = pl.ds(pl.multiple_of(image * size, size), size)
        count = counts[image] if cross else None
        for h in range(NH):
            part = slice(h * width, (h + 1) * width)
            query, key, value, grad = q_v[span, part], k_v[span, part], v_v[span, part], dc[span, part]
            probs = jnp.exp(head_scores(query, key, count, scale) - log_in[span, h : h + 1])
            prob_grad = dot_nt(grad, value)
            dv[span, part] = dot_tn(probs.astype(LOW), grad).astype(LOW)
            inner = jnp.sum(grad.astype(F32) * context_v[span, part].astype(F32), axis=-1, keepdims=True)
            score_grad = (probs * (prob_grad - inner)).astype(LOW)
            dq[span, part] = (dot_nn(score_grad, key) * scale).astype(LOW)
            dk[span, part] = (dot_tn(score_grad, query) * scale).astype(LOW)
        for m, to in enumerate(grads_out):
            pltpu.make_async_copy(grads.at[m, span], to.at[span], sems.at[6 + m]).start()
        return carry

    lax.fori_loop(0, images, one_image, 0)
    await_whole(grads_out, sems.at[pl.ds(6, 3)])


def scores_grad(counts, upstream, saved, whole, images):
    cross = counts is not None
    rows, width = upstream.shape
    return pl.pallas_call(
        functools.partial(scores_grad_kernel, cross, images, rows // images),
        out_shape=[jax.ShapeDtypeStruct((rows, width), LOW)] * 3,
        in_specs=([SMEM] if cross else []) + [ANY] * 5 + [VMEM, ANY],
        out_specs=[ANY] * 3,
        scratch_shapes=[
            pltpu.VMEM((rows, width), F32),
            pltpu.VMEM((4, rows, width), LOW),
            pltpu.VMEM((3, rows, width), LOW),
            pltpu.VMEM((rows, width), LOW),
            pltpu.VMEM(whole.shape[1:], LOW),
            pltpu.SemaphoreType.DMA((9,)),
        ],
        compiler_params=pltpu.CompilerParams(vmem_limit_bytes=48 * MIB),
        cost_estimate=pl.CostEstimate(
            flops=2 * rows * width * width + 10 * rows * width * (rows // images),
            bytes_accessed=18 * rows * width + 4 * width * width,
            transcendentals=rows * NH * (rows // images),
        ),
    )(*([counts] if cross else []), upstream, *saved, whole)


def matrix_shares(count, rows):
    shares = []
    for m in range(count // 2 * 2):
        shares.append((m % 2, m, 0, rows, m // 2 * rows))
    if count % 2:
        for half in range(2):
            shares.append((half, count - 1, half * rows // 2, rows // 2, count // 2 * rows))
    return shares


def matrix_blocks(sums, count, rows):
    parts = [[] for _ in range(count)]
    for half, m, _, length, at in matrix_shares(count, rows):
        parts[m].append(sums[half, at : at + length])
    return [part[0] if len(part) == 1 else jnp.concatenate(part, axis=0) for part in parts]


def matrix_grad_kernel(cross, depth, *refs):
    gains, *refs = refs
    ins, (*outs, target_v, source_v, up_v, kept, grads, normal, sems, send_sems) = refs[: 6 + cross], refs[6 + cross :]
    to = [source_v] * cross + [target_v, up_v] + [kept.at[m] for m in (3, 0, 1, 2)]
    order = (1, 4, 0, 5, 6, 2, 3) if cross else (0, 3, 4, 5, 1, 2)
    come = {at: bring(ins[at], to[at], sems.at[at]) for at in order}
    dq, dk, dv, context = (kept.at[m] for m in range(4))
    key_gain, query_gain = (0, 1) if cross else (2, 2)
    width = target_v.shape[1]

    def finish(m, grad):
        grads[m] = grad.astype(LOW)
        if depth is None:
            bring(grads.at[m], outs[m], send_sems.at[m])
            return
        rows = width // 32

        def part(first, count):
            return lambda owner: grads.at[m, pl.ds(pl.multiple_of(owner * rows + first, count), count), :]

        halves = [
            (half, part(first, count), pl.ds(at, count))
            for half, m_at, first, count, at in matrix_shares(grads.shape[0], rows)
            if m_at == m
        ]
        cut_blocks(halves, outs, depth, send_sems, last=cross)

    come[cross].wait()
    normalise(target_v, gains[query_gain : query_gain + 1, :], normal)
    come[3 + cross].wait()
    finish(0, dot_tn(dq[...], normal[...]))
    if cross:
        come[0].wait()
        normalise(source_v, gains[key_gain : key_gain + 1, :], normal)
    come[4 + cross].wait()
    finish(1, dot_tn(dk[...], normal[...]))
    come[5 + cross].wait()
    finish(2, dot_tn(dv[...], normal[...]))
    come[1 + cross].wait()
    come[2 + cross].wait()
    finish(3, dot_tn(up_v[...].astype(LOW), context[...]))
    await_whole(outs, send_sems)


def matrix_grads(gains, source, target, upstream, context, score_grads, depth):
    cross = source is not None
    rows, width = target.shape
    head = (gains, source, target) if cross else (gains, target)
    count = 4
    if depth is None:
        out_shape = [jax.ShapeDtypeStruct((width, width), LOW)] * count
    else:
        out_shape = blocks_of((count * width // 64, width))
    return pl.pallas_call(
        functools.partial(matrix_grad_kernel, cross, depth),
        out_shape=out_shape,
        in_specs=[VMEM] + [ANY] * (len(head) + 4),
        out_specs=[ANY] * len(out_shape),
        scratch_shapes=[
            pltpu.VMEM((rows, width), target.dtype),
            pltpu.VMEM((rows if cross else 8, width), LOW),
            pltpu.VMEM((rows, width), F32),
            pltpu.VMEM((4, rows, width), LOW),
            pltpu.VMEM((count, width, width), LOW),
            pltpu.VMEM((rows, width), LOW),
            pltpu.SemaphoreType.DMA((7,)),
            pltpu.SemaphoreType.DMA((len(out_shape),)),
        ],
        compiler_params=pltpu.CompilerParams(vmem_limit_bytes=48 * MIB),
        cost_estimate=pl.CostEstimate(
            flops=2 * count * rows * width * width,
            bytes_accessed=16 * rows * width + 2 * count * width * width,
            transcendentals=rows,
        ),
    )(*head, upstream, context, *score_grads)


def project_grad_kernel(cross, *refs):
    gains, *refs = refs
    ins, refs = refs[: 6 + cross], refs[6 + cross :]
    outs = 1 + cross
    grads_out, gain_outs, (target_v, source_v, up_v, kept, weights, result, sems) = refs[:outs], refs[outs : 2 * outs], refs[2 * outs :]
    whole = ins[-1]
    inputs = list(ins[:-1])
    to = [source_v] * cross + [target_v, up_v] + [kept.at[m] for m in range(3)]
    order = (3, 1, 2, 4, 5, 0) if cross else (2, 3, 4, 0, 1)
    come, used = {}, 0
    for at in order:
        come[at] = bring(inputs[at], to[at], sems.at[at])
        if at >= 2 + cross:
            m = at - 2 - cross
            come["w%d" % m] = bring(whole.at[m], weights.at[m], sems.at[6 + m])
    dq, dk, dv = (kept.at[m] for m in range(3))
    key_gain, query_gain = (0, 1) if cross else (2, 2)
    rows = target_v.shape[0]

    def back_through(members, few):
        return sum(dot_nn(kept[m, few, :], matrix(weights.at[m])) for m in members)

    def shares(which, members, source, gain, base):
        gain_grads = []

        def work(at, count):
            back = back_through(members, slice(at, at + count))
            gain_grads.append(norm_grad(source, gain, back, base, result.at[which], at))

        in_shares(rows, work, result.at[which], grads_out[which], sems.at[9 + which])
        gain_outs[which][...] = sum(gain_grads)

    def arrived(*names):
        for name in names:
            come[name].wait()

    if cross:
        arrived(3, "w0", 1, 2)
        shares(0, (0,), target_v, gains[query_gain : query_gain + 1, :], up_v)
        arrived(4, "w1", 5, "w2", 0)
        shares(1, (1, 2), source_v, gains[key_gain : key_gain + 1, :], None)
    else:
        arrived(2, "w0", 3, "w1", 4, "w2", 0, 1)
        shares(0, (0, 1, 2), target_v, gains[key_gain : key_gain + 1, :], up_v)
    for which in range(outs):
        pltpu.make_async_copy(result.at[which], grads_out[which], sems.at[9 + which]).wait()


def project_grad(gains, source, target, upstream, score_grads, whole):
    cross = source is not None
    rows, width = target.shape
    outs = 2 if cross else 1
    head = (gains, source, target) if cross else (gains, target)
    result = pl.pallas_call(
        functools.partial(project_grad_kernel, cross),
        out_shape=[jax.ShapeDtypeStruct((rows, width), F32)] * outs + [jax.ShapeDtypeStruct((1, width), F32)] * outs,
        in_specs=[VMEM] + [ANY] * (len(head) + 4),
        out_specs=[ANY] * outs + [VMEM] * outs,
        scratch_shapes=[
            pltpu.VMEM((rows, width), target.dtype),
            pltpu.VMEM((rows if cross else 8, width), LOW),
            pltpu.VMEM((rows, width), F32),
            pltpu.VMEM((3, rows, width), LOW),
            pltpu.VMEM((3, *whole.shape[1:]), LOW),
            pltpu.VMEM((outs, rows, width), F32),
            pltpu.SemaphoreType.DMA((11,)),
        ],
        compiler_params=pltpu.CompilerParams(vmem_limit_bytes=48 * MIB),
        cost_estimate=pl.CostEstimate(
            flops=6 * rows * width * width, bytes_accessed=20 * rows * width + 6 * width * width, transcendentals=rows
        ),
    )(*head, upstream, *score_grads, whole)
    return result[:outs], result[outs:]


def mlp_forward_kernel(call, depth, second, cotangent, *refs):
    if call == 0:
        gain_row, bands, normal_out, sum_out, hidden_out, *refs = refs
    else:
        normal_in, skip, bands, sum_out, hidden_out, *refs = refs
    *outs, second_v, cot_v, extra_v, normal, cot_t, active, hidden_grad, result, lower_v, lift_v, grad_v, sems, send_sems = refs
    parts, rows, size = lower_v.shape[0], lower_v.shape[2], lower_v.shape[3]
    count, units = lift_v.shape[:2]
    steps = range(0, parts * size, BLOCK)
    share = BLOCK // units

    def bring_lift(step):
        here = pl.ds(step * share, share)
        there = bands.at[pl.ds(call * count + step * share, share), pl.ds(PARTS * rows, units)]
        return bring(there, lift_v.at[here], sems.at[4 + step])

    def bring_lower(c):
        return bring(bands.at[:, pl.ds((call * parts + c) * rows, rows)], lower_v.at[c], sems.at[8 + c])

    if call == 0:
        come = [bring(second, second_v, sems.at[0])]
    else:
        come = [bring(normal_in, normal, sems.at[0])]
    lifts = [bring_lift(0)]
    come.append(bring(cotangent, cot_v, sems.at[1]))
    lowers = [bring_lower(0)]
    lifts += [bring_lift(step) for step in range(1, len(steps))]
    lowers += [bring_lower(c) for c in range(1, parts)]
    if call == 1:
        come += [bring(second, second_v, sems.at[2]), bring(skip, extra_v, sems.at[3])]
    leave = []
    come[0].wait()
    if call == 0:
        normalise(second_v, gain_row[...], normal)
        leave.append(bring(normal, normal_out, sems.at[2]))
    for step, start in enumerate(steps):
        lifts[step].wait()
        hidden = dot_nt(normal[...], lift_v[step * share : (step + 1) * share].reshape(BLOCK, -1))
        if step == 0:
            come[1].wait()
        if start % size == 0:
            lowers[start // size].wait()
        columns = slice(start % size, start % size + BLOCK)
        upstream = dot_nn(cot_v[...], lower_v[start // size, :, :, columns].reshape(-1, BLOCK))
        for at in range(0, hidden.shape[0], ROWS):
            few = slice(at, at + ROWS)
            value = hidden[few]
            square = value * value
            root = 0.7978845608028654
            tanh = jnp.tanh(value * (root + (root * 0.044715) * square))
            half = 0.5 + 0.5 * tanh
            rise = (0.5 * value) * (1.0 - tanh * tanh) * (root + (3 * root * 0.044715) * square)
            active[few, start : start + BLOCK] = (value * half).astype(LOW)
            hidden_grad[few, start : start + BLOCK] = (upstream[few] * (half + rise)).astype(LOW)
        here = slice(start, start + BLOCK)
        bring(hidden_grad.at[:, here], hidden_out.at[:, here], sems.at[10])
        if step == 0:
            cot_t[...] = cot_v[...].T
        if (start + BLOCK) % size == 0:
            c = start // size
            columns = slice(c * size, (c + 1) * size)
            grad_v[:, columns] = dot_nn(cot_t[...], active[:, columns]).astype(LOW)
            if depth is None:
                bring(grad_v.at[:, columns], outs[0].at[:, columns], send_sems.at[0])
            else:
                src_of = lambda owner: grad_v.at[pl.ds(pl.multiple_of(owner * rows, rows), rows), columns]
                cut_blocks([(c, src_of, None)], outs, depth, send_sems)
    for copy in come[2:]:
        copy.wait()

    def work(at, length):
        few = slice(at, at + length)
        total = second_v[few, :]
        for c in range(parts):
            total = total + dot_nt(active[few, c * size : (c + 1) * size], matrix(lower_v.at[c]))
        result[few, :] = total if call == 0 else (total + extra_v[few, :].astype(F32)).astype(LOW)

    in_shares(result.shape[0], work, result, sum_out, sems.at[11])
    for copy in leave:
        copy.wait()
    pltpu.make_async_copy(result, sum_out, sems.at[11]).wait()
    pltpu.make_async_copy(hidden_grad, hidden_out, sems.at[10]).wait()
    await_whole(outs, send_sems)


def mlp_forward(call, second, cotangent, others, bands, hidden, depth):
    rows, width = second.shape
    units, parts = hidden // CALLS, PARTS // CALLS
    low = jax.ShapeDtypeStruct((rows, width), LOW)
    if depth is None:
        outs = [jax.ShapeDtypeStruct((width, units), LOW)]
    else:
        outs = blocks_of((width // 32, units // 2))
    return pl.pallas_call(
        functools.partial(mlp_forward_kernel, call, depth),
        out_shape=[low]
        + [jax.ShapeDtypeStruct((rows, width), F32)] * (call == 0)
        + [jax.ShapeDtypeStruct((rows, units), LOW)]
        + outs,
        in_specs=[ANY] * 2 + ([VMEM] if call == 0 else [ANY] * 2) + [ANY],
        out_specs=[ANY] * (3 if call == 0 else 2) + [ANY] * len(outs),
        scratch_shapes=[
            pltpu.VMEM((rows, width), F32),
            pltpu.VMEM((rows, width), LOW),
            pltpu.VMEM((8 if call == 0 else rows, width), LOW),
            pltpu.VMEM((rows, width), LOW),
            pltpu.VMEM((width, rows), LOW),
            pltpu.VMEM((rows, units), LOW),
            pltpu.VMEM((rows, units), LOW),
            pltpu.VMEM((rows, width), F32 if call == 0 else LOW),
            pltpu.VMEM((parts, 32, width // 32, units // parts), LOW),
            pltpu.VMEM((32 // CALLS, hidden // 32, width), LOW),
            pltpu.VMEM((width, units), LOW),
            pltpu.SemaphoreType.DMA((12,)),
            pltpu.SemaphoreType.DMA((len(outs),)),
        ],
        compiler_params=pltpu.CompilerParams(vmem_limit_bytes=56 * MIB),
        cost_estimate=pl.CostEstimate(
            flops=8 * rows * width * units,
            bytes_accessed=6 * width * units + 12 * rows * width + 2 * rows * units,
            transcendentals=rows * units,
        ),
    )(second, cotangent, *others, bands)


def mlp_backward_kernel(depth, gain_row, second, cotangent, normal, hidden_grad0, hidden_grad1, bands, *refs):
    second_grad, gain_grad, *refs = refs
    *outs, second_v, cot_v, normal_v, hidden_grads, normal_t, result, lift_v, grad_v, sems, send_sems = refs
    units = lift_v.shape[1]
    share, half = BLOCK // units, lift_v.shape[0] // 2
    come = [bring(normal, normal_v, sems.at[0])]
    come += [bring(src, hidden_grads.at[h], sems.at[1 + h]) for h, src in enumerate((hidden_grad0, hidden_grad1))]
    come.append(bring(bands.at[:, pl.ds(bands.shape[1] - units, units)], lift_v, sems.at[3]))
    come += [bring(second, second_v, sems.at[4]), bring(cotangent, cot_v, sems.at[5])]
    come[0].wait()
    normal_t[...] = normal_v[...].T
    steps = grad_v.shape[0] // 2
    for h in range(2):
        come[1 + h].wait()

        def one_block(at, carry):
            columns = pl.ds(pl.multiple_of(at * BLOCK, BLOCK), BLOCK)
            step = h * steps + at
            grad_v[step] = dot_nn(normal_t[...], hidden_grads[h, :, columns]).astype(LOW)
            if depth is None:
                columns = pl.ds(pl.multiple_of(step * BLOCK, BLOCK), BLOCK)
                pltpu.make_async_copy(grad_v.at[step], outs[0].at[:, columns], send_sems.at[0]).start()
                return carry
            size = grad_v.shape[1] // 2
            for c in range(share):
                mask = (step * share + c) ^ device_index()
                group = mask // (2 * depth)
                place = z_place(mask, None, depth, False)
                for away in range(2):

                    @pl.when((mask // depth) % 2 == away)
                    def send():
                        for part in range(2):
                            to = group if part == 0 else group // 2 + group % 2 * 2
                            pltpu.make_async_copy(
                                grad_v.at[step, part * size : (part + 1) * size, c * units : (c + 1) * units],
                                outs[away].at[part, to * depth + place],
                                send_sems.at[away],
                            ).start()

            return carry

        lax.fori_loop(0, steps, one_block, 0)
    for copy in come[3:]:
        copy.wait()
    gain_grads = []

    def work(at, count):
        few = slice(at, at + count)
        back = sum(
            dot_nn(hidden_grads[h, few, :], lift_v[h * half : (h + 1) * half].reshape(half * units, -1)) for h in range(2)
        )
        gain_grads.append(norm_grad(second_v, gain_row[...], back, cot_v, result, at))

    in_shares(result.shape[0], work, result, second_grad, sems.at[6])
    gain_grad[...] = sum(gain_grads)
    pltpu.make_async_copy(result, second_grad, sems.at[6]).wait()
    await_whole(outs, send_sems)


def mlp_backward(gain_row, second, cotangent, normal, hidden_grads, bands, hidden, depth):
    rows, width = second.shape
    if depth is None:
        outs = [jax.ShapeDtypeStruct((width, hidden), LOW)]
    else:
        outs = blocks_of((width // 2, hidden // 32))
    return pl.pallas_call(
        functools.partial(mlp_backward_kernel, depth),
        out_shape=[jax.ShapeDtypeStruct((rows, width), F32), jax.ShapeDtypeStruct((1, width), F32)] + outs,
        in_specs=[VMEM] + [ANY] * 6,
        out_specs=[ANY, VMEM] + [ANY] * len(outs),
        scratch_shapes=[
            pltpu.VMEM((rows, width), F32),
            pltpu.VMEM((rows, width), LOW),
            pltpu.VMEM((rows, width), LOW),
            pltpu.VMEM((2, rows, hidden // 2), LOW),
            pltpu.VMEM((width, rows), LOW),
            pltpu.VMEM((rows, width), F32),
            pltpu.VMEM((32, hidden // 32, width), LOW),
            pltpu.VMEM((hidden // BLOCK, width, BLOCK), LOW),
            pltpu.SemaphoreType.DMA((7,)),
            pltpu.SemaphoreType.DMA((len(outs),)),
        ],
        compiler_params=pltpu.CompilerParams(vmem_limit_bytes=56 * MIB),
        cost_estimate=pl.CostEstimate(
            flops=4 * rows * width * hidden,
            bytes_accessed=4 * width * hidden + 12 * rows * width + 2 * rows * hidden,
            transcendentals=0,
        ),
    )(gain_row, second, cotangent, normal, *hidden_grads, bands)


def local(
    pixels,
    latents,
    skip,
    counts,
    cotangent,
    attn_in,
    attn_out,
    w_in,
    w_out,
    gains,
    attn_in_first,
    attn_in_second,
    attn_out_first,
    attn_out_second,
    w_in_first,
    w_in_second,
    w_out_first,
    w_out_second,
    gains_first,
    gains_second,
):
    groups, depth = lax.axis_size("grp"), lax.axis_size("hd")
    total, core = groups * depth, log2(depth)
    fast = total == 32 and depth == 4
    images, size, width = latents.shape
    hidden = w_out.shape[0]
    flat = lambda rows: rows.reshape(-1, width)
    whole = lambda rows: rows.reshape(images, -1, width)
    pixel_rows, latent_rows, cot_rows = flat(pixels), flat(latents), flat(cotangent)
    attn_in_t, attn_out_t, w_out_t = jnp.swapaxes(attn_in, 1, 2), jnp.swapaxes(attn_out, 1, 2), w_out.T
    own_counts = lax.dynamic_slice_in_dim(counts, lax.axis_index("hd") * images, images)
    cut = depth if fast else None

    def cross_forward(pieces, spreads):
        return attend_block(gain_rows, pixel_rows, latent_rows, own_counts, pieces, spreads, images)

    def self_forward(pieces, spreads):
        return attend_block(gain_rows, None, first_sum, None, pieces, spreads, images)

    if fast:
        (x_bit,), (y_bit,) = outer_bits(groups, depth)
        *shards, mlp_shard = pack(attn_in_t, attn_out_t, w_out_t, w_in)
        orders = ((1, 0, x_bit, y_bit), (1, 0, y_bit, x_bit), (x_bit, y_bit, 1, 0), (y_bit, x_bit, 1, 0))
        spreads = [spread_of(order, core, total) for order in orders]
        chains = [Chain(gather_steps(shard, order, core, total)) for shard, order in zip(shards, orders)]
        in_round(chains)
        mlp_shard = in_round(chains, None, mlp_shard)
        bands = lax.all_gather(mlp_shard, AXES, axis=0)
        gain_rows = in_round(chains, lambda: gather_gains(gains))
        while any(chain.wanted for chain in chains):
            in_round(chains)
        *saved, first_sum, logs, weights = cross_forward(chains[0].result + chains[2].result, spreads[::2])
        *saved2, second_sum, logs2, weights2 = self_forward(chains[1].result + chains[3].result, spreads[1::2])
    else:
        every = lambda shard: lax.all_gather(shard.astype(LOW), AXES, axis=0, tiled=True).reshape(32, -1, shard.shape[1])
        inward = lambda m: jnp.concatenate([every(attn_in_t[3 * m + k]) for k in range(3)], axis=1)
        gain_rows = gather_gains(gains)
        lower = every(w_out_t)
        lift = lax.all_gather(w_in.astype(LOW), AXES, axis=1, tiled=True).T.reshape(32, -1, width)
        bands = jnp.concatenate([*jnp.split(lower, PARTS, axis=2), lift], axis=1)
        *saved, first_sum, logs, weights = cross_forward([inward(0), every(attn_out_t[0])], (None, None))
        *saved2, second_sum, logs2, weights2 = self_forward([inward(1), every(attn_out_t[1])], (None, None))

    normal, partial, hidden_grad0, *lower_grad0 = mlp_forward(
        0, second_sum, cot_rows, (gain_rows[3:],), bands, hidden, cut
    )

    def mlp_second():
        return mlp_forward(1, partial, cot_rows, (normal, flat(skip)), bands, hidden, cut)

    def mlp_back():
        return mlp_backward(
            gain_rows[3:], second_sum, cot_rows, normal, (hidden_grad0, hidden_grad1), bands, hidden, cut
        )

    def self_scores():
        return scores_grad(None, second_grad, (*saved2, logs2), weights2, images)

    def self_matrices():
        return matrix_grads(gain_rows, None, first_sum, second_grad, saved2[3], score_grads2, cut)

    def self_project():
        return project_grad(gain_rows, None, first_sum, second_grad, score_grads2, weights2)

    def cross_scores():
        return scores_grad(own_counts, first_grad, (*saved, logs), weights, images)

    def cross_matrices():
        return matrix_grads(gain_rows, pixel_rows, latent_rows, first_grad, saved[3], score_grads, cut)

    def cross_project():
        return project_grad(gain_rows, pixel_rows, latent_rows, first_grad, score_grads, weights)

    if fast:
        scatter = lambda blocks, last=False: Chain(scatter_steps(*blocks, x_bit, y_bit, core, total, last))
        live = [scatter(lower_grad0)]
        latents_out, hidden_grad1, *lower_grad1 = in_round(live, mlp_second)
        live.append(scatter(lower_grad1))
        second_grad, gain3_grad, *lift_grad = in_round(live, mlp_back)
        live.append(scatter(lift_grad))
        score_grads2 = in_round(live, self_scores)
        live.append(scatter(in_round(live, self_matrices, longer=live[2:])))
        (first_grad,), (gain2_grad,) = in_round(live, self_project)
        score_grads = in_round(live, cross_scores, longer=live[3:])
        live.append(scatter(in_round(live, cross_matrices), True))
        in_round(live)
        (latents_grad, pixels_grad), (gain1_grad, gain0_grad) = in_round(live, cross_project)
        gains_grad = jnp.concatenate([gain0_grad, gain1_grad, gain2_grad, gain3_grad], axis=0)
        gains_sum = scatter_gains(gains_grad)
        while any(chain.wanted for chain in live):
            in_round(live)
        lower0, lower1, lift_sum, own, cross = [chain.result for chain in live]
        lower_sum = jnp.concatenate([*lower0, *lower1], axis=1)
        lift_sum = jnp.concatenate([*lift_sum], axis=0)
        sums, sums2 = [matrix_blocks(block, 4, attn_in.shape[2]) for block in (cross, own)]
    else:
        latents_out, hidden_grad1, lower_grad1 = mlp_second()
        second_grad, gain3_grad, lift_grad = mlp_back()
        score_grads2 = self_scores()
        grads2 = self_matrices()
        (first_grad,), (gain2_grad,) = self_project()
        score_grads = cross_scores()
        grads = cross_matrices()
        (latents_grad, pixels_grad), (gain1_grad, gain0_grad) = cross_project()
        gains_grad = jnp.concatenate([gain0_grad, gain1_grad, gain2_grad, gain3_grad], axis=0)
        gains_sum = scatter_gains(gains_grad)
        sum_of = lambda grad, along: lax.psum_scatter(grad, AXES, scatter_dimension=along, tiled=True)
        sums = [sum_of(g, 0) for g in grads]
        sums2 = [sum_of(g, 0) for g in grads2]
        lift_sum = sum_of(lift_grad, 1)
        lower_sum = sum_of(jnp.concatenate([*lower_grad0, lower_grad1], axis=1), 0)
    mixing_sum = jnp.swapaxes(jnp.stack([*sums[:3], *sums2[:3]]), 1, 2).astype(F32)
    outward_sum = jnp.swapaxes(jnp.stack([sums[3], sums2[3]]), 1, 2).astype(F32)
    mix = adamw(attn_in, mixing_sum, attn_in_first, attn_in_second, 0.05, 0.1)
    out = adamw(attn_out, outward_sum, attn_out_first, attn_out_second, 0.3, 0.1)
    lift_new = adamw(w_in, lift_sum.astype(F32), w_in_first, w_in_second, 0.05, 0.1)
    lower_new = adamw(w_out, lower_sum.T.astype(F32), w_out_first, w_out_second, 0.03, 0.1)
    gain_first, gain_second, gain_new = adamw(
        gains, gains_sum, gains_first, gains_second, 0.4, 0.0
    )
    return (
        whole(latents_out),
        whole(pixels_grad),
        whole(latents_grad),
        *mix,
        *out,
        *lift_new,
        *lower_new,
        gain_first,
        gain_second[:3],
        gain_second[3],
        gain_new,
    )


def solution(mesh):
    return jax.shard_map(
        local,
        mesh=mesh,
        in_specs=(
            P(("grp", "hd"), None, None),
            P(("grp", "hd"), None, None),
            P(("grp", "hd"), None, None),
            P("grp"),
            P(("grp", "hd"), None, None),
            P(None, None, ("grp", "hd")),
            P(None, None, ("grp", "hd")),
            P(None, ("grp", "hd")),
            P(None, ("grp", "hd")),
            P(None, ("grp", "hd")),
            P(None, None, ("grp", "hd")),
            P(None, None, ("grp", "hd")),
            P(None, None, ("grp", "hd")),
            P(None, None, ("grp", "hd")),
            P(None, ("grp", "hd")),
            P(None, ("grp", "hd")),
            P(None, ("grp", "hd")),
            P(None, ("grp", "hd")),
            P(None, ("grp", "hd")),
            P(None, ("grp", "hd")),
        ),
        out_specs=(
            P(("grp", "hd"), None, None),
            P(("grp", "hd"), None, None),
            P(("grp", "hd"), None, None),
            P(None, None, ("grp", "hd")),
            P(None, None, ("grp", "hd")),
            P(None, None, ("grp", "hd")),
            P(None, None, ("grp", "hd")),
            P(None, None, ("grp", "hd")),
            P(None, None, ("grp", "hd")),
            P(None, ("grp", "hd")),
            P(None, ("grp", "hd")),
            P(None, ("grp", "hd")),
            P(None, ("grp", "hd")),
            P(None, ("grp", "hd")),
            P(None, ("grp", "hd")),
            P(None, ("grp", "hd")),
            P(None, ("grp", "hd")),
            P(("grp", "hd")),
            P(None, ("grp", "hd")),
        ),
        check_vma=False,
    )
```

```python
import functools

import jax
import jax.numpy as jnp
from jax import lax
from jax.experimental import pallas as pl
from jax.experimental.pallas import tpu as pltpu
from jax.sharding import PartitionSpec as P

NH = 8
STEP = 5
AXES = ("grp", "hd")

MIB = 1 << 20
F32, LOW = jnp.float32, jnp.bfloat16
VMEM = pl.BlockSpec(memory_space=pltpu.VMEM)
SMEM = pl.BlockSpec(memory_space=pltpu.SMEM)


ANY = pl.BlockSpec(memory_space=pl.ANY)


def adamw(weight, grad, first_old, second_old, learn_rate, decay):
    first_new = 0.5 * first_old + 0.5 * grad
    second_new = 0.5 * second_old + 0.5 * grad * grad
    correction = 1.0 - 0.5**STEP
    normed_step = first_new / correction / (jnp.sqrt(second_new / correction) + 1e-08)
    return (first_new, second_new, weight - learn_rate * (normed_step + decay * weight))


def log2(n):
    return n.bit_length() - 1


def outer_bits(groups, depth):
    first, last = log2(depth) + 1, log2(depth) + log2(groups)
    middle = (first + last) // 2
    return list(range(first, middle)), list(range(middle, last))


def swap(block, bit, total):
    return lax.ppermute(block, AXES, [(j, j ^ (1 << bit)) for j in range(total)])


def spread_of(order, core, total):
    bits = list(order) + [core]
    return tuple(sum(((p >> t) & 1) << b for t, b in enumerate(bits)) for p in range(total))


def added(a, b):
    return (a.astype(F32) + b.astype(F32)).astype(LOW)


def device_index():
    return lax.axis_index("grp") * lax.axis_size("hd") + lax.axis_index("hd")


def gather_steps(shard, order, core, total):
    held = shard
    for bit in order[:-1]:
        (came,) = yield [functools.partial(swap, held, bit, total)]
        held = jnp.concatenate([held, came], axis=0)
    (came,) = yield [functools.partial(swap, held, order[-1], total)]
    first, second = yield [functools.partial(swap, held, core, total), functools.partial(swap, came, core, total)]
    return [held, came, first, second]


def gather_gains_steps(gains, x_bit, y_bit, core, total):
    rows = gains.shape[0]
    held = gains.astype(LOW).reshape(1, -1)
    outer = (x_bit, y_bit)
    masks = [1 << x_bit, 1 << y_bit, (1 << x_bit) | (1 << y_bit)]
    exchange = lambda mask: functools.partial(lax.ppermute, held, AXES, [(j, j ^ mask) for j in range(total)])
    came = yield [exchange(mask) for mask in masks]
    held = jnp.concatenate([held, *came], axis=0)
    for bit in (1, 0, core):
        (came,) = yield [functools.partial(swap, held, bit, total)]
        held = jnp.concatenate([held, came], axis=0)
    owners = jnp.array(spread_of((*outer, 1, 0), core, total), jnp.int32) ^ device_index()
    place = lax.broadcasted_iota(jnp.int32, (total, total), 0) == owners[None, :]
    every = jnp.dot(place.astype(LOW), held, preferred_element_type=F32)
    return jnp.swapaxes(every.reshape(total, rows, -1), 0, 1).reshape(rows, -1)


def scatter_steps(mine, theirs, x_bit, y_bit, core, total, last=False):
    (came,) = yield [functools.partial(swap, theirs, core, total)]
    half = mine.shape[1] // 2
    away = [added(mine[k, half:], came[k, half:]) for k in range(2)]
    held = [added(mine[k, :half], came[k, :half]) for k in range(2)]
    came = yield [functools.partial(swap, block, bit, total) for block, bit in zip(away, (y_bit, x_bit))]
    half //= 2
    away = [added(held[k][half:], came[k][half:]) for k in range(2)]
    held = [added(held[k][:half], came[k][:half]) for k in range(2)]
    came = yield [functools.partial(swap, block, bit, total) for block, bit in zip(away, (x_bit, y_bit))]
    both = jnp.stack([added(held[k], came[k]) for k in range(2)], axis=1)
    if last:
        (came,) = yield [functools.partial(lax.all_to_all, both, "hd", 0, 0, tiled=True)]
        return jnp.sum(came.astype(F32), axis=0)
    for bit in range(core):
        half = both.shape[0] // 2
        (came,) = yield [functools.partial(swap, both[half:], bit, total)]
        both = added(both[:half], came)
    return both[0].astype(F32)


class Chain:
    def __init__(self, steps):
        self.steps, self.result, self.under_way = steps, None, None
        self.wanted = next(steps)

    def start(self):
        if self.under_way is None:
            self.under_way = [exchange() for exchange in self.wanted]

    def advance(self, came):
        self.under_way = None
        try:
            self.wanted = self.steps.send(came)
        except StopIteration as stop:
            self.wanted, self.result = [], stop.value


def in_round(chains, compute=None, *, beside=None, longer=()):
    chains = [chain for chain in chains if chain.wanted]
    for chain in chains:
        chain.start()
    ending = [chain for chain in chains if chain not in longer]
    done = compute() if compute else ()
    came, done, beside = lax.optimization_barrier(([chain.under_way for chain in ending], done, beside))
    for chain, blocks in zip(ending, came):
        chain.advance(blocks)
    return done if beside is None else (done, beside)


def place_blocks(refs, spread, dst, rows, sem):
    if spread is None:
        pltpu.make_async_copy(refs[0].at[:, rows], dst, sem).start()
        return
    me, each = device_index(), len(spread) // 4
    for p, mask in enumerate(spread):
        pltpu.make_async_copy(refs[p // each].at[p % each, rows], dst.at[me ^ mask], sem).start()


def z_place(mask, owner, depth, last):
    if last:
        return owner & (depth - 1)
    return sum(((mask >> bit) & 1) << (log2(depth) - 1 - bit) for bit in range(log2(depth)))


def cut_blocks(halves, refs, depth, sems, last=False):
    me = device_index()
    for mask in range(32):
        owner = me ^ mask
        place = mask // (2 * depth)
        for half, src_of, rows in halves:
            group = place if half == 0 else place // 2 + place % 2 * 2
            dst = refs[mask // depth % 2].at[half, group * depth + z_place(mask, owner, depth, last)]
            dst = dst if rows is None else dst.at[rows]
            pltpu.make_async_copy(src_of(owner), dst, sems.at[mask // depth % 2]).start()


def bring(src, dst, sem):
    copy = pltpu.make_async_copy(src, dst, sem)
    copy.start()
    return copy


def await_whole(refs, sems):
    for at, ref in enumerate(refs):
        pltpu.make_async_copy(ref, ref, sems.at[at]).wait()


def blocks_of(shape):
    return [jax.ShapeDtypeStruct((2, 16, *shape), LOW)] * 2


BLOCK = 512
PARTS = 4
CALLS = 2


def pack_kernel(attn_in_ref, attn_out_ref, w_out_ref, w_in_ref, *refs):
    cross, own, cross_out, own_out, mlp, attn_in, attn_out, w_out, w_in, sems = refs
    sources, places = (attn_in_ref, attn_out_ref, w_in_ref, w_out_ref), (attn_in, attn_out, w_in, w_out)
    for copy in [bring(src, dst, sems.at[at]) for at, (src, dst) in enumerate(zip(sources, places))]:
        copy.wait()
    rows = attn_in.shape[1]
    for at, (to, to_out) in enumerate(((cross, cross_out), (own, own_out))):
        for m in range(3):
            to[0, m * rows : (m + 1) * rows, :] = attn_in[3 * at + m].astype(LOW)
        to_out[0] = attn_out[at].astype(LOW)
    width = w_out.shape[1] // PARTS
    for c in range(PARTS):
        mlp[c * rows : (c + 1) * rows, :] = w_out[:, c * width : (c + 1) * width].astype(LOW)
    mlp[PARTS * rows :, :] = w_in[...].T.astype(LOW)


def pack(attn_in_t, attn_out_t, w_out_t, w_in):
    rows, width = attn_in_t.shape[1:]
    return pl.pallas_call(
        pack_kernel,
        out_shape=[jax.ShapeDtypeStruct((1, 3 * rows, width), LOW)] * 2
        + [jax.ShapeDtypeStruct((1, rows, width), LOW)] * 2
        + [jax.ShapeDtypeStruct((PARTS * rows + w_in.shape[1], width), LOW)],
        in_specs=[ANY] * 4,
        out_specs=[VMEM] * 5,
        scratch_shapes=[pltpu.VMEM(a.shape, F32) for a in (attn_in_t, attn_out_t, w_out_t, w_in)]
        + [pltpu.SemaphoreType.DMA((4,))],
        compiler_params=pltpu.CompilerParams(vmem_limit_bytes=16 * MIB),
    )(attn_in_t, attn_out_t, w_out_t, w_in)


def from_all(own):
    total = lax.axis_size("grp") * lax.axis_size("hd")
    return lax.all_to_all(jnp.broadcast_to(own[None], (total, *own.shape)), AXES, 0, 0, tiled=True)


def gather_gains(gains):
    rows = gains.shape[0]
    every = from_all(gains.astype(LOW).reshape(-1)).astype(F32)
    return jnp.swapaxes(every.reshape(every.shape[0], rows, -1), 0, 1).reshape(rows, -1)


def scatter_gains(grads):
    total = lax.axis_size("grp") * lax.axis_size("hd")
    rows = grads.shape[0]
    blocks = jnp.swapaxes(grads.reshape(rows, total, -1), 0, 1).reshape(total, -1)
    came = lax.all_to_all(blocks, AXES, 0, 0, tiled=True)
    return jnp.sum(came, axis=0).reshape(rows, -1)


def dot_nn(a, b):
    return lax.dot_general(a, b, (((1,), (0,)), ((), ())), preferred_element_type=F32)


def dot_nt(a, b):
    return lax.dot_general(a, b, (((1,), (1,)), ((), ())), preferred_element_type=F32)


def dot_tn(a, b):
    return lax.dot_general(a, b, (((0,), (0,)), ((), ())), preferred_element_type=F32)


ROWS = 32


def unit_rows(rows):
    inverse = lax.rsqrt(jnp.mean(rows * rows, axis=-1, keepdims=True) + 1e-06)
    return rows * inverse, inverse


def normalise(source, gain, out):
    for at in range(0, source.shape[0], ROWS):
        span = slice(at, at + ROWS)
        out[span, :] = (unit_rows(source[span, :].astype(F32))[0] * gain).astype(LOW)


def norm_grad(source, gain, upstream, base, out, first=0):
    gain_grad = 0.0
    for at in range(0, upstream.shape[0], ROWS):
        span = slice(first + at, first + at + ROWS)
        unit, inverse = unit_rows(source[span, :].astype(F32))
        grad = upstream[at : at + ROWS]
        scaled = grad * gain
        inner = jnp.mean(scaled * unit, axis=-1, keepdims=True)
        extra = (scaled - unit * inner) * inverse
        out[span, :] = extra if base is None else base[span, :].astype(F32) + extra
        gain_grad += jnp.sum((grad * unit).reshape(ROWS // 8, 8, -1), axis=0)
    return jnp.sum(gain_grad, axis=0, keepdims=True)


SHARES = 2


def in_shares(rows, work, scratch, out, sem):
    count = rows // SHARES
    for at in range(0, rows, count):
        work(at, count)
        bring(scratch.at[at : at + count], out.at[at : at + count], sem)


def head_scores(query, key, count, scale):
    scores = dot_nt(query, key) * scale
    if count is not None:
        place = lax.broadcasted_iota(jnp.int32, scores.shape, 1)
        scores = jnp.where(place < count, scores, -1e30)
    return scores


def matrix(weights):
    return weights[...].reshape(-1, weights.shape[2])


def attend_kernel(cross, images, size, spreads, *refs):
    if cross:
        counts, gains, source, target, *refs = refs
    else:
        gains, target, *refs = refs
    *pieces, q_out, k_out, v_out, context_out, sum_out, log_out, whole, refs = *refs[:-14], *refs[-14:-7], refs[-7:]
    kept, target_v, source_v, weights, normal, total, sems = refs
    q_v, k_v, v_v, context_v = (kept.at[m] for m in range(4))
    rows = weights.shape[2]
    count = len(pieces) // 2
    come = [bring(source, source_v, sems.at[4])] if cross else []
    come.append(bring(target, target_v, sems.at[5]))
    for m in (1, 2, 0):
        place_blocks(pieces[:count], spreads[0], weights.at[m], pl.ds(m * rows, rows), sems.at[m])
    place_blocks(pieces[count:], spreads[1], weights.at[3], slice(None), sems.at[3])

    def arrived(m):
        pltpu.make_async_copy(weights.at[m], weights.at[m], sems.at[m]).wait()
        return matrix(weights.at[m])

    key_gain, query_gain = (0, 1) if cross else (2, 2)
    come[0].wait()
    normalise(source_v if cross else target_v, gains[key_gain : key_gain + 1, :], normal)
    k_v[...] = dot_nt(normal[...], arrived(1)).astype(LOW)
    leave = [bring(k_v, k_out, sems.at[6])]
    v_v[...] = dot_nt(normal[...], arrived(2)).astype(LOW)
    leave.append(bring(v_v, v_out, sems.at[7]))
    if cross:
        come[1].wait()
        normalise(target_v, gains[query_gain : query_gain + 1, :], normal)
    q_v[...] = dot_nt(normal[...], arrived(0)).astype(LOW)
    leave.append(bring(q_v, q_out, sems.at[8]))
    out_weights = arrived(3)
    leave.append(bring(weights, whole, sems.at[9]))
    width = q_v.shape[1] // NH
    scale = width ** (-0.5)

    def one_image(image, carry):
        span = pl.ds(pl.multiple_of(image * size, size), size)
        count = counts[image] if cross else None
        for h in range(NH):
            part = slice(h * width, (h + 1) * width)
            scores = head_scores(q_v[span, part], k_v[span, part], count, scale)
            highest = jnp.max(scores, axis=-1, keepdims=True)
            exponent = jnp.exp(scores - highest)
            row_total = jnp.sum(exponent, axis=-1, keepdims=True)
            probs = (exponent * (1.0 / row_total)).astype(LOW)
            context_v[span, part] = dot_nn(probs, v_v[span, part]).astype(LOW)
            log_out[span, h : h + 1] = highest + jnp.log(row_total)
        return carry

    lax.fori_loop(0, images, one_image, 0)
    leave.append(bring(context_v, context_out, sems.at[10]))

    def work(at, count):
        span = slice(at, at + count)
        total[span, :] = target_v[span, :].astype(F32) + dot_nt(context_v[span, :], out_weights)

    in_shares(total.shape[0], work, total, sum_out, sems.at[11])
    for copy in leave:
        copy.wait()
    pltpu.make_async_copy(total, sum_out, sems.at[11]).wait()


def attend_block(gains, source, target, counts, pieces, spreads, images):
    cross = source is not None
    rows, width = target.shape
    low = jax.ShapeDtypeStruct((rows, width), LOW)
    weights = (4, 32, width // 32, width)
    head = (counts, gains, source, target) if cross else (gains, target)
    return pl.pallas_call(
        functools.partial(attend_kernel, cross, images, rows // images, spreads),
        out_shape=[low] * 4
        + [jax.ShapeDtypeStruct(shape, F32) for shape in ((rows, width), (rows, NH))]
        + [jax.ShapeDtypeStruct(weights, LOW)],
        in_specs=([SMEM] if cross else []) + [VMEM] + [ANY] * (2 if cross else 1) + [ANY] * len(pieces),
        out_specs=[ANY] * 5 + [VMEM, ANY],
        scratch_shapes=[
            pltpu.VMEM((4, rows, width), LOW),
            pltpu.VMEM((rows, width), target.dtype),
            pltpu.VMEM((rows if cross else 8, width), LOW),
            pltpu.VMEM(weights, LOW),
            pltpu.VMEM((rows, width), LOW),
            pltpu.VMEM((rows, width), F32),
            pltpu.SemaphoreType.DMA((12,)),
        ],
        compiler_params=pltpu.CompilerParams(vmem_limit_bytes=48 * MIB),
        cost_estimate=pl.CostEstimate(
            flops=8 * rows * width * width + 4 * rows * width * (rows // images),
            bytes_accessed=12 * rows * width + 8 * width * width,
            transcendentals=rows * NH * (rows // images),
        ),
    )(*head, *pieces)


def scores_grad_kernel(cross, images, size, *refs):
    if cross:
        counts, *refs = refs
    upstream, q_in, k_in, v_in, context_in, log_in, whole, *refs = refs
    grads_out, (up_v, kept, grads, dc, wo_v, sems) = refs[:3], refs[3:]
    come = [bring(upstream, up_v, sems.at[0]), bring(whole.at[3], wo_v, sems.at[1])]
    come += [bring(src, kept.at[m], sems.at[2 + m]) for m, src in enumerate((q_in, k_in, v_in, context_in))]
    q_v, k_v, v_v, context_v = (kept.at[m] for m in range(4))
    dq, dk, dv = (grads.at[m] for m in range(3))
    for copy in come[:2]:
        copy.wait()
    dc[...] = dot_nn(up_v[...].astype(LOW), matrix(wo_v)).astype(LOW)
    for copy in come[2:]:
        copy.wait()
    width = q_v.shape[1] // NH
    scale = width ** (-0.5)

    def one_image(image, carry):
        span = pl.ds(pl.multiple_of(image * size, size), size)
        count = counts[image] if cross else None
        for h in range(NH):
            part = slice(h * width, (h + 1) * width)
            query, key, value, grad = q_v[span, part], k_v[span, part], v_v[span, part], dc[span, part]
            probs = jnp.exp(head_scores(query, key, count, scale) - log_in[span, h : h + 1])
            prob_grad = dot_nt(grad, value)
            dv[span, part] = dot_tn(probs.astype(LOW), grad).astype(LOW)
            inner = jnp.sum(grad.astype(F32) * context_v[span, part].astype(F32), axis=-1, keepdims=True)
            score_grad = (probs * (prob_grad - inner)).astype(LOW)
            dq[span, part] = (dot_nn(score_grad, key) * scale).astype(LOW)
            dk[span, part] = (dot_tn(score_grad, query) * scale).astype(LOW)
        for m, to in enumerate(grads_out):
            pltpu.make_async_copy(grads.at[m, span], to.at[span], sems.at[6 + m]).start()
        return carry

    lax.fori_loop(0, images, one_image, 0)
    await_whole(grads_out, sems.at[pl.ds(6, 3)])


def scores_grad(counts, upstream, saved, whole, images):
    cross = counts is not None
    rows, width = upstream.shape
    return pl.pallas_call(
        functools.partial(scores_grad_kernel, cross, images, rows // images),
        out_shape=[jax.ShapeDtypeStruct((rows, width), LOW)] * 3,
        in_specs=([SMEM] if cross else []) + [ANY] * 5 + [VMEM, ANY],
        out_specs=[ANY] * 3,
        scratch_shapes=[
            pltpu.VMEM((rows, width), F32),
            pltpu.VMEM((4, rows, width), LOW),
            pltpu.VMEM((3, rows, width), LOW),
            pltpu.VMEM((rows, width), LOW),
            pltpu.VMEM(whole.shape[1:], LOW),
            pltpu.SemaphoreType.DMA((9,)),
        ],
        compiler_params=pltpu.CompilerParams(vmem_limit_bytes=48 * MIB),
        cost_estimate=pl.CostEstimate(
            flops=2 * rows * width * width + 10 * rows * width * (rows // images),
            bytes_accessed=18 * rows * width + 4 * width * width,
            transcendentals=rows * NH * (rows // images),
        ),
    )(*([counts] if cross else []), upstream, *saved, whole)


def matrix_shares(count, rows):
    shares = []
    for m in range(count // 2 * 2):
        shares.append((m % 2, m, 0, rows, m // 2 * rows))
    if count % 2:
        for half in range(2):
            shares.append((half, count - 1, half * rows // 2, rows // 2, count // 2 * rows))
    return shares


def matrix_blocks(sums, count, rows):
    parts = [[] for _ in range(count)]
    for half, m, _, length, at in matrix_shares(count, rows):
        parts[m].append(sums[half, at : at + length])
    return [part[0] if len(part) == 1 else jnp.concatenate(part, axis=0) for part in parts]


def matrix_grad_kernel(cross, depth, *refs):
    gains, *refs = refs
    ins, (*outs, target_v, source_v, up_v, kept, grads, normal, sems, send_sems) = refs[: 6 + cross], refs[6 + cross :]
    to = [source_v] * cross + [target_v, up_v] + [kept.at[m] for m in (3, 0, 1, 2)]
    order = (1, 4, 0, 5, 6, 2, 3) if cross else (0, 3, 4, 5, 1, 2)
    come = {at: bring(ins[at], to[at], sems.at[at]) for at in order}
    dq, dk, dv, context = (kept.at[m] for m in range(4))
    key_gain, query_gain = (0, 1) if cross else (2, 2)
    width = target_v.shape[1]

    def finish(m, grad):
        grads[m] = grad.astype(LOW)
        if depth is None:
            bring(grads.at[m], outs[m], send_sems.at[m])
            return
        rows = width // 32

        def part(first, count):
            return lambda owner: grads.at[m, pl.ds(pl.multiple_of(owner * rows + first, count), count), :]

        halves = [
            (half, part(first, count), pl.ds(at, count))
            for half, m_at, first, count, at in matrix_shares(grads.shape[0], rows)
            if m_at == m
        ]
        cut_blocks(halves, outs, depth, send_sems, last=cross)

    come[cross].wait()
    normalise(target_v, gains[query_gain : query_gain + 1, :], normal)
    come[3 + cross].wait()
    finish(0, dot_tn(dq[...], normal[...]))
    if cross:
        come[0].wait()
        normalise(source_v, gains[key_gain : key_gain + 1, :], normal)
    come[4 + cross].wait()
    finish(1, dot_tn(dk[...], normal[...]))
    come[5 + cross].wait()
    finish(2, dot_tn(dv[...], normal[...]))
    come[1 + cross].wait()
    come[2 + cross].wait()
    finish(3, dot_tn(up_v[...].astype(LOW), context[...]))
    await_whole(outs, send_sems)


def matrix_grads(gains, source, target, upstream, context, score_grads, depth):
    cross = source is not None
    rows, width = target.shape
    head = (gains, source, target) if cross else (gains, target)
    count = 4
    if depth is None:
        out_shape = [jax.ShapeDtypeStruct((width, width), LOW)] * count
    else:
        out_shape = blocks_of((count * width // 64, width))
    return pl.pallas_call(
        functools.partial(matrix_grad_kernel, cross, depth),
        out_shape=out_shape,
        in_specs=[VMEM] + [ANY] * (len(head) + 4),
        out_specs=[ANY] * len(out_shape),
        scratch_shapes=[
            pltpu.VMEM((rows, width), target.dtype),
            pltpu.VMEM((rows if cross else 8, width), LOW),
            pltpu.VMEM((rows, width), F32),
            pltpu.VMEM((4, rows, width), LOW),
            pltpu.VMEM((count, width, width), LOW),
            pltpu.VMEM((rows, width), LOW),
            pltpu.SemaphoreType.DMA((7,)),
            pltpu.SemaphoreType.DMA((len(out_shape),)),
        ],
        compiler_params=pltpu.CompilerParams(vmem_limit_bytes=48 * MIB),
        cost_estimate=pl.CostEstimate(
            flops=2 * count * rows * width * width,
            bytes_accessed=16 * rows * width + 2 * count * width * width,
            transcendentals=rows,
        ),
    )(*head, upstream, context, *score_grads)


def project_grad_kernel(cross, *refs):
    gains, *refs = refs
    ins, refs = refs[: 6 + cross], refs[6 + cross :]
    outs = 1 + cross
    grads_out, gain_outs, (target_v, source_v, up_v, kept, weights, result, sems) = refs[:outs], refs[outs : 2 * outs], refs[2 * outs :]
    whole = ins[-1]
    inputs = list(ins[:-1])
    to = [source_v] * cross + [target_v, up_v] + [kept.at[m] for m in range(3)]
    order = (3, 1, 2, 4, 5, 0) if cross else (2, 3, 4, 0, 1)
    come, used = {}, 0
    for at in order:
        come[at] = bring(inputs[at], to[at], sems.at[at])
        if at >= 2 + cross:
            m = at - 2 - cross
            come["w%d" % m] = bring(whole.at[m], weights.at[m], sems.at[6 + m])
    dq, dk, dv = (kept.at[m] for m in range(3))
    key_gain, query_gain = (0, 1) if cross else (2, 2)
    rows = target_v.shape[0]

    def back_through(members, few):
        return sum(dot_nn(kept[m, few, :], matrix(weights.at[m])) for m in members)

    def shares(which, members, source, gain, base):
        gain_grads = []

        def work(at, count):
            back = back_through(members, slice(at, at + count))
            gain_grads.append(norm_grad(source, gain, back, base, result.at[which], at))

        in_shares(rows, work, result.at[which], grads_out[which], sems.at[9 + which])
        gain_outs[which][...] = sum(gain_grads)

    def arrived(*names):
        for name in names:
            come[name].wait()

    if cross:
        arrived(3, "w0", 1, 2)
        shares(0, (0,), target_v, gains[query_gain : query_gain + 1, :], up_v)
        arrived(4, "w1", 5, "w2", 0)
        shares(1, (1, 2), source_v, gains[key_gain : key_gain + 1, :], None)
    else:
        arrived(2, "w0", 3, "w1", 4, "w2", 0, 1)
        shares(0, (0, 1, 2), target_v, gains[key_gain : key_gain + 1, :], up_v)
    for which in range(outs):
        pltpu.make_async_copy(result.at[which], grads_out[which], sems.at[9 + which]).wait()


def project_grad(gains, source, target, upstream, score_grads, whole):
    cross = source is not None
    rows, width = target.shape
    outs = 2 if cross else 1
    head = (gains, source, target) if cross else (gains, target)
    result = pl.pallas_call(
        functools.partial(project_grad_kernel, cross),
        out_shape=[jax.ShapeDtypeStruct((rows, width), F32)] * outs + [jax.ShapeDtypeStruct((1, width), F32)] * outs,
        in_specs=[VMEM] + [ANY] * (len(head) + 4),
        out_specs=[ANY] * outs + [VMEM] * outs,
        scratch_shapes=[
            pltpu.VMEM((rows, width), target.dtype),
            pltpu.VMEM((rows if cross else 8, width), LOW),
            pltpu.VMEM((rows, width), F32),
            pltpu.VMEM((3, rows, width), LOW),
            pltpu.VMEM((3, *whole.shape[1:]), LOW),
            pltpu.VMEM((outs, rows, width), F32),
            pltpu.SemaphoreType.DMA((11,)),
        ],
        compiler_params=pltpu.CompilerParams(vmem_limit_bytes=48 * MIB),
        cost_estimate=pl.CostEstimate(
            flops=6 * rows * width * width, bytes_accessed=20 * rows * width + 6 * width * width, transcendentals=rows
        ),
    )(*head, upstream, *score_grads, whole)
    return result[:outs], result[outs:]


def mlp_forward_kernel(call, depth, second, cotangent, *refs):
    if call == 0:
        gain_row, bands, normal_out, sum_out, hidden_out, *refs = refs
    else:
        normal_in, skip, bands, sum_out, hidden_out, *refs = refs
    *outs, second_v, cot_v, extra_v, normal, cot_t, active, hidden_grad, result, lower_v, lift_v, grad_v, sems, send_sems = refs
    parts, rows, size = lower_v.shape[0], lower_v.shape[2], lower_v.shape[3]
    count, units = lift_v.shape[:2]
    steps = range(0, parts * size, BLOCK)
    share = BLOCK // units

    def bring_lift(step):
        here = pl.ds(step * share, share)
        there = bands.at[pl.ds(call * count + step * share, share), pl.ds(PARTS * rows, units)]
        return bring(there, lift_v.at[here], sems.at[4 + step])

    def bring_lower(c):
        return bring(bands.at[:, pl.ds((call * parts + c) * rows, rows)], lower_v.at[c], sems.at[8 + c])

    if call == 0:
        come = [bring(second, second_v, sems.at[0])]
    else:
        come = [bring(normal_in, normal, sems.at[0])]
    lifts = [bring_lift(0)]
    come.append(bring(cotangent, cot_v, sems.at[1]))
    lowers = [bring_lower(0)]
    lifts += [bring_lift(step) for step in range(1, len(steps))]
    lowers += [bring_lower(c) for c in range(1, parts)]
    if call == 1:
        come += [bring(second, second_v, sems.at[2]), bring(skip, extra_v, sems.at[3])]
    leave = []
    come[0].wait()
    if call == 0:
        normalise(second_v, gain_row[...], normal)
        leave.append(bring(normal, normal_out, sems.at[2]))
    for step, start in enumerate(steps):
        lifts[step].wait()
        hidden = dot_nt(normal[...], lift_v[step * share : (step + 1) * share].reshape(BLOCK, -1))
        if step == 0:
            come[1].wait()
        if start % size == 0:
            lowers[start // size].wait()
        columns = slice(start % size, start % size + BLOCK)
        upstream = dot_nn(cot_v[...], lower_v[start // size, :, :, columns].reshape(-1, BLOCK))
        for at in range(0, hidden.shape[0], ROWS):
            few = slice(at, at + ROWS)
            value = hidden[few]
            square = value * value
            root = 0.7978845608028654
            tanh = jnp.tanh(value * (root + (root * 0.044715) * square))
            half = 0.5 + 0.5 * tanh
            rise = (0.5 * value) * (1.0 - tanh * tanh) * (root + (3 * root * 0.044715) * square)
            active[few, start : start + BLOCK] = (value * half).astype(LOW)
            hidden_grad[few, start : start + BLOCK] = (upstream[few] * (half + rise)).astype(LOW)
        here = slice(start, start + BLOCK)
        bring(hidden_grad.at[:, here], hidden_out.at[:, here], sems.at[10])
        if step == 0:
            cot_t[...] = cot_v[...].T
        if (start + BLOCK) % size == 0:
            c = start // size
            columns = slice(c * size, (c + 1) * size)
            grad_v[:, columns] = dot_nn(cot_t[...], active[:, columns]).astype(LOW)
            if depth is None:
                bring(grad_v.at[:, columns], outs[0].at[:, columns], send_sems.at[0])
            else:
                src_of = lambda owner: grad_v.at[pl.ds(pl.multiple_of(owner * rows, rows), rows), columns]
                cut_blocks([(c, src_of, None)], outs, depth, send_sems)
    for copy in come[2:]:
        copy.wait()

    def work(at, length):
        few = slice(at, at + length)
        total = second_v[few, :]
        for c in range(parts):
            total = total + dot_nt(active[few, c * size : (c + 1) * size], matrix(lower_v.at[c]))
        result[few, :] = total if call == 0 else (total + extra_v[few, :].astype(F32)).astype(LOW)

    in_shares(result.shape[0], work, result, sum_out, sems.at[11])
    for copy in leave:
        copy.wait()
    pltpu.make_async_copy(result, sum_out, sems.at[11]).wait()
    pltpu.make_async_copy(hidden_grad, hidden_out, sems.at[10]).wait()
    await_whole(outs, send_sems)


def mlp_forward(call, second, cotangent, others, bands, hidden, depth):
    rows, width = second.shape
    units, parts = hidden // CALLS, PARTS // CALLS
    low = jax.ShapeDtypeStruct((rows, width), LOW)
    if depth is None:
        outs = [jax.ShapeDtypeStruct((width, units), LOW)]
    else:
        outs = blocks_of((width // 32, units // 2))
    return pl.pallas_call(
        functools.partial(mlp_forward_kernel, call, depth),
        out_shape=[low]
        + [jax.ShapeDtypeStruct((rows, width), F32)] * (call == 0)
        + [jax.ShapeDtypeStruct((rows, units), LOW)]
        + outs,
        in_specs=[ANY] * 2 + ([VMEM] if call == 0 else [ANY] * 2) + [ANY],
        out_specs=[ANY] * (3 if call == 0 else 2) + [ANY] * len(outs),
        scratch_shapes=[
            pltpu.VMEM((rows, width), F32),
            pltpu.VMEM((rows, width), LOW),
            pltpu.VMEM((8 if call == 0 else rows, width), LOW),
            pltpu.VMEM((rows, width), LOW),
            pltpu.VMEM((width, rows), LOW),
            pltpu.VMEM((rows, units), LOW),
            pltpu.VMEM((rows, units), LOW),
            pltpu.VMEM((rows, width), F32 if call == 0 else LOW),
            pltpu.VMEM((parts, 32, width // 32, units // parts), LOW),
            pltpu.VMEM((32 // CALLS, hidden // 32, width), LOW),
            pltpu.VMEM((width, units), LOW),
            pltpu.SemaphoreType.DMA((12,)),
            pltpu.SemaphoreType.DMA((len(outs),)),
        ],
        compiler_params=pltpu.CompilerParams(vmem_limit_bytes=56 * MIB),
        cost_estimate=pl.CostEstimate(
            flops=8 * rows * width * units,
            bytes_accessed=6 * width * units + 12 * rows * width + 2 * rows * units,
            transcendentals=rows * units,
        ),
    )(second, cotangent, *others, bands)


def mlp_backward_kernel(depth, gain_row, second, cotangent, normal, hidden_grad0, hidden_grad1, bands, *refs):
    second_grad, gain_grad, *refs = refs
    *outs, second_v, cot_v, normal_v, hidden_grads, normal_t, result, lift_v, grad_v, sems, send_sems = refs
    units = lift_v.shape[1]
    share, half = BLOCK // units, lift_v.shape[0] // 2
    come = [bring(normal, normal_v, sems.at[0])]
    come += [bring(src, hidden_grads.at[h], sems.at[1 + h]) for h, src in enumerate((hidden_grad0, hidden_grad1))]
    come.append(bring(bands.at[:, pl.ds(bands.shape[1] - units, units)], lift_v, sems.at[3]))
    come += [bring(second, second_v, sems.at[4]), bring(cotangent, cot_v, sems.at[5])]
    come[0].wait()
    normal_t[...] = normal_v[...].T
    steps = grad_v.shape[0] // 2
    for h in range(2):
        come[1 + h].wait()

        def one_block(at, carry):
            columns = pl.ds(pl.multiple_of(at * BLOCK, BLOCK), BLOCK)
            step = h * steps + at
            grad_v[step] = dot_nn(normal_t[...], hidden_grads[h, :, columns]).astype(LOW)
            if depth is None:
                columns = pl.ds(pl.multiple_of(step * BLOCK, BLOCK), BLOCK)
                pltpu.make_async_copy(grad_v.at[step], outs[0].at[:, columns], send_sems.at[0]).start()
                return carry
            size = grad_v.shape[1] // 2
            for c in range(share):
                mask = (step * share + c) ^ device_index()
                group = mask // (2 * depth)
                place = z_place(mask, None, depth, False)
                for away in range(2):

                    @pl.when((mask // depth) % 2 == away)
                    def send():
                        for part in range(2):
                            to = group if part == 0 else group // 2 + group % 2 * 2
                            pltpu.make_async_copy(
                                grad_v.at[step, part * size : (part + 1) * size, c * units : (c + 1) * units],
                                outs[away].at[part, to * depth + place],
                                send_sems.at[away],
                            ).start()

            return carry

        lax.fori_loop(0, steps, one_block, 0)
    for copy in come[3:]:
        copy.wait()
    gain_grads = []

    def work(at, count):
        few = slice(at, at + count)
        back = sum(
            dot_nn(hidden_grads[h, few, :], lift_v[h * half : (h + 1) * half].reshape(half * units, -1)) for h in range(2)
        )
        gain_grads.append(norm_grad(second_v, gain_row[...], back, cot_v, result, at))

    in_shares(result.shape[0], work, result, second_grad, sems.at[6])
    gain_grad[...] = sum(gain_grads)
    pltpu.make_async_copy(result, second_grad, sems.at[6]).wait()
    await_whole(outs, send_sems)


def mlp_backward(gain_row, second, cotangent, normal, hidden_grads, bands, hidden, depth):
    rows, width = second.shape
    if depth is None:
        outs = [jax.ShapeDtypeStruct((width, hidden), LOW)]
    else:
        outs = blocks_of((width // 2, hidden // 32))
    return pl.pallas_call(
        functools.partial(mlp_backward_kernel, depth),
        out_shape=[jax.ShapeDtypeStruct((rows, width), F32), jax.ShapeDtypeStruct((1, width), F32)] + outs,
        in_specs=[VMEM] + [ANY] * 6,
        out_specs=[ANY, VMEM] + [ANY] * len(outs),
        scratch_shapes=[
            pltpu.VMEM((rows, width), F32),
            pltpu.VMEM((rows, width), LOW),
            pltpu.VMEM((rows, width), LOW),
            pltpu.VMEM((2, rows, hidden // 2), LOW),
            pltpu.VMEM((width, rows), LOW),
            pltpu.VMEM((rows, width), F32),
            pltpu.VMEM((32, hidden // 32, width), LOW),
            pltpu.VMEM((hidden // BLOCK, width, BLOCK), LOW),
            pltpu.SemaphoreType.DMA((7,)),
            pltpu.SemaphoreType.DMA((len(outs),)),
        ],
        compiler_params=pltpu.CompilerParams(vmem_limit_bytes=56 * MIB),
        cost_estimate=pl.CostEstimate(
            flops=4 * rows * width * hidden,
            bytes_accessed=4 * width * hidden + 12 * rows * width + 2 * rows * hidden,
            transcendentals=0,
        ),
    )(gain_row, second, cotangent, normal, *hidden_grads, bands)


def local(
    pixels,
    latents,
    skip,
    counts,
    cotangent,
    attn_in,
    attn_out,
    w_in,
    w_out,
    gains,
    attn_in_first,
    attn_in_second,
    attn_out_first,
    attn_out_second,
    w_in_first,
    w_in_second,
    w_out_first,
    w_out_second,
    gains_first,
    gains_second,
):
    groups, depth = lax.axis_size("grp"), lax.axis_size("hd")
    total, core = groups * depth, log2(depth)
    fast = total == 32 and depth == 4
    images, size, width = latents.shape
    hidden = w_out.shape[0]
    flat = lambda rows: rows.reshape(-1, width)
    whole = lambda rows: rows.reshape(images, -1, width)
    pixel_rows, latent_rows, cot_rows = flat(pixels), flat(latents), flat(cotangent)
    attn_in_t, attn_out_t, w_out_t = jnp.swapaxes(attn_in, 1, 2), jnp.swapaxes(attn_out, 1, 2), w_out.T
    own_counts = lax.dynamic_slice_in_dim(counts, lax.axis_index("hd") * images, images)
    cut = depth if fast else None

    def cross_forward(pieces, spreads):
        return attend_block(gain_rows, pixel_rows, latent_rows, own_counts, pieces, spreads, images)

    def self_forward(pieces, spreads):
        return attend_block(gain_rows, None, first_sum, None, pieces, spreads, images)

    if fast:
        (x_bit,), (y_bit,) = outer_bits(groups, depth)
        *shards, mlp_shard = pack(attn_in_t, attn_out_t, w_out_t, w_in)
        orders = ((1, 0, x_bit, y_bit), (1, 0, y_bit, x_bit), (x_bit, y_bit, 1, 0), (y_bit, x_bit, 1, 0))
        spreads = [spread_of(order, core, total) for order in orders]
        chains = [Chain(gather_steps(shard, order, core, total)) for shard, order in zip(shards, orders)]
        small = Chain(gather_gains_steps(gains, x_bit, y_bit, core, total))
        both = [*chains, small]
        in_round(both)
        _, mlp_shard = in_round(both, beside=mlp_shard)
        bands = lax.all_gather(mlp_shard, AXES, axis=0)
        in_round(both)
        in_round(both)
        _, gain_rows = in_round(both, beside=small.result)
        *saved, first_sum, logs, weights = cross_forward(chains[0].result + chains[2].result, spreads[::2])
        *saved2, second_sum, logs2, weights2 = self_forward(chains[1].result + chains[3].result, spreads[1::2])
    else:
        every = lambda shard: lax.all_gather(shard.astype(LOW), AXES, axis=0, tiled=True).reshape(32, -1, shard.shape[1])
        inward = lambda m: jnp.concatenate([every(attn_in_t[3 * m + k]) for k in range(3)], axis=1)
        gain_rows = gather_gains(gains)
        lower = every(w_out_t)
        lift = lax.all_gather(w_in.astype(LOW), AXES, axis=1, tiled=True).T.reshape(32, -1, width)
        bands = jnp.concatenate([*jnp.split(lower, PARTS, axis=2), lift], axis=1)
        *saved, first_sum, logs, weights = cross_forward([inward(0), every(attn_out_t[0])], (None, None))
        *saved2, second_sum, logs2, weights2 = self_forward([inward(1), every(attn_out_t[1])], (None, None))

    normal, partial, hidden_grad0, *lower_grad0 = mlp_forward(
        0, second_sum, cot_rows, (gain_rows[3:],), bands, hidden, cut
    )

    def mlp_second():
        return mlp_forward(1, partial, cot_rows, (normal, flat(skip)), bands, hidden, cut)

    def mlp_back():
        return mlp_backward(
            gain_rows[3:], second_sum, cot_rows, normal, (hidden_grad0, hidden_grad1), bands, hidden, cut
        )

    def self_scores():
        return scores_grad(None, second_grad, (*saved2, logs2), weights2, images)

    def self_matrices():
        return matrix_grads(gain_rows, None, first_sum, second_grad, saved2[3], score_grads2, cut)

    def self_project():
        return project_grad(gain_rows, None, first_sum, second_grad, score_grads2, weights2)

    def cross_scores():
        return scores_grad(own_counts, first_grad, (*saved, logs), weights, images)

    def cross_matrices():
        return matrix_grads(gain_rows, pixel_rows, latent_rows, first_grad, saved[3], score_grads, cut)

    def cross_project():
        return project_grad(gain_rows, pixel_rows, latent_rows, first_grad, score_grads, weights)

    if fast:
        scatter = lambda blocks, last=False: Chain(scatter_steps(*blocks, x_bit, y_bit, core, total, last))
        live = [scatter(lower_grad0)]
        latents_out, hidden_grad1, *lower_grad1 = in_round(live, mlp_second)
        live.append(scatter(lower_grad1))
        second_grad, gain3_grad, *lift_grad = in_round(live, mlp_back)
        live.append(scatter(lift_grad))
        score_grads2 = in_round(live, self_scores)
        live.append(scatter(in_round(live, self_matrices, longer=live[2:])))
        (first_grad,), (gain2_grad,) = in_round(live, self_project)
        score_grads = in_round(live, cross_scores, longer=live[3:])
        blocks, score_grads = in_round(live, cross_matrices, beside=score_grads)
        live.append(scatter(blocks, True))
        (latents_grad, pixels_grad), (gain1_grad, gain0_grad) = in_round(live, cross_project)
        in_round(live, longer=live[4:])
        in_round(live)
        gains_grad = jnp.concatenate([gain0_grad, gain1_grad, gain2_grad, gain3_grad], axis=0)
        gains_sum = scatter_gains(gains_grad)
        while any(chain.wanted for chain in live):
            in_round(live)
        lower0, lower1, lift_sum, own, cross = [chain.result for chain in live]
        lower_sum = jnp.concatenate([*lower0, *lower1], axis=1)
        lift_sum = jnp.concatenate([*lift_sum], axis=0)
        sums, sums2 = [matrix_blocks(block, 4, attn_in.shape[2]) for block in (cross, own)]
    else:
        latents_out, hidden_grad1, lower_grad1 = mlp_second()
        second_grad, gain3_grad, lift_grad = mlp_back()
        score_grads2 = self_scores()
        grads2 = self_matrices()
        (first_grad,), (gain2_grad,) = self_project()
        score_grads = cross_scores()
        grads = cross_matrices()
        (latents_grad, pixels_grad), (gain1_grad, gain0_grad) = cross_project()
        gains_grad = jnp.concatenate([gain0_grad, gain1_grad, gain2_grad, gain3_grad], axis=0)
        gains_sum = scatter_gains(gains_grad)
        sum_of = lambda grad, along: lax.psum_scatter(grad, AXES, scatter_dimension=along, tiled=True)
        sums = [sum_of(g, 0) for g in grads]
        sums2 = [sum_of(g, 0) for g in grads2]
        lift_sum = sum_of(lift_grad, 1)
        lower_sum = sum_of(jnp.concatenate([*lower_grad0, lower_grad1], axis=1), 0)
    mixing_sum = jnp.swapaxes(jnp.stack([*sums[:3], *sums2[:3]]), 1, 2).astype(F32)
    outward_sum = jnp.swapaxes(jnp.stack([sums[3], sums2[3]]), 1, 2).astype(F32)
    mix = adamw(attn_in, mixing_sum, attn_in_first, attn_in_second, 0.05, 0.1)
    out = adamw(attn_out, outward_sum, attn_out_first, attn_out_second, 0.3, 0.1)
    lift_new = adamw(w_in, lift_sum.astype(F32), w_in_first, w_in_second, 0.05, 0.1)
    lower_new = adamw(w_out, lower_sum.T.astype(F32), w_out_first, w_out_second, 0.03, 0.1)
    gain_first, gain_second, gain_new = adamw(
        gains, gains_sum, gains_first, gains_second, 0.4, 0.0
    )
    return (
        whole(latents_out),
        whole(pixels_grad),
        whole(latents_grad),
        *mix,
        *out,
        *lift_new,
        *lower_new,
        gain_first,
        gain_second[:3],
        gain_second[3],
        gain_new,
    )


def solution(mesh):
    return jax.shard_map(
        local,
        mesh=mesh,
        in_specs=(
            P(("grp", "hd"), None, None),
            P(("grp", "hd"), None, None),
            P(("grp", "hd"), None, None),
            P("grp"),
            P(("grp", "hd"), None, None),
            P(None, None, ("grp", "hd")),
            P(None, None, ("grp", "hd")),
            P(None, ("grp", "hd")),
            P(None, ("grp", "hd")),
            P(None, ("grp", "hd")),
            P(None, None, ("grp", "hd")),
            P(None, None, ("grp", "hd")),
            P(None, None, ("grp", "hd")),
            P(None, None, ("grp", "hd")),
            P(None, ("grp", "hd")),
            P(None, ("grp", "hd")),
            P(None, ("grp", "hd")),
            P(None, ("grp", "hd")),
            P(None, ("grp", "hd")),
            P(None, ("grp", "hd")),
        ),
        out_specs=(
            P(("grp", "hd"), None, None),
            P(("grp", "hd"), None, None),
            P(("grp", "hd"), None, None),
            P(None, None, ("grp", "hd")),
            P(None, None, ("grp", "hd")),
            P(None, None, ("grp", "hd")),
            P(None, None, ("grp", "hd")),
            P(None, None, ("grp", "hd")),
            P(None, None, ("grp", "hd")),
            P(None, ("grp", "hd")),
            P(None, ("grp", "hd")),
            P(None, ("grp", "hd")),
            P(None, ("grp", "hd")),
            P(None, ("grp", "hd")),
            P(None, ("grp", "hd")),
            P(None, ("grp", "hd")),
            P(None, ("grp", "hd")),
            P(("grp", "hd")),
            P(None, ("grp", "hd")),
        ),
        check_vma=False,
    )
```

```python
import functools

import jax
import jax.numpy as jnp
from jax import lax
from jax.experimental import pallas as pl
from jax.experimental.pallas import tpu as pltpu
from jax.sharding import PartitionSpec as P

NH = 8
STEP = 5
AXES = ("grp", "hd")

MIB = 1 << 20
F32, LOW = jnp.float32, jnp.bfloat16
VMEM = pl.BlockSpec(memory_space=pltpu.VMEM)
SMEM = pl.BlockSpec(memory_space=pltpu.SMEM)


ANY = pl.BlockSpec(memory_space=pl.ANY)


def adamw(weight, grad, first_old, second_old, learn_rate, decay):
    first_new = 0.5 * first_old + 0.5 * grad
    second_new = 0.5 * second_old + 0.5 * grad * grad
    correction = 1.0 - 0.5**STEP
    normed_step = first_new / correction / (jnp.sqrt(second_new / correction) + 1e-08)
    return (first_new, second_new, weight - learn_rate * (normed_step + decay * weight))


def log2(n):
    return n.bit_length() - 1


def outer_bits(groups, depth):
    first, last = log2(depth) + 1, log2(depth) + log2(groups)
    middle = (first + last) // 2
    return list(range(first, middle)), list(range(middle, last))


def swap(block, bit, total):
    return lax.ppermute(block, AXES, [(j, j ^ (1 << bit)) for j in range(total)])


def spread_of(order, core, total):
    bits = list(order) + [core]
    return tuple(sum(((p >> t) & 1) << b for t, b in enumerate(bits)) for p in range(total))


def added(a, b):
    return (a.astype(F32) + b.astype(F32)).astype(LOW)


def device_index():
    return lax.axis_index("grp") * lax.axis_size("hd") + lax.axis_index("hd")


def gather_steps(shard, order, core, total):
    held = shard
    for bit in order[:-1]:
        (came,) = yield [functools.partial(swap, held, bit, total)]
        held = jnp.concatenate([held, came], axis=0)
    (came,) = yield [functools.partial(swap, held, order[-1], total)]
    first, second = yield [functools.partial(swap, held, core, total), functools.partial(swap, came, core, total)]
    return [held, came, first, second]


def gather_gains_steps(gains, x_bit, y_bit, core, total):
    rows = gains.shape[0]
    held = gains.astype(LOW).reshape(1, -1)
    outer = (x_bit, y_bit)
    masks = [1 << x_bit, 1 << y_bit, (1 << x_bit) | (1 << y_bit)]
    exchange = lambda mask: functools.partial(lax.ppermute, held, AXES, [(j, j ^ mask) for j in range(total)])
    came = yield [exchange(mask) for mask in masks]
    held = jnp.concatenate([held, *came], axis=0)
    for bit in (1, 0, core):
        (came,) = yield [functools.partial(swap, held, bit, total)]
        held = jnp.concatenate([held, came], axis=0)
    owners = jnp.array(spread_of((*outer, 1, 0), core, total), jnp.int32) ^ device_index()
    place = lax.broadcasted_iota(jnp.int32, (total, total), 0) == owners[None, :]
    every = jnp.dot(place.astype(LOW), held, preferred_element_type=F32)
    return jnp.swapaxes(every.reshape(total, rows, -1), 0, 1).reshape(rows, -1)


def scatter_steps(mine, theirs, x_bit, y_bit, core, total, last=False):
    (came,) = yield [functools.partial(swap, theirs, core, total)]
    half = mine.shape[1] // 2
    away = [added(mine[k, half:], came[k, half:]) for k in range(2)]
    held = [added(mine[k, :half], came[k, :half]) for k in range(2)]
    came = yield [functools.partial(swap, block, bit, total) for block, bit in zip(away, (y_bit, x_bit))]
    half //= 2
    away = [added(held[k][half:], came[k][half:]) for k in range(2)]
    held = [added(held[k][:half], came[k][:half]) for k in range(2)]
    came = yield [functools.partial(swap, block, bit, total) for block, bit in zip(away, (x_bit, y_bit))]
    both = jnp.stack([added(held[k], came[k]) for k in range(2)], axis=1)
    if last:
        (came,) = yield [functools.partial(lax.all_to_all, both, "hd", 0, 0, tiled=True)]
        return jnp.sum(came.astype(F32), axis=0)
    for bit in range(core):
        half = both.shape[0] // 2
        (came,) = yield [functools.partial(swap, both[half:], bit, total)]
        both = added(both[:half], came)
    return both[0].astype(F32)


class Chain:
    def __init__(self, steps):
        self.steps, self.result, self.under_way = steps, None, None
        self.wanted = next(steps)

    def start(self):
        if self.under_way is None:
            self.under_way = [exchange() for exchange in self.wanted]

    def advance(self, came):
        self.under_way = None
        try:
            self.wanted = self.steps.send(came)
        except StopIteration as stop:
            self.wanted, self.result = [], stop.value


def in_round(chains, compute=None, *, beside=None, longer=()):
    chains = [chain for chain in chains if chain.wanted]
    for chain in chains:
        chain.start()
    ending = [chain for chain in chains if chain not in longer]
    done = compute() if compute else ()
    came, done, beside = lax.optimization_barrier(([chain.under_way for chain in ending], done, beside))
    for chain, blocks in zip(ending, came):
        chain.advance(blocks)
    return done if beside is None else (done, beside)


def place_blocks(refs, spread, dst, rows, sem):
    if spread is None:
        pltpu.make_async_copy(refs[0].at[:, rows], dst, sem).start()
        return
    me, each = device_index(), len(spread) // 4
    for p, mask in enumerate(spread):
        pltpu.make_async_copy(refs[p // each].at[p % each, rows], dst.at[me ^ mask], sem).start()


def z_place(mask, owner, depth, last):
    if last:
        return owner & (depth - 1)
    return sum(((mask >> bit) & 1) << (log2(depth) - 1 - bit) for bit in range(log2(depth)))


def cut_blocks(halves, refs, depth, sems, last=False):
    me = device_index()
    for mask in range(32):
        owner = me ^ mask
        place = mask // (2 * depth)
        for half, src_of, rows in halves:
            group = place if half == 0 else place // 2 + place % 2 * 2
            dst = refs[mask // depth % 2].at[half, group * depth + z_place(mask, owner, depth, last)]
            dst = dst if rows is None else dst.at[rows]
            pltpu.make_async_copy(src_of(owner), dst, sems.at[mask // depth % 2]).start()


def bring(src, dst, sem):
    copy = pltpu.make_async_copy(src, dst, sem)
    copy.start()
    return copy


def await_whole(refs, sems):
    for at, ref in enumerate(refs):
        pltpu.make_async_copy(ref, ref, sems.at[at]).wait()


def blocks_of(shape):
    return [jax.ShapeDtypeStruct((2, 16, *shape), LOW)] * 2


BLOCK = 512
PARTS = 4
CALLS = 2


def pack_kernel(attn_in_ref, attn_out_ref, w_out_ref, w_in_ref, *refs):
    cross, own, cross_out, own_out, mlp, attn_in, attn_out, w_out, w_in, sems = refs
    sources, places = (attn_in_ref, attn_out_ref, w_in_ref, w_out_ref), (attn_in, attn_out, w_in, w_out)
    for copy in [bring(src, dst, sems.at[at]) for at, (src, dst) in enumerate(zip(sources, places))]:
        copy.wait()
    rows = attn_in.shape[1]
    for at, (to, to_out) in enumerate(((cross, cross_out), (own, own_out))):
        for m in range(3):
            to[0, m * rows : (m + 1) * rows, :] = attn_in[3 * at + m].astype(LOW)
        to_out[0] = attn_out[at].astype(LOW)
    width = w_out.shape[1] // PARTS
    for c in range(PARTS):
        mlp[c * rows : (c + 1) * rows, :] = w_out[:, c * width : (c + 1) * width].astype(LOW)
    mlp[PARTS * rows :, :] = w_in[...].T.astype(LOW)


def pack(attn_in_t, attn_out_t, w_out_t, w_in):
    rows, width = attn_in_t.shape[1:]
    return pl.pallas_call(
        pack_kernel,
        out_shape=[jax.ShapeDtypeStruct((1, 3 * rows, width), LOW)] * 2
        + [jax.ShapeDtypeStruct((1, rows, width), LOW)] * 2
        + [jax.ShapeDtypeStruct((PARTS * rows + w_in.shape[1], width), LOW)],
        in_specs=[ANY] * 4,
        out_specs=[VMEM] * 5,
        scratch_shapes=[pltpu.VMEM(a.shape, F32) for a in (attn_in_t, attn_out_t, w_out_t, w_in)]
        + [pltpu.SemaphoreType.DMA((4,))],
        compiler_params=pltpu.CompilerParams(vmem_limit_bytes=16 * MIB),
    )(attn_in_t, attn_out_t, w_out_t, w_in)


def from_all(own):
    total = lax.axis_size("grp") * lax.axis_size("hd")
    return lax.all_to_all(jnp.broadcast_to(own[None], (total, *own.shape)), AXES, 0, 0, tiled=True)


def gather_gains(gains):
    rows = gains.shape[0]
    every = from_all(gains.astype(LOW).reshape(-1)).astype(F32)
    return jnp.swapaxes(every.reshape(every.shape[0], rows, -1), 0, 1).reshape(rows, -1)


def scatter_gains(grads):
    total = lax.axis_size("grp") * lax.axis_size("hd")
    rows = grads.shape[0]
    blocks = jnp.swapaxes(grads.reshape(rows, total, -1), 0, 1).reshape(total, -1)
    came = lax.all_to_all(blocks, AXES, 0, 0, tiled=True)
    return jnp.sum(came, axis=0).reshape(rows, -1)


def dot_nn(a, b):
    return lax.dot_general(a, b, (((1,), (0,)), ((), ())), preferred_element_type=F32)


def dot_nt(a, b):
    return lax.dot_general(a, b, (((1,), (1,)), ((), ())), preferred_element_type=F32)


def dot_tn(a, b):
    return lax.dot_general(a, b, (((0,), (0,)), ((), ())), preferred_element_type=F32)


ROWS = 32


def unit_rows(rows):
    inverse = lax.rsqrt(jnp.mean(rows * rows, axis=-1, keepdims=True) + 1e-06)
    return rows * inverse, inverse


def normalise(source, gain, out):
    for at in range(0, source.shape[0], ROWS):
        span = slice(at, at + ROWS)
        out[span, :] = (unit_rows(source[span, :].astype(F32))[0] * gain).astype(LOW)


def norm_grad(source, gain, upstream, base, out, first=0):
    gain_grad = 0.0
    for at in range(0, upstream.shape[0], ROWS):
        span = slice(first + at, first + at + ROWS)
        unit, inverse = unit_rows(source[span, :].astype(F32))
        grad = upstream[at : at + ROWS]
        scaled = grad * gain
        inner = jnp.mean(scaled * unit, axis=-1, keepdims=True)
        extra = (scaled - unit * inner) * inverse
        out[span, :] = extra if base is None else base[span, :].astype(F32) + extra
        gain_grad += jnp.sum((grad * unit).reshape(ROWS // 8, 8, -1), axis=0)
    return jnp.sum(gain_grad, axis=0, keepdims=True)


SHARES = 2


def in_shares(rows, work, scratch, out, sem):
    count = rows // SHARES
    for at in range(0, rows, count):
        work(at, count)
        bring(scratch.at[at : at + count], out.at[at : at + count], sem)


def head_scores(query, key, count, scale):
    scores = dot_nt(query, key) * scale
    if count is not None:
        place = lax.broadcasted_iota(jnp.int32, scores.shape, 1)
        scores = jnp.where(place < count, scores, -1e30)
    return scores


def matrix(weights):
    return weights[...].reshape(-1, weights.shape[2])


def attend_kernel(cross, images, size, spreads, *refs):
    if cross:
        counts, gains, source, target, *refs = refs
    else:
        gains, target, *refs = refs
    *pieces, q_out, k_out, v_out, context_out, sum_out, log_out, whole, refs = *refs[:-14], *refs[-14:-7], refs[-7:]
    kept, target_v, source_v, weights, normal, total, sems = refs
    q_v, k_v, v_v, context_v = (kept.at[m] for m in range(4))
    rows = weights.shape[2]
    count = len(pieces) // 2
    come = [bring(source, source_v, sems.at[4])] if cross else []
    come.append(bring(target, target_v, sems.at[5]))
    for m in (1, 2, 0):
        place_blocks(pieces[:count], spreads[0], weights.at[m], pl.ds(m * rows, rows), sems.at[m])
    place_blocks(pieces[count:], spreads[1], weights.at[3], slice(None), sems.at[3])

    def arrived(m):
        pltpu.make_async_copy(weights.at[m], weights.at[m], sems.at[m]).wait()
        return matrix(weights.at[m])

    key_gain, query_gain = (0, 1) if cross else (2, 2)
    come[0].wait()
    normalise(source_v if cross else target_v, gains[key_gain : key_gain + 1, :], normal)
    k_v[...] = dot_nt(normal[...], arrived(1)).astype(LOW)
    leave = [bring(k_v, k_out, sems.at[6])]
    v_v[...] = dot_nt(normal[...], arrived(2)).astype(LOW)
    leave.append(bring(v_v, v_out, sems.at[7]))
    if cross:
        come[1].wait()
        normalise(target_v, gains[query_gain : query_gain + 1, :], normal)
    q_v[...] = dot_nt(normal[...], arrived(0)).astype(LOW)
    leave.append(bring(q_v, q_out, sems.at[8]))
    out_weights = arrived(3)
    leave.append(bring(weights, whole, sems.at[9]))
    width = q_v.shape[1] // NH
    scale = width ** (-0.5)

    def one_image(image, carry):
        span = pl.ds(pl.multiple_of(image * size, size), size)
        count = counts[image] if cross else None
        for h in range(NH):
            part = slice(h * width, (h + 1) * width)
            scores = head_scores(q_v[span, part], k_v[span, part], count, scale)
            highest = jnp.max(scores, axis=-1, keepdims=True)
            exponent = jnp.exp(scores - highest)
            row_total = jnp.sum(exponent, axis=-1, keepdims=True)
            probs = (exponent * (1.0 / row_total)).astype(LOW)
            context_v[span, part] = dot_nn(probs, v_v[span, part]).astype(LOW)
            log_out[span, h : h + 1] = highest + jnp.log(row_total)
        return carry

    lax.fori_loop(0, images, one_image, 0)
    leave.append(bring(context_v, context_out, sems.at[10]))

    def work(at, count):
        span = slice(at, at + count)
        total[span, :] = target_v[span, :].astype(F32) + dot_nt(context_v[span, :], out_weights)

    in_shares(total.shape[0], work, total, sum_out, sems.at[11])
    for copy in leave:
        copy.wait()
    pltpu.make_async_copy(total, sum_out, sems.at[11]).wait()


def attend_block(gains, source, target, counts, pieces, spreads, images):
    cross = source is not None
    rows, width = target.shape
    low = jax.ShapeDtypeStruct((rows, width), LOW)
    weights = (4, 32, width // 32, width)
    head = (counts, gains, source, target) if cross else (gains, target)
    return pl.pallas_call(
        functools.partial(attend_kernel, cross, images, rows // images, spreads),
        out_shape=[low] * 4
        + [jax.ShapeDtypeStruct(shape, F32) for shape in ((rows, width), (rows, NH))]
        + [jax.ShapeDtypeStruct(weights, LOW)],
        in_specs=([SMEM] if cross else []) + [VMEM] + [ANY] * (2 if cross else 1) + [ANY] * len(pieces),
        out_specs=[ANY] * 5 + [VMEM, ANY],
        scratch_shapes=[
            pltpu.VMEM((4, rows, width), LOW),
            pltpu.VMEM((rows, width), target.dtype),
            pltpu.VMEM((rows if cross else 8, width), LOW),
            pltpu.VMEM(weights, LOW),
            pltpu.VMEM((rows, width), LOW),
            pltpu.VMEM((rows, width), F32),
            pltpu.SemaphoreType.DMA((12,)),
        ],
        compiler_params=pltpu.CompilerParams(vmem_limit_bytes=48 * MIB),
        cost_estimate=pl.CostEstimate(
            flops=8 * rows * width * width + 4 * rows * width * (rows // images),
            bytes_accessed=12 * rows * width + 8 * width * width,
            transcendentals=rows * NH * (rows // images),
        ),
    )(*head, *pieces)


def scores_grad_kernel(cross, images, size, *refs):
    if cross:
        counts, *refs = refs
    upstream, q_in, k_in, v_in, context_in, log_in, whole, *refs = refs
    grads_out, (up_v, kept, grads, dc, wo_v, sems) = refs[:3], refs[3:]
    come = [bring(upstream, up_v, sems.at[0]), bring(whole.at[3], wo_v, sems.at[1])]
    come += [bring(src, kept.at[m], sems.at[2 + m]) for m, src in enumerate((q_in, k_in, v_in, context_in))]
    q_v, k_v, v_v, context_v = (kept.at[m] for m in range(4))
    dq, dk, dv = (grads.at[m] for m in range(3))
    for copy in come[:2]:
        copy.wait()
    dc[...] = dot_nn(up_v[...].astype(LOW), matrix(wo_v)).astype(LOW)
    for copy in come[2:]:
        copy.wait()
    width = q_v.shape[1] // NH
    scale = width ** (-0.5)

    def one_image(image, carry):
        span = pl.ds(pl.multiple_of(image * size, size), size)
        count = counts[image] if cross else None
        for h in range(NH):
            part = slice(h * width, (h + 1) * width)
            query, key, value, grad = q_v[span, part], k_v[span, part], v_v[span, part], dc[span, part]
            probs = jnp.exp(head_scores(query, key, count, scale) - log_in[span, h : h + 1])
            prob_grad = dot_nt(grad, value)
            dv[span, part] = dot_tn(probs.astype(LOW), grad).astype(LOW)
            inner = jnp.sum(grad.astype(F32) * context_v[span, part].astype(F32), axis=-1, keepdims=True)
            score_grad = (probs * (prob_grad - inner)).astype(LOW)
            dq[span, part] = (dot_nn(score_grad, key) * scale).astype(LOW)
            dk[span, part] = (dot_tn(score_grad, query) * scale).astype(LOW)
        for m, to in enumerate(grads_out):
            pltpu.make_async_copy(grads.at[m, span], to.at[span], sems.at[6 + m]).start()
        return carry

    lax.fori_loop(0, images, one_image, 0)
    await_whole(grads_out, sems.at[pl.ds(6, 3)])


def scores_grad(counts, upstream, saved, whole, images):
    cross = counts is not None
    rows, width = upstream.shape
    return pl.pallas_call(
        functools.partial(scores_grad_kernel, cross, images, rows // images),
        out_shape=[jax.ShapeDtypeStruct((rows, width), LOW)] * 3,
        in_specs=([SMEM] if cross else []) + [ANY] * 5 + [VMEM, ANY],
        out_specs=[ANY] * 3,
        scratch_shapes=[
            pltpu.VMEM((rows, width), F32),
            pltpu.VMEM((4, rows, width), LOW),
            pltpu.VMEM((3, rows, width), LOW),
            pltpu.VMEM((rows, width), LOW),
            pltpu.VMEM(whole.shape[1:], LOW),
            pltpu.SemaphoreType.DMA((9,)),
        ],
        compiler_params=pltpu.CompilerParams(vmem_limit_bytes=48 * MIB),
        cost_estimate=pl.CostEstimate(
            flops=2 * rows * width * width + 10 * rows * width * (rows // images),
            bytes_accessed=18 * rows * width + 4 * width * width,
            transcendentals=rows * NH * (rows // images),
        ),
    )(*([counts] if cross else []), upstream, *saved, whole)


def matrix_shares(count, rows):
    shares = []
    for m in range(count // 2 * 2):
        shares.append((m % 2, m, 0, rows, m // 2 * rows))
    if count % 2:
        for half in range(2):
            shares.append((half, count - 1, half * rows // 2, rows // 2, count // 2 * rows))
    return shares


def matrix_blocks(sums, count, rows):
    parts = [[] for _ in range(count)]
    for half, m, _, length, at in matrix_shares(count, rows):
        parts[m].append(sums[half, at : at + length])
    return [part[0] if len(part) == 1 else jnp.concatenate(part, axis=0) for part in parts]


def matrix_grad_kernel(cross, depth, *refs):
    gains, *refs = refs
    ins, (*outs, target_v, source_v, up_v, kept, grads, normal, sems, send_sems) = refs[: 6 + cross], refs[6 + cross :]
    to = [source_v] * cross + [target_v, up_v] + [kept.at[m] for m in (3, 0, 1, 2)]
    order = (1, 4, 0, 5, 6, 2, 3) if cross else (0, 3, 4, 5, 1, 2)
    come = {at: bring(ins[at], to[at], sems.at[at]) for at in order}
    dq, dk, dv, context = (kept.at[m] for m in range(4))
    key_gain, query_gain = (0, 1) if cross else (2, 2)
    width = target_v.shape[1]

    def finish(m, grad):
        grads[m] = grad.astype(LOW)
        if depth is None:
            bring(grads.at[m], outs[m], send_sems.at[m])
            return
        rows = width // 32

        def part(first, count):
            return lambda owner: grads.at[m, pl.ds(pl.multiple_of(owner * rows + first, count), count), :]

        halves = [
            (half, part(first, count), pl.ds(at, count))
            for half, m_at, first, count, at in matrix_shares(grads.shape[0], rows)
            if m_at == m
        ]
        cut_blocks(halves, outs, depth, send_sems, last=cross)

    come[cross].wait()
    normalise(target_v, gains[query_gain : query_gain + 1, :], normal)
    come[3 + cross].wait()
    finish(0, dot_tn(dq[...], normal[...]))
    if cross:
        come[0].wait()
        normalise(source_v, gains[key_gain : key_gain + 1, :], normal)
    come[4 + cross].wait()
    finish(1, dot_tn(dk[...], normal[...]))
    come[5 + cross].wait()
    finish(2, dot_tn(dv[...], normal[...]))
    come[1 + cross].wait()
    come[2 + cross].wait()
    finish(3, dot_tn(up_v[...].astype(LOW), context[...]))
    await_whole(outs, send_sems)


def matrix_grads(gains, source, target, upstream, context, score_grads, depth):
    cross = source is not None
    rows, width = target.shape
    head = (gains, source, target) if cross else (gains, target)
    count = 4
    if depth is None:
        out_shape = [jax.ShapeDtypeStruct((width, width), LOW)] * count
    else:
        out_shape = blocks_of((count * width // 64, width))
    return pl.pallas_call(
        functools.partial(matrix_grad_kernel, cross, depth),
        out_shape=out_shape,
        in_specs=[VMEM] + [ANY] * (len(head) + 4),
        out_specs=[ANY] * len(out_shape),
        scratch_shapes=[
            pltpu.VMEM((rows, width), target.dtype),
            pltpu.VMEM((rows if cross else 8, width), LOW),
            pltpu.VMEM((rows, width), F32),
            pltpu.VMEM((4, rows, width), LOW),
            pltpu.VMEM((count, width, width), LOW),
            pltpu.VMEM((rows, width), LOW),
            pltpu.SemaphoreType.DMA((7,)),
            pltpu.SemaphoreType.DMA((len(out_shape),)),
        ],
        compiler_params=pltpu.CompilerParams(vmem_limit_bytes=48 * MIB),
        cost_estimate=pl.CostEstimate(
            flops=2 * count * rows * width * width,
            bytes_accessed=16 * rows * width + 2 * count * width * width,
            transcendentals=rows,
        ),
    )(*head, upstream, context, *score_grads)


def project_grad_kernel(cross, *refs):
    gains, *refs = refs
    ins, refs = refs[: 6 + cross], refs[6 + cross :]
    outs = 1 + cross
    grads_out, gain_outs, (target_v, source_v, up_v, kept, weights, result, sems) = refs[:outs], refs[outs : 2 * outs], refs[2 * outs :]
    whole = ins[-1]
    inputs = list(ins[:-1])
    to = [source_v] * cross + [target_v, up_v] + [kept.at[m] for m in range(3)]
    order = (3, 1, 2, 4, 5, 0) if cross else (2, 3, 4, 0, 1)
    come, used = {}, 0
    for at in order:
        come[at] = bring(inputs[at], to[at], sems.at[at])
        if at >= 2 + cross:
            m = at - 2 - cross
            come["w%d" % m] = bring(whole.at[m], weights.at[m], sems.at[6 + m])
    dq, dk, dv = (kept.at[m] for m in range(3))
    key_gain, query_gain = (0, 1) if cross else (2, 2)
    rows = target_v.shape[0]

    def back_through(members, few):
        return sum(dot_nn(kept[m, few, :], matrix(weights.at[m])) for m in members)

    def shares(which, members, source, gain, base):
        gain_grads = []

        def work(at, count):
            back = back_through(members, slice(at, at + count))
            gain_grads.append(norm_grad(source, gain, back, base, result.at[which], at))

        in_shares(rows, work, result.at[which], grads_out[which], sems.at[9 + which])
        gain_outs[which][...] = sum(gain_grads)

    def arrived(*names):
        for name in names:
            come[name].wait()

    if cross:
        arrived(3, "w0", 1, 2)
        shares(0, (0,), target_v, gains[query_gain : query_gain + 1, :], up_v)
        arrived(4, "w1", 5, "w2", 0)
        shares(1, (1, 2), source_v, gains[key_gain : key_gain + 1, :], None)
    else:
        arrived(2, "w0", 3, "w1", 4, "w2", 0, 1)
        shares(0, (0, 1, 2), target_v, gains[key_gain : key_gain + 1, :], up_v)
    for which in range(outs):
        pltpu.make_async_copy(result.at[which], grads_out[which], sems.at[9 + which]).wait()


def project_grad(gains, source, target, upstream, score_grads, whole):
    cross = source is not None
    rows, width = target.shape
    outs = 2 if cross else 1
    head = (gains, source, target) if cross else (gains, target)
    result = pl.pallas_call(
        functools.partial(project_grad_kernel, cross),
        out_shape=[jax.ShapeDtypeStruct((rows, width), F32)] * outs + [jax.ShapeDtypeStruct((1, width), F32)] * outs,
        in_specs=[VMEM] + [ANY] * (len(head) + 4),
        out_specs=[ANY] * outs + [VMEM] * outs,
        scratch_shapes=[
            pltpu.VMEM((rows, width), target.dtype),
            pltpu.VMEM((rows if cross else 8, width), LOW),
            pltpu.VMEM((rows, width), F32),
            pltpu.VMEM((3, rows, width), LOW),
            pltpu.VMEM((3, *whole.shape[1:]), LOW),
            pltpu.VMEM((outs, rows, width), F32),
            pltpu.SemaphoreType.DMA((11,)),
        ],
        compiler_params=pltpu.CompilerParams(vmem_limit_bytes=48 * MIB),
        cost_estimate=pl.CostEstimate(
            flops=6 * rows * width * width, bytes_accessed=20 * rows * width + 6 * width * width, transcendentals=rows
        ),
    )(*head, upstream, *score_grads, whole)
    return result[:outs], result[outs:]


def mlp_forward_kernel(call, depth, second, cotangent, *refs):
    if call == 0:
        gain_row, bands, normal_out, sum_out, hidden_out, *refs = refs
    else:
        normal_in, skip, bands, sum_out, hidden_out, *refs = refs
    *outs, second_v, cot_v, extra_v, normal, cot_t, active, hidden_grad, result, lower_v, lift_v, grad_v, sems, send_sems = refs
    parts, rows, size = lower_v.shape[0], lower_v.shape[2], lower_v.shape[3]
    count, units = lift_v.shape[:2]
    steps = range(0, parts * size, BLOCK)
    share = BLOCK // units

    def bring_lift(step):
        here = pl.ds(step * share, share)
        there = bands.at[pl.ds(call * count + step * share, share), pl.ds(PARTS * rows, units)]
        return bring(there, lift_v.at[here], sems.at[4 + step])

    def bring_lower(c):
        return bring(bands.at[:, pl.ds((call * parts + c) * rows, rows)], lower_v.at[c], sems.at[8 + c])

    if call == 0:
        come = [bring(second, second_v, sems.at[0])]
    else:
        come = [bring(normal_in, normal, sems.at[0])]
    lifts = [bring_lift(0)]
    come.append(bring(cotangent, cot_v, sems.at[1]))
    lowers = [bring_lower(0)]
    lifts += [bring_lift(step) for step in range(1, len(steps))]
    lowers += [bring_lower(c) for c in range(1, parts)]
    if call == 1:
        come += [bring(second, second_v, sems.at[2]), bring(skip, extra_v, sems.at[3])]
    leave = []
    come[0].wait()
    if call == 0:
        normalise(second_v, gain_row[...], normal)
        leave.append(bring(normal, normal_out, sems.at[2]))
    for step, start in enumerate(steps):
        lifts[step].wait()
        hidden = dot_nt(normal[...], lift_v[step * share : (step + 1) * share].reshape(BLOCK, -1))
        if step == 0:
            come[1].wait()
        if start % size == 0:
            lowers[start // size].wait()
        columns = slice(start % size, start % size + BLOCK)
        upstream = dot_nn(cot_v[...], lower_v[start // size, :, :, columns].reshape(-1, BLOCK))
        for at in range(0, hidden.shape[0], ROWS):
            few = slice(at, at + ROWS)
            value = hidden[few]
            square = value * value
            root = 0.7978845608028654
            tanh = jnp.tanh(value * (root + (root * 0.044715) * square))
            half = 0.5 + 0.5 * tanh
            rise = (0.5 * value) * (1.0 - tanh * tanh) * (root + (3 * root * 0.044715) * square)
            active[few, start : start + BLOCK] = (value * half).astype(LOW)
            hidden_grad[few, start : start + BLOCK] = (upstream[few] * (half + rise)).astype(LOW)
        here = slice(start, start + BLOCK)
        bring(hidden_grad.at[:, here], hidden_out.at[:, here], sems.at[10])
        if step == 0:
            cot_t[...] = cot_v[...].T
        if (start + BLOCK) % size == 0:
            c = start // size
            columns = slice(c * size, (c + 1) * size)
            grad_v[:, columns] = dot_nn(cot_t[...], active[:, columns]).astype(LOW)
            if depth is None:
                bring(grad_v.at[:, columns], outs[0].at[:, columns], send_sems.at[0])
            else:
                src_of = lambda owner: grad_v.at[pl.ds(pl.multiple_of(owner * rows, rows), rows), columns]
                cut_blocks([(c, src_of, None)], outs, depth, send_sems)
    for copy in come[2:]:
        copy.wait()

    def work(at, length):
        few = slice(at, at + length)
        total = second_v[few, :]
        for c in range(parts):
            total = total + dot_nt(active[few, c * size : (c + 1) * size], matrix(lower_v.at[c]))
        result[few, :] = total if call == 0 else (total + extra_v[few, :].astype(F32)).astype(LOW)

    in_shares(result.shape[0], work, result, sum_out, sems.at[11])
    for copy in leave:
        copy.wait()
    pltpu.make_async_copy(result, sum_out, sems.at[11]).wait()
    pltpu.make_async_copy(hidden_grad, hidden_out, sems.at[10]).wait()
    await_whole(outs, send_sems)


def mlp_forward(call, second, cotangent, others, bands, hidden, depth):
    rows, width = second.shape
    units, parts = hidden // CALLS, PARTS // CALLS
    low = jax.ShapeDtypeStruct((rows, width), LOW)
    if depth is None:
        outs = [jax.ShapeDtypeStruct((width, units), LOW)]
    else:
        outs = blocks_of((width // 32, units // 2))
    return pl.pallas_call(
        functools.partial(mlp_forward_kernel, call, depth),
        out_shape=[low]
        + [jax.ShapeDtypeStruct((rows, width), F32)] * (call == 0)
        + [jax.ShapeDtypeStruct((rows, units), LOW)]
        + outs,
        in_specs=[ANY] * 2 + ([VMEM] if call == 0 else [ANY] * 2) + [ANY],
        out_specs=[ANY] * (3 if call == 0 else 2) + [ANY] * len(outs),
        scratch_shapes=[
            pltpu.VMEM((rows, width), F32),
            pltpu.VMEM((rows, width), LOW),
            pltpu.VMEM((8 if call == 0 else rows, width), LOW),
            pltpu.VMEM((rows, width), LOW),
            pltpu.VMEM((width, rows), LOW),
            pltpu.VMEM((rows, units), LOW),
            pltpu.VMEM((rows, units), LOW),
            pltpu.VMEM((rows, width), F32 if call == 0 else LOW),
            pltpu.VMEM((parts, 32, width // 32, units // parts), LOW),
            pltpu.VMEM((32 // CALLS, hidden // 32, width), LOW),
            pltpu.VMEM((width, units), LOW),
            pltpu.SemaphoreType.DMA((12,)),
            pltpu.SemaphoreType.DMA((len(outs),)),
        ],
        compiler_params=pltpu.CompilerParams(vmem_limit_bytes=56 * MIB),
        cost_estimate=pl.CostEstimate(
            flops=8 * rows * width * units,
            bytes_accessed=6 * width * units + 12 * rows * width + 2 * rows * units,
            transcendentals=rows * units,
        ),
    )(second, cotangent, *others, bands)


def mlp_backward_kernel(depth, gain_row, second, cotangent, normal, hidden_grad0, hidden_grad1, bands, *refs):
    second_grad, gain_grad, *refs = refs
    *outs, second_v, cot_v, normal_v, hidden_grads, normal_t, result, lift_v, grad_v, sems, send_sems = refs
    units = lift_v.shape[1]
    share, half = BLOCK // units, lift_v.shape[0] // 2
    come = [bring(normal, normal_v, sems.at[0])]
    come += [bring(src, hidden_grads.at[h], sems.at[1 + h]) for h, src in enumerate((hidden_grad0, hidden_grad1))]
    come.append(bring(bands.at[:, pl.ds(bands.shape[1] - units, units)], lift_v, sems.at[3]))
    come += [bring(second, second_v, sems.at[4]), bring(cotangent, cot_v, sems.at[5])]
    come[0].wait()
    normal_t[...] = normal_v[...].T
    steps = grad_v.shape[0] // 2
    for h in range(2):
        come[1 + h].wait()

        def one_block(at, carry):
            columns = pl.ds(pl.multiple_of(at * BLOCK, BLOCK), BLOCK)
            step = h * steps + at
            grad_v[step] = dot_nn(normal_t[...], hidden_grads[h, :, columns]).astype(LOW)
            if depth is None:
                columns = pl.ds(pl.multiple_of(step * BLOCK, BLOCK), BLOCK)
                pltpu.make_async_copy(grad_v.at[step], outs[0].at[:, columns], send_sems.at[0]).start()
                return carry
            size = grad_v.shape[1] // 2
            for c in range(share):
                mask = (step * share + c) ^ device_index()
                group = mask // (2 * depth)
                place = z_place(mask, None, depth, False)
                for away in range(2):

                    @pl.when((mask // depth) % 2 == away)
                    def send():
                        for part in range(2):
                            to = group if part == 0 else group // 2 + group % 2 * 2
                            pltpu.make_async_copy(
                                grad_v.at[step, part * size : (part + 1) * size, c * units : (c + 1) * units],
                                outs[away].at[part, to * depth + place],
                                send_sems.at[away],
                            ).start()

            return carry

        lax.fori_loop(0, steps, one_block, 0)
    for copy in come[3:]:
        copy.wait()
    gain_grads = []

    def work(at, count):
        few = slice(at, at + count)
        back = sum(
            dot_nn(hidden_grads[h, few, :], lift_v[h * half : (h + 1) * half].reshape(half * units, -1)) for h in range(2)
        )
        gain_grads.append(norm_grad(second_v, gain_row[...], back, cot_v, result, at))

    in_shares(result.shape[0], work, result, second_grad, sems.at[6])
    gain_grad[...] = sum(gain_grads)
    pltpu.make_async_copy(result, second_grad, sems.at[6]).wait()
    await_whole(outs, send_sems)


def mlp_backward(gain_row, second, cotangent, normal, hidden_grads, bands, hidden, depth):
    rows, width = second.shape
    if depth is None:
        outs = [jax.ShapeDtypeStruct((width, hidden), LOW)]
    else:
        outs = blocks_of((width // 2, hidden // 32))
    return pl.pallas_call(
        functools.partial(mlp_backward_kernel, depth),
        out_shape=[jax.ShapeDtypeStruct((rows, width), F32), jax.ShapeDtypeStruct((1, width), F32)] + outs,
        in_specs=[VMEM] + [ANY] * 6,
        out_specs=[ANY, VMEM] + [ANY] * len(outs),
        scratch_shapes=[
            pltpu.VMEM((rows, width), F32),
            pltpu.VMEM((rows, width), LOW),
            pltpu.VMEM((rows, width), LOW),
            pltpu.VMEM((2, rows, hidden // 2), LOW),
            pltpu.VMEM((width, rows), LOW),
            pltpu.VMEM((rows, width), F32),
            pltpu.VMEM((32, hidden // 32, width), LOW),
            pltpu.VMEM((hidden // BLOCK, width, BLOCK), LOW),
            pltpu.SemaphoreType.DMA((7,)),
            pltpu.SemaphoreType.DMA((len(outs),)),
        ],
        compiler_params=pltpu.CompilerParams(vmem_limit_bytes=56 * MIB),
        cost_estimate=pl.CostEstimate(
            flops=4 * rows * width * hidden,
            bytes_accessed=4 * width * hidden + 12 * rows * width + 2 * rows * hidden,
            transcendentals=0,
        ),
    )(gain_row, second, cotangent, normal, *hidden_grads, bands)


def local(
    pixels,
    latents,
    skip,
    counts,
    cotangent,
    attn_in,
    attn_out,
    w_in,
    w_out,
    gains,
    attn_in_first,
    attn_in_second,
    attn_out_first,
    attn_out_second,
    w_in_first,
    w_in_second,
    w_out_first,
    w_out_second,
    gains_first,
    gains_second,
):
    groups, depth = lax.axis_size("grp"), lax.axis_size("hd")
    total, core = groups * depth, log2(depth)
    fast = total == 32 and depth == 4
    images, size, width = latents.shape
    hidden = w_out.shape[0]
    flat = lambda rows: rows.reshape(-1, width)
    whole = lambda rows: rows.reshape(images, -1, width)
    pixel_rows, latent_rows, cot_rows = flat(pixels), flat(latents), flat(cotangent)
    attn_in_t, attn_out_t, w_out_t = jnp.swapaxes(attn_in, 1, 2), jnp.swapaxes(attn_out, 1, 2), w_out.T
    own_counts = lax.dynamic_slice_in_dim(counts, lax.axis_index("hd") * images, images)
    cut = depth if fast else None

    def cross_forward(pieces, spreads):
        return attend_block(gain_rows, pixel_rows, latent_rows, own_counts, pieces, spreads, images)

    def self_forward(pieces, spreads):
        return attend_block(gain_rows, None, first_sum, None, pieces, spreads, images)

    if fast:
        (x_bit,), (y_bit,) = outer_bits(groups, depth)
        *shards, mlp_shard = pack(attn_in_t, attn_out_t, w_out_t, w_in)
        orders = ((1, 0, x_bit, y_bit), (1, 0, y_bit, x_bit), (x_bit, y_bit, 1, 0), (y_bit, x_bit, 1, 0))
        spreads = [spread_of(order, core, total) for order in orders]
        chains = [Chain(gather_steps(shard, order, core, total)) for shard, order in zip(shards, orders)]
        small = Chain(gather_gains_steps(gains, x_bit, y_bit, core, total))
        both = [*chains, small]
        in_round(both)
        _, mlp_shard = in_round(both, beside=mlp_shard)
        bands = lax.all_gather(mlp_shard, AXES, axis=0)
        in_round(both)
        in_round(both)
        _, gain_rows = in_round(both, beside=small.result, longer=chains[1::2])
        *saved, first_sum, logs, weights = in_round(
            both, lambda: cross_forward(chains[0].result + chains[2].result, spreads[::2])
        )
        *saved2, second_sum, logs2, weights2 = self_forward(chains[1].result + chains[3].result, spreads[1::2])
    else:
        every = lambda shard: lax.all_gather(shard.astype(LOW), AXES, axis=0, tiled=True).reshape(32, -1, shard.shape[1])
        inward = lambda m: jnp.concatenate([every(attn_in_t[3 * m + k]) for k in range(3)], axis=1)
        gain_rows = gather_gains(gains)
        lower = every(w_out_t)
        lift = lax.all_gather(w_in.astype(LOW), AXES, axis=1, tiled=True).T.reshape(32, -1, width)
        bands = jnp.concatenate([*jnp.split(lower, PARTS, axis=2), lift], axis=1)
        *saved, first_sum, logs, weights = cross_forward([inward(0), every(attn_out_t[0])], (None, None))
        *saved2, second_sum, logs2, weights2 = self_forward([inward(1), every(attn_out_t[1])], (None, None))

    normal, partial, hidden_grad0, *lower_grad0 = mlp_forward(
        0, second_sum, cot_rows, (gain_rows[3:],), bands, hidden, cut
    )

    def mlp_second():
        return mlp_forward(1, partial, cot_rows, (normal, flat(skip)), bands, hidden, cut)

    def mlp_back():
        return mlp_backward(
            gain_rows[3:], second_sum, cot_rows, normal, (hidden_grad0, hidden_grad1), bands, hidden, cut
        )

    def self_scores():
        return scores_grad(None, second_grad, (*saved2, logs2), weights2, images)

    def self_matrices():
        return matrix_grads(gain_rows, None, first_sum, second_grad, saved2[3], score_grads2, cut)

    def self_project():
        return project_grad(gain_rows, None, first_sum, second_grad, score_grads2, weights2)

    def cross_scores():
        return scores_grad(own_counts, first_grad, (*saved, logs), weights, images)

    def cross_matrices():
        return matrix_grads(gain_rows, pixel_rows, latent_rows, first_grad, saved[3], score_grads, cut)

    def cross_project():
        return project_grad(gain_rows, pixel_rows, latent_rows, first_grad, score_grads, weights)

    if fast:
        scatter = lambda blocks, last=False: Chain(scatter_steps(*blocks, x_bit, y_bit, core, total, last))
        live = [scatter(lower_grad0)]
        latents_out, hidden_grad1, *lower_grad1 = in_round(live, mlp_second)
        live.append(scatter(lower_grad1))
        second_grad, gain3_grad, *lift_grad = in_round(live, mlp_back)
        live.append(scatter(lift_grad))
        score_grads2 = in_round(live, self_scores)
        live.append(scatter(in_round(live, self_matrices, longer=live[2:])))
        (first_grad,), (gain2_grad,) = in_round(live, self_project)
        score_grads = in_round(live, cross_scores, longer=live[3:])
        blocks, score_grads = in_round(live, cross_matrices, beside=score_grads)
        live.append(scatter(blocks, True))
        (latents_grad, pixels_grad), (gain1_grad, gain0_grad) = in_round(live, cross_project)
        in_round(live, longer=live[4:])
        in_round(live)
        gains_grad = jnp.concatenate([gain0_grad, gain1_grad, gain2_grad, gain3_grad], axis=0)
        gains_sum = scatter_gains(gains_grad)
        while any(chain.wanted for chain in live):
            in_round(live)
        lower0, lower1, lift_sum, own, cross = [chain.result for chain in live]
        lower_sum = jnp.concatenate([*lower0, *lower1], axis=1)
        lift_sum = jnp.concatenate([*lift_sum], axis=0)
        sums, sums2 = [matrix_blocks(block, 4, attn_in.shape[2]) for block in (cross, own)]
    else:
        latents_out, hidden_grad1, lower_grad1 = mlp_second()
        second_grad, gain3_grad, lift_grad = mlp_back()
        score_grads2 = self_scores()
        grads2 = self_matrices()
        (first_grad,), (gain2_grad,) = self_project()
        score_grads = cross_scores()
        grads = cross_matrices()
        (latents_grad, pixels_grad), (gain1_grad, gain0_grad) = cross_project()
        gains_grad = jnp.concatenate([gain0_grad, gain1_grad, gain2_grad, gain3_grad], axis=0)
        gains_sum = scatter_gains(gains_grad)
        sum_of = lambda grad, along: lax.psum_scatter(grad, AXES, scatter_dimension=along, tiled=True)
        sums = [sum_of(g, 0) for g in grads]
        sums2 = [sum_of(g, 0) for g in grads2]
        lift_sum = sum_of(lift_grad, 1)
        lower_sum = sum_of(jnp.concatenate([*lower_grad0, lower_grad1], axis=1), 0)
    mixing_sum = jnp.swapaxes(jnp.stack([*sums[:3], *sums2[:3]]), 1, 2).astype(F32)
    outward_sum = jnp.swapaxes(jnp.stack([sums[3], sums2[3]]), 1, 2).astype(F32)
    mix = adamw(attn_in, mixing_sum, attn_in_first, attn_in_second, 0.05, 0.1)
    out = adamw(attn_out, outward_sum, attn_out_first, attn_out_second, 0.3, 0.1)
    lift_new = adamw(w_in, lift_sum.astype(F32), w_in_first, w_in_second, 0.05, 0.1)
    lower_new = adamw(w_out, lower_sum.T.astype(F32), w_out_first, w_out_second, 0.03, 0.1)
    gain_first, gain_second, gain_new = adamw(
        gains, gains_sum, gains_first, gains_second, 0.4, 0.0
    )
    return (
        whole(latents_out),
        whole(pixels_grad),
        whole(latents_grad),
        *mix,
        *out,
        *lift_new,
        *lower_new,
        gain_first,
        gain_second[:3],
        gain_second[3],
        gain_new,
    )


def solution(mesh):
    return jax.shard_map(
        local,
        mesh=mesh,
        in_specs=(
            P(("grp", "hd"), None, None),
            P(("grp", "hd"), None, None),
            P(("grp", "hd"), None, None),
            P("grp"),
            P(("grp", "hd"), None, None),
            P(None, None, ("grp", "hd")),
            P(None, None, ("grp", "hd")),
            P(None, ("grp", "hd")),
            P(None, ("grp", "hd")),
            P(None, ("grp", "hd")),
            P(None, None, ("grp", "hd")),
            P(None, None, ("grp", "hd")),
            P(None, None, ("grp", "hd")),
            P(None, None, ("grp", "hd")),
            P(None, ("grp", "hd")),
            P(None, ("grp", "hd")),
            P(None, ("grp", "hd")),
            P(None, ("grp", "hd")),
            P(None, ("grp", "hd")),
            P(None, ("grp", "hd")),
        ),
        out_specs=(
            P(("grp", "hd"), None, None),
            P(("grp", "hd"), None, None),
            P(("grp", "hd"), None, None),
            P(None, None, ("grp", "hd")),
            P(None, None, ("grp", "hd")),
            P(None, None, ("grp", "hd")),
            P(None, None, ("grp", "hd")),
            P(None, None, ("grp", "hd")),
            P(None, None, ("grp", "hd")),
            P(None, ("grp", "hd")),
            P(None, ("grp", "hd")),
            P(None, ("grp", "hd")),
            P(None, ("grp", "hd")),
            P(None, ("grp", "hd")),
            P(None, ("grp", "hd")),
            P(None, ("grp", "hd")),
            P(None, ("grp", "hd")),
            P(("grp", "hd")),
            P(None, ("grp", "hd")),
        ),
        check_vma=False,
    )
```
